32 devices in a mesh: dp: 8 (over z, y), section: 4 (over x, core).
Axes of the slice: x: 2, y: 2, z: 4, core: 2. Of those that a mesh axis runs over, the one named last changes fastest.
Arguments:
- tokens: bfloat16 [8192, 1024], P('dp'), may hold values from -6 to 6
- doc_lengths: int32 [16, 4], P('dp'), may hold values from 1 to 256, 512 in all within a row
- first_weights: bfloat16 [4, 1024, 4096], P('section'), may hold values from -0.1875 to 0.1875
- down_weights: bfloat16 [4, 2048, 1024], P('section'), may hold values from -0.09375 to 0.09375
- norm_gains: float32 [4, 2, 1024], P('section'), may hold values from 0.5 to 1.5
- norm_biases: float32 [4, 2, 1024], P('section'), may hold values from -1.2 to 1.2
- cotangent: bfloat16 [8192, 1024], P('dp'), may hold values from -6 to 6
Outputs:
- section_outputs: bfloat16 [4, 8192, 1024], P('section', 'dp')
- input_grads: bfloat16 [4, 8192, 1024], P('section', 'dp')
- first_grad: float32 [4, 1024, 4096], P('section', 'dp')
- down_grad: float32 [4, 2048, 1024], P('section', 'dp')
- gain_grad: float32 [4, 2, 1024], P('section', None, 'dp')
- bias_grad: float32 [4, 2, 1024], P('section', None, 'dp')
The draws below stay inside these ranges and needn't reach their ends.
Inputs may be any that keep to these rules, and one draw needn't show every extreme that they name: `doc_lengths`: each row's lengths add up to 512.
All inputs are finite; a program needn't handle non-finite values.
Results may differ from the reference program's by a relative error of at most 0.02.
Values may be sent and summed in bfloat16 or wider, within the bound.
A program may use at most 384 MiB of HBM per device.

```python
import math
import jax
import jax.numpy as jnp
import numpy as np
from jax import lax

D = 1024
HEADS = 16
HEAD = 64
FF = 4096
ROW_LEN = 512
DOCS = 4
ROWS = 16
TOKENS = 8192
N_SECTION = 4


def levels(own_key, shape, cuts, smallest, largest):
    level = 1.0
    for dim, parts in cuts:
        draws = jax.random.uniform(jax.random.fold_in(jax.random.fold_in(own_key, 6), dim), (parts,), jnp.float32, smallest / len(cuts), largest / len(cuts))
        level = level * jnp.repeat(jnp.exp(draws), shape[dim] // parts).reshape((-1,) + (1,) * (len(shape) - 1 - dim))
    return level


def length_profile(count, total, bound, skew):
    portions = [(1 << 20) // math.isqrt(standing ** skew) + 1 for standing in range(2, count + 1)]
    surplus, holding = total - bound - (count - 1), [1] * (count - 1)
    while surplus > 0:
        movable = [i for i in range(count - 1) if holding[i] < bound]
        mass, left = sum([portions[i] for i in movable]), surplus
        for i in movable:
            more = min(bound - holding[i], max(1, left * portions[i] // mass), surplus)
            holding[i] = holding[i] + more
            surplus = surplus - more
    return np.array([bound] + holding)


def uneven(key, amount, total, reach, slope):
    if amount == 2:
        one = jax.random.randint(key, (), max(1, total - reach), min(reach, total - 1) + 1)
        return jnp.stack([one, total - one])
    sizes = jnp.asarray(length_profile(amount, total, reach, slope), jnp.int32)
    twos = (amount - 1) // 2
    source_of, taker = sizes[1:1 + 2 * twos:2], sizes[2:2 + 2 * twos:2]
    margin = jnp.minimum(source_of - 1, reach - taker)
    passed = jax.random.randint(jax.random.fold_in(key, 1), (twos,), 0, 1 << 20) % (margin + 1)
    sizes = sizes.at[1:1 + 2 * twos:2].set(source_of - passed).at[2:2 + 2 * twos:2].set(taker + passed)
    return sizes[jax.random.permutation(jax.random.fold_in(key, 2), amount)]


def gaussian(rng, shape, spread, most, cuts=(), held_as=jnp.bfloat16):
    result = jax.random.normal(rng, shape, jnp.float32) * spread
    if len(cuts) > 0:
        result = levels(rng, shape, cuts, -0.22, 0.18) * result
    return jnp.clip(result, min=-most, max=most).astype(held_as)


def setup_inputs(seed: int = 0) -> dict:
    key_list = jax.random.split(jax.random.key(seed), 8)
    tokens = gaussian(key_list[0], (TOKENS, D), 1.0, 6.0, ((0, 8),))
    doc_lengths = jax.vmap(lambda own: uneven(own, DOCS, ROW_LEN, ROW_LEN // 2, 2))(jax.random.split(key_list[1], ROWS)).reshape((ROWS, DOCS)).astype(jnp.int32)
    first_weights = gaussian(key_list[2], (N_SECTION, D, FF), D ** -0.5, 0.1875, ((0, 4),))
    down_weights = gaussian(key_list[3], (N_SECTION, FF // 2, D), FF ** -0.5, 0.09375, ((0, 4),))
    norm_gains = jnp.clip(0.5 + 1.0 * jax.random.uniform(key_list[4], (N_SECTION, 2, D), jnp.float32) ** levels(key_list[4], (N_SECTION, 2, D), ((0, 4),), -0.2, 0.2), 0.5, 1.5)
    norm_biases = gaussian(key_list[5], (N_SECTION, 2, D), 0.3, 1.2, ((0, 4),), jnp.float32)
    cotangent = gaussian(key_list[6], (TOKENS, D), 1.0, 6.0, ((0, 8),))
    return {"tokens": tokens, "doc_lengths": doc_lengths, "first_weights": first_weights, "down_weights": down_weights, "norm_gains": norm_gains, "norm_biases": norm_biases, "cotangent": cotangent}


@jax.custom_vjp
def low(v):
    return lax.optimization_barrier(v.astype(jnp.bfloat16)).astype(jnp.float32)

@jax.custom_vjp
def low_back(v):
    return v

def low_keep(v):
    return (low(v), None)

def low_pass(kept, grad):
    return (grad,)

def back_keep(v):
    return (v, None)

def back_low(kept, grad):
    return (low(grad),)
low.defvjp(low_keep, low_pass)
low_back.defvjp(back_keep, back_low)
eps = 1e-05
masked_value = -1e+30

def normalize(inputs, gain, shift_bias):
    average = lax.optimization_barrier(jnp.mean(inputs, axis=-1, keepdims=True))
    centered = inputs - average
    variance = lax.optimization_barrier(jnp.mean(centered * centered, axis=-1, keepdims=True))
    return centered * lax.rsqrt(variance + eps) * gain + shift_bias

def allowed_pairs(lengths):
    ends = jnp.cumsum(lengths).astype(jnp.int32)
    places = jnp.arange(ROW_LEN, dtype=jnp.int32)
    segment = lax.optimization_barrier(jnp.sum((places[:, None] >= ends[None, :]).astype(jnp.int32), axis=1))
    return (segment[:, None] == segment[None, :]) & (places[None, :] <= places[:, None])

def attention_branch(normed, weight, lengths):
    highest = lax.Precision.HIGHEST
    projected = low(low_back(jnp.dot(normed, weight[:, :3 * D], precision=highest)))
    query_heads = projected[:, :D].reshape(ROW_LEN, HEADS, HEAD)
    key_heads = projected[:, D:2 * D].reshape(ROW_LEN, HEADS, HEAD)
    value_heads = projected[:, 2 * D:].reshape(ROW_LEN, HEADS, HEAD)
    scores = low_back(jnp.einsum('qhd,khd->hqk', query_heads, key_heads, precision=highest) * HEAD ** (-0.5))
    scores = jnp.where(allowed_pairs(lengths)[None], scores, masked_value)
    row_top = lax.optimization_barrier(jnp.max(scores, axis=-1, keepdims=True))
    exponent = jnp.exp(scores - row_top)
    prob_full = exponent / lax.optimization_barrier(jnp.sum(exponent, axis=-1, keepdims=True))
    context = jnp.einsum('hqk,khd->qhd', low(prob_full), value_heads, precision=highest)
    context = low(low_back(context.reshape(ROW_LEN, D)))
    return low_back(jnp.dot(context, weight[:, 3 * D:].T, precision=highest))

def feed_branch(normed, weight, down_full):
    highest = lax.Precision.HIGHEST
    hidden_pre = low_back(jnp.dot(normed, weight, precision=highest))
    hidden = low(jax.nn.gelu(hidden_pre))
    return low_back(jnp.dot(hidden, down_full, precision=highest))

def row_forward(firsts, downs, gains, biases, row_tokens, row_lengths, row_probes):
    current = low_back(row_tokens)
    results = []
    for sublayer in range(N_SECTION):
        normed = low(normalize(current, gains[sublayer, 0], biases[sublayer, 0]))
        if sublayer % 2 == 0:
            branch = attention_branch(normed, firsts[sublayer], row_lengths)
        else:
            down_full = jnp.concatenate([downs[sublayer - 1], downs[sublayer]], axis=0)
            branch = feed_branch(normed, firsts[sublayer], down_full)
        summed = current + normalize(branch, gains[sublayer, 1], biases[sublayer, 1])
        if sublayer < N_SECTION - 1:
            summed = summed + row_probes[sublayer]
        current = low(low_back(summed))
        results.append(current)
    return results

def group_size():
    chosen = 1
    for candidate in range(1, ROWS + 1):
        if ROWS % candidate == 0 and candidate * ROW_LEN <= 4096:
            chosen = candidate
    return chosen

def reference(tokens, doc_lengths, first_weights, down_weights, norm_gains, norm_biases, cotangent):
    per_group = group_size()
    group_count = ROWS // per_group
    length_groups = doc_lengths.reshape(group_count, per_group, DOCS)

    def forward(firsts, downs, gains, biases, inputs, probes):
        input_groups = inputs.reshape(group_count, per_group, ROW_LEN, D)
        probe_groups = probes.reshape(N_SECTION - 1, group_count, per_group, ROW_LEN, D).transpose(1, 2, 0, 3, 4)

        def one_row(row_tokens, row_lengths, row_probes):
            return jnp.stack(row_forward(firsts, downs, gains, biases, row_tokens, row_lengths, row_probes), axis=0)

        def one_group(carry, pieces):
            return (carry, jax.vmap(one_row)(pieces[0], pieces[1], pieces[2]))
        _, stacked = lax.scan(jax.checkpoint(one_group), jnp.zeros((), jnp.float32), (input_groups, length_groups, probe_groups))
        stacked = stacked.transpose(2, 0, 1, 3, 4).reshape(N_SECTION, TOKENS, D)
        return (stacked[N_SECTION - 1], stacked[:N_SECTION - 1])
    probes = jnp.zeros((N_SECTION - 1, TOKENS, D), jnp.float32)
    final, pullback, middle = jax.vjp(forward, first_weights.astype(jnp.float32), down_weights.astype(jnp.float32), norm_gains.astype(jnp.float32), norm_biases.astype(jnp.float32), tokens.astype(jnp.float32), probes, has_aux=True)
    grads = pullback(cotangent.astype(jnp.float32))
    section_outputs = jnp.concatenate([middle, final[None]], axis=0).astype(jnp.bfloat16)
    input_grads = jnp.concatenate([grads[4][None], grads[5]], axis=0).astype(jnp.bfloat16)
    return (section_outputs, input_grads, grads[0], grads[1], grads[2], grads[3])
```

```python
import functools

import jax
import jax.numpy as jnp
from jax import lax
from jax.experimental import pallas as pl
from jax.experimental.pallas import tpu as pltpu
from jax.sharding import PartitionSpec as P

HEADS = 16
HEAD = 64
eps = 1e-05
masked_value = -1e30
MESH = pl.DeviceIdType.MESH


def swap_pair(value):
    length = lax.axis_size("section")
    return lax.ppermute(value, "section", [(i, i ^ 1) for i in range(length)])


def hop(value, by):
    length = lax.axis_size("section")
    pairs = [(i, i + by) for i in range(length) if 0 <= i + by < length]
    return lax.ppermute(value, "section", pairs)


def normalize(inputs, gain, shift_bias):
    average = jnp.mean(inputs, axis=-1, keepdims=True)
    centered = inputs - average
    variance = jnp.mean(centered * centered, axis=-1, keepdims=True)
    return centered * lax.rsqrt(variance + eps) * gain + shift_bias


def allowed_pairs(lengths, row_len):
    ends = jnp.cumsum(lengths)
    places = jnp.arange(row_len, dtype=jnp.int32)
    segment = jnp.sum((places[:, None] >= ends[None, :]).astype(jnp.int32), axis=1)
    return (segment[:, None] == segment[None, :]) & (places[None, :] <= places[:, None])


def split_heads(matrix):
    return matrix.reshape(matrix.shape[0], HEADS, HEAD)


def contract_cols(left, right):
    return lax.dot_general(
        left, right, (((1,), (1,)), ((), ())), preferred_element_type=jnp.float32
    )


def ring_place(index, count):
    return jnp.where(index % 2 == 0, index // 2, count - 1 - index // 2)


def ring_index(place, count):
    return jnp.where(place < count // 2, 2 * place, 2 * (count - 1 - place) + 1)


def gradient_kernel(
    count,
    lhs,
    hidden_t,
    rhs,
    dz_down,
    small,
    first_out,
    down_out,
    small_out,
    total,
    pair_send,
    pair_recv,
    ring_send,
    ring_recv,
    small_pair,
    small_sum,
    small_recv,
    pair_ss,
    pair_rs,
    ring_ss,
    ring_rs,
    small_sems,
    small_ss,
    small_rs,
):
    rows = first_out.shape[0]
    half_units = hidden_t.shape[0] // 2
    dp = lax.axis_index("dp")
    section = lax.axis_index("section")
    core = lax.rem(section, 2)
    peer = section + 1 - 2 * core
    place = ring_place(dp, count)

    barrier = pltpu.get_barrier_semaphore()

    def greet(step, carry):
        other = lax.rem(dp + step, count)
        pl.semaphore_signal(barrier, inc=1, device_id=(other, section), device_id_type=MESH)
        return carry

    lax.fori_loop(1, count, greet, 0)
    pl.semaphore_signal(barrier, inc=1, device_id=(dp, peer), device_id_type=MESH)
    pl.semaphore_wait(barrier, count)

    def pair_copy(step):
        return pltpu.make_async_remote_copy(
            src_ref=pair_send.at[lax.rem(step, 2)],
            dst_ref=pair_recv.at[step],
            send_sem=pair_ss.at[lax.rem(step, 2)],
            recv_sem=pair_rs.at[step],
            device_id=(dp, peer),
            device_id_type=MESH,
        )

    def ring_copy(step, stream):
        ahead = 1 if stream < 3 else count - 1
        return pltpu.make_async_remote_copy(
            src_ref=ring_send.at[lax.rem(step, 2), stream],
            dst_ref=ring_recv.at[step, stream],
            send_sem=ring_ss.at[lax.rem(step, 2), stream],
            recv_sem=ring_rs.at[step, stream],
            device_id=(ring_index(lax.rem(place + ahead, count), count), section),
            device_id_type=MESH,
        )

    def product(step, stream, part):
        if stream < 3:
            block = lax.rem(place + 2 * count - 1 - step, count)
        else:
            block = lax.rem(place + 1 + step, count)
        block = ring_index(block, count)
        if stream % 3 < 2:
            group = stream % 3 + 2 * (stream // 3)
            left_index = jnp.where(part == 1, 2, 1 if group == 3 else 0)
            left = lhs[left_index, pl.ds(pl.multiple_of(block * rows, rows), rows), :]
            right = rhs[part * 4 + group]
        else:
            start = part * half_units + block * (2 * rows) + (stream // 3) * rows
            left = hidden_t[pl.ds(pl.multiple_of(start, rows), rows), :]
            right = dz_down[...]
        return jnp.dot(left, right, preferred_element_type=jnp.float32)

    def local_part(step):
        slot = lax.rem(step, 2)

        @pl.when(step >= 2)
        def _():
            pair_copy(step - 2).wait_send()

        for stream in range(6):
            pair_send[slot, stream] = product(step, stream, 1 - core).astype(jnp.bfloat16)
        pair_copy(step).start()
        for stream in range(6):
            total[stream] = product(step, stream, core)

    gb_pair = pltpu.make_async_remote_copy(
        src_ref=small.at[1 - core],
        dst_ref=small_pair,
        send_sem=small_sems.at[0],
        recv_sem=small_sems.at[1],
        device_id=(dp, peer),
        device_id_type=MESH,
    )
    gb_pair.start()

    def gb_copy(step):
        other = lax.rem(dp + step, count)
        return pltpu.make_async_remote_copy(
            src_ref=small_sum.at[other],
            dst_ref=small_recv.at[step],
            send_sem=small_ss.at[step],
            recv_sem=small_rs.at[step],
            device_id=(other, section),
            device_id_type=MESH,
        )

    local_part(0)
    gb_pair.wait()
    small_sum[...] = small[core] + small_pair[...]

    def gb_start(step, carry):
        gb_copy(step).start()
        return carry

    lax.fori_loop(1, count, gb_start, 0)

    def ring_step(step, carry):
        slot = lax.rem(step, 2)
        pair_copy(step).wait_recv()
        for stream in (0, 3, 1, 4, 2, 5):
            total[stream] += pair_recv[step, stream].astype(jnp.float32)

            @pl.when(step >= 1)
            def _():
                ring_copy(step - 1, stream).wait_recv()
                total[stream] += ring_recv[step - 1, stream].astype(jnp.float32)

            @pl.when(step >= 2)
            def _():
                ring_copy(step - 2, stream).wait_send()

            ring_send[slot, stream] = total[stream].astype(jnp.bfloat16)
            ring_copy(step, stream).start()
        local_part(step + 1)
        return carry

    lax.fori_loop(0, count - 1, ring_step, 0)

    last = count - 1
    pair_copy(last).wait_recv()
    width = total.shape[2]
    for stream in (0, 3, 1, 4, 2, 5):
        ring_copy(last - 1, stream).wait_recv()
        value = total[stream] + pair_recv[last, stream].astype(jnp.float32)
        value = value + ring_recv[last - 1, stream].astype(jnp.float32)
        if stream % 3 < 2:
            group = stream % 3 + 2 * (stream // 3)
            first_out[:, group * width : (group + 1) * width] = value
        else:
            down_out[(stream // 3) * rows : (stream // 3 + 1) * rows, :] = value

    small_out[...] = small_sum[dp]

    def gb_finish(step, carry):
        gb_copy(step).wait()
        small_out[...] += small_recv[step]
        return carry

    lax.fori_loop(1, count, gb_finish, 0)
    for stream in range(6):
        ring_copy(last - 1, stream).wait_send()
        if count >= 3:
            ring_copy(last - 2, stream).wait_send()
    pair_copy(last).wait_send()
    pair_copy(last - 1).wait_send()


def reduce_gradients(lhs, hidden_t, rhs, dz_down, small):
    count = lax.axis_size("dp")
    width = rhs.shape[2]
    rows = width // count
    vmem = pl.BlockSpec(memory_space=pltpu.VMEM)
    sem = pltpu.SemaphoreType.DMA
    low = jnp.bfloat16
    return pl.pallas_call(
        functools.partial(gradient_kernel, count),
        out_shape=(
            jax.ShapeDtypeStruct((rows, 4 * width), jnp.float32),
            jax.ShapeDtypeStruct((2 * rows, width), jnp.float32),
            jax.ShapeDtypeStruct(small.shape[2:], jnp.float32),
        ),
        in_specs=[vmem] * 5,
        out_specs=(vmem, vmem, vmem),
        scratch_shapes=[
            pltpu.VMEM((6, rows, width), jnp.float32),
            pltpu.VMEM((2, 6, rows, width), low),
            pltpu.VMEM((count, 6, rows, width), low),
            pltpu.VMEM((2, 6, rows, width), low),
            pltpu.VMEM((count - 1, 6, rows, width), low),
            pltpu.VMEM(small.shape[1:], jnp.float32),
            pltpu.VMEM(small.shape[1:], jnp.float32),
            pltpu.VMEM(small.shape[1:], jnp.float32),
            sem((2,)),
            sem((count,)),
            sem((2, 6)),
            sem((count - 1, 6)),
            sem((2,)),
            sem((count,)),
            sem((count,)),
        ],
        compiler_params=pltpu.CompilerParams(
            collective_id=0, has_side_effects=True, vmem_limit_bytes=60 * 1024 * 1024
        ),
        name="gradients",
    )(lhs, hidden_t, rhs, dz_down, small)


def local(tokens, doc_lengths, first_weights, down_weights, norm_gains, norm_biases, cotangent):
    section_index = lax.axis_index("section")
    count = lax.axis_size("dp")
    core = section_index % 2
    late = section_index >= 2
    row_count = doc_lengths.shape[0]
    row_len = tokens.shape[0] // row_count
    width = tokens.shape[1]
    peer_first, peer_down, peer_gains, peer_biases = (
        swap_pair(first_weights[0]),
        swap_pair(down_weights[0]),
        swap_pair(norm_gains[0]),
        swap_pair(norm_biases[0]),
    )

    def ordered(own, other):
        return jnp.where(core == 0, own, other), jnp.where(core == 0, other, own)

    weight_a, weight_f = ordered(first_weights[0], peer_first)
    down_upper, down_lower = ordered(down_weights[0], peer_down)
    gains = ordered(norm_gains[0], peer_gains)
    biases = ordered(norm_biases[0], peer_biases)
    half_units = down_upper.shape[0]
    scale = HEAD ** (-0.5)
    low = jnp.bfloat16

    row = tokens.reshape(row_count, row_len, width)[core]
    row_cot = cotangent.reshape(row_count, row_len, width)[core]
    allowed = allowed_pairs(doc_lengths[core], row_len)[None]

    def scores_of(projected):
        query, key = (split_heads(projected[:, i * width : (i + 1) * width]) for i in (0, 1))
        scores = jnp.einsum("qhd,khd->hqk", query, key, preferred_element_type=jnp.float32)
        return jnp.where(allowed, scores * scale, masked_value)

    def forward(inputs):
        current = inputs.astype(jnp.float32)
        normed_a = normalize(current, gains[0][0], biases[0][0]).astype(low)
        projected = jnp.dot(
            normed_a, weight_a[:, : 3 * width], preferred_element_type=jnp.float32
        ).astype(low)
        scores = scores_of(projected)
        row_top = jnp.max(scores, axis=-1, keepdims=True)
        exponent = jnp.exp(scores - row_top)
        row_total = jnp.sum(exponent, axis=-1, keepdims=True)
        prob = (exponent / row_total).astype(low)
        context = jnp.einsum(
            "hqk,khd->qhd",
            prob,
            split_heads(projected[:, 2 * width :]),
            preferred_element_type=jnp.float32,
        )
        context = context.reshape(row_len, width).astype(low)
        branch_a = contract_cols(context, weight_a[:, 3 * width :])
        log_total = row_top + jnp.log(row_total)
        middle = (current + normalize(branch_a, gains[0][1], biases[0][1])).astype(low)
        normed_f = normalize(middle.astype(jnp.float32), gains[1][0], biases[1][0]).astype(low)
        hidden_pre = jnp.dot(normed_f, weight_f, preferred_element_type=jnp.float32)
        hidden = jax.nn.gelu(hidden_pre).astype(low)
        branch_f = jnp.dot(hidden[:, :half_units], down_upper, preferred_element_type=jnp.float32)
        branch_f = branch_f + jnp.dot(
            hidden[:, half_units:], down_lower, preferred_element_type=jnp.float32
        )
        output = middle.astype(jnp.float32) + normalize(branch_f, gains[1][1], biases[1][1])
        kept = (inputs, projected, context, log_total, branch_a, middle, hidden_pre, branch_f)
        return output.astype(low), kept

    arriving = hop(forward(row)[0], 2)
    output, kept = forward(jnp.where(late, arriving, row))
    inputs, projected, context, log_total, branch_a, middle, hidden_pre, branch_f = kept

    def backward(upstream):
        grad_out = upstream.astype(jnp.float32)
        out_back = jax.vjp(normalize, branch_f, gains[1][1], biases[1][1])[1]
        dz_f, dg_f1, db_f1 = out_back(grad_out)
        dz_f = dz_f.astype(low)
        hidden_full, gelu_back = jax.vjp(jax.nn.gelu, hidden_pre)
        d_hidden = jnp.concatenate(
            [contract_cols(dz_f, down_upper), contract_cols(dz_f, down_lower)], axis=1
        )
        d_pre = gelu_back(d_hidden)[0].astype(low)
        normed_f, in_back = jax.vjp(
            normalize, middle.astype(jnp.float32), gains[1][0], biases[1][0]
        )
        d_ln, dg_f0, db_f0 = in_back(contract_cols(d_pre, weight_f))
        d_middle = (grad_out + d_ln).astype(low)

        grad_mid = d_middle.astype(jnp.float32)
        out_back = jax.vjp(normalize, branch_a, gains[0][1], biases[0][1])[1]
        dz_a, dg_a1, db_a1 = out_back(grad_mid)
        dz_a = dz_a.astype(low)
        d_context = split_heads(
            jnp.dot(dz_a, weight_a[:, 3 * width :], preferred_element_type=jnp.float32).astype(low)
        )
        query, key, value = (
            split_heads(projected[:, i * width : (i + 1) * width]) for i in range(3)
        )
        prob = jnp.exp(scores_of(projected) - log_total)
        d_prob = jnp.einsum("qhd,khd->hqk", d_context, value, preferred_element_type=jnp.float32)
        d_value = jnp.einsum(
            "hqk,qhd->khd", prob.astype(low), d_context, preferred_element_type=jnp.float32
        )
        d_scores = prob * (d_prob - jnp.sum(d_prob * prob, axis=-1, keepdims=True))
        d_scores = d_scores.astype(low)
        d_query = scale * jnp.einsum(
            "hqk,khd->qhd", d_scores, key, preferred_element_type=jnp.float32
        )
        d_key = scale * jnp.einsum(
            "hqk,qhd->khd", d_scores, query, preferred_element_type=jnp.float32
        )
        d_proj = [v.reshape(row_len, width).astype(low) for v in (d_query, d_key, d_value)]
        normed_a, in_back = jax.vjp(
            normalize, inputs.astype(jnp.float32), gains[0][0], biases[0][0]
        )
        d_normed = contract_cols(jnp.concatenate(d_proj, axis=1), weight_a[:, : 3 * width])
        d_ln, dg_a0, db_a0 = in_back(d_normed)
        d_input = (grad_mid + d_ln).astype(low)
        small = jnp.stack([dg_a0, dg_a1, db_a0, db_a1, dg_f0, dg_f1, db_f0, db_f1])
        lhs = jnp.stack([normed_a.astype(low).T, dz_a.T, normed_f.astype(low).T])
        rhs = jnp.stack(d_proj + [context] + jnp.split(d_pre, 4, axis=1))
        return d_input, (lhs, hidden_full.astype(low).T, rhs, dz_f, small, d_middle)

    arriving = hop(backward(row_cot)[0], -2)
    d_input, parts = backward(jnp.where(late, row_cot, arriving))
    lhs, hidden_t, rhs, dz_f, small, d_middle = parts

    slices = small.reshape(2, 4, count, width // count).transpose(0, 2, 1, 3)
    slices = jnp.pad(slices, ((0, 0), (0, 0), (0, 4), (0, 128 - width // count)))
    first_part, down_part, small_part = reduce_gradients(lhs, hidden_t, rhs, dz_f, slices)
    small_part = small_part[:4, : width // count].reshape(2, 2, width // count)

    def both_rows(for_attention, for_feed):
        own = jnp.where(core == 0, for_attention, for_feed)
        other = swap_pair(jnp.where(core == 0, for_feed, for_attention))
        return jnp.concatenate(ordered(own, other), axis=0)

    return (
        both_rows(middle, output)[None],
        both_rows(d_input, d_middle)[None],
        first_part[None],
        down_part[None],
        small_part[0][None],
        small_part[1][None],
    )


def solution(mesh):
    placed = (
        P("dp", None),
        P("dp", None),
        P("section", None, None),
        P("section", None, None),
        P("section", None, None),
        P("section", None, None),
        P("dp", None),
    )
    return jax.shard_map(
        local,
        mesh=mesh,
        in_specs=placed,
        out_specs=(
            P("section", "dp", None),
            P("section", "dp", None),
            P("section", "dp", None),
            P("section", "dp", None),
            P("section", None, "dp"),
            P("section", None, "dp"),
        ),
        check_vma=False,
    )
```

```python
import functools

import jax
import jax.numpy as jnp
from jax import lax
from jax.experimental import pallas as pl
from jax.experimental.pallas import tpu as pltpu
from jax.sharding import PartitionSpec as P

HEADS = 16
HEAD = 64
PAIRS = HEADS // 2
LANES = 2 * HEAD
eps = 1e-05
masked_value = -1e30
score_scale = HEAD ** (-0.5)
MESH = pl.DeviceIdType.MESH
low = jnp.bfloat16
f32 = jnp.float32
tanh_linear = (2.0 / 3.141592653589793) ** 0.5
tanh_cubic = tanh_linear * 0.044715


def ring_place(index, count):
    return jnp.where(index % 2 == 0, index // 2, count - 1 - index // 2)


def ring_index(place, count):
    return jnp.where(place < count // 2, 2 * place, 2 * (count - 1 - place) + 1)


def dot(left, right):
    return jnp.dot(left, right, preferred_element_type=f32)


def dot_cols(left, right):
    return lax.dot_general(left, right, (((1,), (1,)), ((), ())), preferred_element_type=f32)


def whiten(values):
    average = jnp.mean(values, axis=-1, keepdims=True)
    centered = values - average
    variance = jnp.mean(centered * centered, axis=-1, keepdims=True)
    spread = lax.rsqrt(variance + eps)
    return centered * spread, spread


def whiten_back(grad, normal, spread):
    first = jnp.mean(grad, axis=-1, keepdims=True)
    second = jnp.mean(grad * normal, axis=-1, keepdims=True)
    return spread * (grad - first - normal * second)


def gelu(u):
    inner = u * (tanh_linear + tanh_cubic * (u * u))
    return u * (0.5 + 0.5 * jnp.tanh(inner))


def gelu_both(u):
    square = u * u
    half = 0.5 + 0.5 * jnp.tanh(u * (tanh_linear + tanh_cubic * square))
    value = u * half
    slope = half + value * (1.0 - half) * (2.0 * tanh_linear + 6.0 * tanh_cubic * square)
    return value, slope


def layers_kernel(
    count,
    tokens,
    cotangent,
    lengths,
    first,
    down,
    gains,
    biases,
    outputs,
    input_grads,
    first_grad,
    down_grad,
    small_out,
    pool,
    sends,
    stash,
    grad_in,
    spreads,
    kept,
    grads,
    mask,
    total,
    lhs,
    hidden_t,
    rhs,
    dz_down,
    affine,
    log_t,
    log_rows,
    delta_t,
    sums,
    small,
    small_pair,
    small_sum,
    small_recv,
    weight_ls,
    weight_ss,
    weight_rs,
    row_ls,
    hop_ss,
    hop_rs,
    out_ls,
    out_ss,
    out_rs,
    ready,
    pair_ss,
    pair_rs,
    ring_ss,
    ring_rs,
    small_sems,
    small_ss,
    small_rs,
    grad_ls,
):
    rows, width = pool.shape[1:]
    row_len = rhs.shape[1]
    unit = row_len // 2
    blocks = unit // rows
    dp = lax.axis_index("dp")
    section = lax.axis_index("section")
    section_count = lax.axis_size("section")
    core = lax.rem(section, 2)
    peer = section + 1 - 2 * core
    early = section < 2
    late = section >= 2
    partner = lax.rem(section + 2, section_count)
    place = ring_place(dp, count)
    left = ring_index(lax.rem(place + count - 1, count), count)
    right = ring_index(lax.rem(place + 1, count), count)

    barrier = pltpu.get_barrier_semaphore()

    def greet(step, carry):
        other = lax.rem(dp + step, count)
        pl.semaphore_signal(barrier, inc=1, device_id=(other, section), device_id_type=MESH)
        return carry

    lax.fori_loop(1, count, greet, 0)
    for other in (peer, partner):
        pl.semaphore_signal(barrier, inc=1, device_id=(dp, other), device_id_type=MESH)

    def own_chunk(k):
        if k < 4:
            return first.at[:, :, pl.ds(k * width, width)], 4 * core + k
        return down.at[pl.ds((k - 4) * count, count)], 8 + 2 * core + k - 4

    def weight_local(k):
        source, chunk = own_chunk(k)
        target = pool.at[pl.ds(chunk * count, count)]
        return pltpu.make_async_copy(source, target, weight_ls.at[k])

    def to_peer(source, target, send_sem, recv_sem):
        return pltpu.make_async_remote_copy(
            src_ref=source,
            dst_ref=target,
            send_sem=send_sem,
            recv_sem=recv_sem,
            device_id=(dp, peer),
            device_id_type=MESH,
        )

    def weight_remote(k):
        source, chunk = own_chunk(k)
        target = pool.at[pl.ds(chunk * count, count)]
        return to_peer(source, target, weight_ss.at[k], weight_rs.at[k])

    def affine_local(i):
        source = (gains, biases)[i].at[0]
        return pltpu.make_async_copy(source, affine.at[core, i], weight_ls.at[6 + i])

    def affine_remote(i):
        source = (gains, biases)[i].at[0]
        return to_peer(source, affine.at[core, i], weight_ss.at[6 + i], weight_rs.at[6 + i])

    def await_chunk(chunk):
        owner = 1 if 4 <= chunk < 8 or chunk >= 10 else 0
        k = chunk % 4 if chunk < 8 else 4 + chunk % 2

        @pl.when(core == owner)
        def _():
            weight_local(k).wait()

        @pl.when(core != owner)
        def _():
            weight_remote(k).wait_recv()

    def weight(chunk):
        return pool[pl.ds(chunk * count, count)].reshape(width, width)

    def weight_cols(chunk, some):
        return pool[pl.ds(chunk * count, count), :, some].reshape(width, width // 2)

    def weight_rows(chunk, half):
        start = chunk * count + half * (count // 2)
        return pool[pl.ds(start, count // 2)].reshape(width // 2, width)

    def stash_at(place_in):
        return stash.at[pl.ds(place_in * blocks, blocks)]

    def stash_read(place_in):
        return stash[pl.ds(place_in * blocks, blocks)].reshape(unit, width)

    def stash_write(place_in, value):
        stash[pl.ds(place_in * blocks, blocks)] = value.astype(low).reshape(blocks, rows, width)

    def row_copy(u, source, target, sem):
        start = (core * 2 + u) * blocks
        return pltpu.make_async_copy(source.at[pl.ds(start, blocks)], target, sem)

    def token_copy(u):
        return row_copy(u, tokens, stash_at(u), row_ls.at[u])

    def cotangent_copy(u):
        return row_copy(u, cotangent, grad_in.at[u], row_ls.at[2 + u])

    def hop_copy(k):
        u = k % 2
        return pltpu.make_async_remote_copy(
            src_ref=kept.at[1, u] if k < 2 else grads.at[0, u],
            dst_ref=stash_at(u) if k < 2 else grad_in.at[u],
            send_sem=hop_ss.at[k],
            recv_sem=hop_rs.at[k],
            device_id=(dp, partner),
            device_id_type=MESH,
        )

    def out_copies(kind, u):
        source, target = ((kept, outputs), (grads, input_grads))[kind]
        place_out = target.at[pl.ds((core * 2 + u) * blocks, blocks)]
        k = 2 * kind + u
        return (
            pltpu.make_async_copy(source.at[core, u], place_out, out_ls.at[k]),
            to_peer(source.at[1 - core, u], place_out, out_ss.at[k], out_rs.at[k]),
        )

    for k in range(6):
        weight_local(k).start()
    for i in range(2):
        affine_local(i).start()

    @pl.when(early)
    def _():
        for u in range(2):
            token_copy(u).start()

    @pl.when(late)
    def _():
        for u in range(2):
            cotangent_copy(u).start()

    pl.semaphore_wait(barrier, count + 1)
    for i in range(2):
        affine_remote(i).start()
    for k in range(6):
        weight_remote(k).start()

    sums[...] = jnp.zeros_like(sums)
    log_rows[...] = jnp.zeros_like(log_rows)
    small[...] = jnp.zeros_like(small)
    for i in range(2):
        affine_local(i).wait()
        affine_remote(i).wait_recv()

    def gain(sub, which):
        return affine[sub, 0, which : which + 1, :]

    def bias(sub, which):
        return affine[sub, 1, which : which + 1, :]

    ends = [lengths[core, 0]]
    for j in range(1, lengths.shape[1]):
        ends.append(ends[-1] + lengths[core, j])

    def mask_of(shape, query_axis, first_query, first_key):
        query = lax.broadcasted_iota(jnp.int32, shape, query_axis) + first_query
        key = lax.broadcasted_iota(jnp.int32, shape, 1 - query_axis) + first_key
        apart = jnp.zeros(shape, jnp.int32)
        for end in ends:
            apart += (query >= end).astype(jnp.int32) - (key >= end).astype(jnp.int32)
        return jnp.where((apart == 0) & (key <= query), 0.0, masked_value)

    def projected(part, lanes, u=0, halves=1):
        span = pl.ds((2 * part + u) * blocks, halves * blocks)
        return sends[span, :, lanes].reshape(halves * unit, LANES)

    def half_lanes(h, scale):
        lane = lax.broadcasted_iota(jnp.int32, (1, LANES), 1)
        return jnp.where((lane >= h * HEAD) & (lane < (h + 1) * HEAD), scale, 0.0)

    def pair_lanes(p):
        return pl.ds(pl.multiple_of(p * LANES, LANES), LANES)

    def branch():
        return total[pl.ds(2 * blocks, blocks)].reshape(unit, width)

    def add_branch(term, begin):
        value = term if begin else branch() + term
        total[pl.ds(2 * blocks, blocks)] = value.reshape(blocks, rows, width)

    size = min(rows, 32)
    groups = rows // size

    def by_rows(body):
        def step(i, carry):
            block, start = i // groups, pl.multiple_of(lax.rem(i, groups) * size, size)
            body(block, pl.ds(start, size), pl.ds(pl.multiple_of(i * size, size), size))
            return carry

        lax.fori_loop(0, unit // size, step, 0, unroll=2)

    def add_sums(sub, which, grad, normal):
        row = 4 * sub + which
        sums[row] += jnp.sum((grad * normal).reshape(size // 8, 8, width), axis=0)
        sums[row + 2] += jnp.sum(grad.reshape(size // 8, 8, width), axis=0)

    def normed_input(sub, values):
        return (whiten(values)[0] * gain(sub, 0) + bias(sub, 0)).astype(low)

    def attention_forward(u):
        span = slice(u * unit, (u + 1) * unit)

        def norm_in(block, some, _):
            values = stash[u * blocks + block, some, :].astype(f32)
            stash[6 * blocks + block, some, :] = normed_input(0, values)

        by_rows(norm_in)
        for part in range(3):
            if u == 0:
                await_chunk(part)
            value = dot(stash_read(6), weight(part)).astype(low)
            sends[pl.ds((2 * part + u) * blocks, blocks)] = value.reshape(blocks, rows, width)
        lhs[0, :, span] = stash_read(6).T
        for i in range(u + 1):
            mask[i * unit : (i + 1) * unit, :] = mask_of((unit, unit), 0, u * unit, i * unit)
        lane = lax.broadcasted_iota(jnp.int32, (unit, LANES), 1)

        def pair(p, carry):
            lanes = pair_lanes(p)
            query = projected(0, lanes, u).astype(f32)
            key = projected(1, lanes, 0, u + 1)
            value = projected(2, lanes, 0, u + 1)
            added = jnp.concatenate([mask[i * unit : (i + 1) * unit, :] for i in range(u + 1)], 1)
            context = None
            for h in range(2):
                scores = dot_cols((query * half_lanes(h, score_scale)).astype(low), key)
                scores = scores + added
                top = jnp.max(scores, axis=-1, keepdims=True)
                exponent = jnp.exp(scores - top)
                summed = jnp.sum(exponent, axis=-1, keepdims=True)
                part = dot(exponent.astype(low), value) * (1.0 / summed)
                context = part if h == 0 else jnp.where(lane < HEAD, context, part)
                log_total = top + jnp.log(summed)
                log_rows[...] = jnp.where(lane == 2 * p + h, log_total, log_rows[...])
            rhs[3, span, lanes] = context.astype(low)
            return carry

        lax.fori_loop(0, PAIRS, pair, 0)
        log_t[u] = log_rows[...].T[:HEADS]
        if u == 0:
            await_chunk(3)
        add_branch(dot_cols(rhs[3, span, :], weight(3)), True)

        def norm_out(block, some, across):
            normal, spread = whiten(total[2 * blocks + block, some, :])
            stash[(2 + u) * blocks + block, some, :] = normal.astype(low)
            spreads[pl.ds(u * unit + across.start, size), 0:1] = spread
            middle = stash[u * blocks + block, some, :].astype(f32)
            middle = (middle + (normal * gain(0, 1) + bias(0, 1))).astype(low)
            kept[0, u, block, some, :] = middle
            stash[6 * blocks + block, some, :] = normed_input(1, middle.astype(f32))

        by_rows(norm_out)

    def feed_forward(u):
        span = slice(u * unit, (u + 1) * unit)
        lhs[2, :, span] = stash_read(6).T
        for c in range(4):
            if u == 0:
                await_chunk(4 + c)
                await_chunk(8 + c)
            for half in range(2):
                some = slice(half * (width // 2), (half + 1) * (width // 2))
                hidden_pre = dot(stash_read(6), weight_cols(4 + c, some))
                rhs[4 + c, span, some] = hidden_pre.astype(low)
                term = dot(gelu(hidden_pre).astype(low), weight_rows(8 + c, half))
                add_branch(term, c + half == 0)

        def norm_out(block, some, across):
            normal, spread = whiten(total[2 * blocks + block, some, :])
            stash[(4 + u) * blocks + block, some, :] = normal.astype(low)
            spreads[pl.ds(u * unit + across.start, size), 1:2] = spread
            middle = kept[0, u, block, some, :].astype(f32)
            output = middle + (normal * gain(1, 1) + bias(1, 1))
            kept[1, u, block, some, :] = output.astype(low)

        by_rows(norm_out)

    def feed_backward(u):
        span = slice(u * unit, (u + 1) * unit)

        def back_out(block, some, across):
            own = pl.ds(u * unit + across.start, size)
            upstream = grad_in[u, block, some, :].astype(f32)
            normal = stash[(4 + u) * blocks + block, some, :].astype(f32)
            add_sums(1, 1, upstream, normal)
            dz = whiten_back(upstream * gain(1, 1), normal, spreads[own, 1:2])
            dz_down[own, :] = dz.astype(low)

        by_rows(back_out)
        for c in range(4):
            for half in range(2):
                some = slice(half * (width // 2), (half + 1) * (width // 2))
                start = (2 * c + half) * (width // 2)
                d_hidden = dot_cols(dz_down[span, :], weight_rows(8 + c, half))
                hidden, slope = gelu_both(rhs[4 + c, span, some].astype(f32))
                hidden_t[start : start + width // 2, span] = hidden.astype(low).T
                d_pre = (d_hidden * slope).astype(low)
                rhs[4 + c, span, some] = d_pre
                term = dot_cols(d_pre, weight_cols(4 + c, some))
                add_branch(term, c + half == 0)

        def back_in(block, some, across):
            own = pl.ds(u * unit + across.start, size)
            normal, spread = whiten(kept[0, u, block, some, :].astype(f32))
            d_normed = total[2 * blocks + block, some, :]
            add_sums(1, 0, d_normed, normal)
            d_ln = whiten_back(d_normed * gain(1, 0), normal, spread)
            d_middle = (grad_in[u, block, some, :].astype(f32) + d_ln).astype(low)
            grads[1, u, block, some, :] = d_middle
            upstream = d_middle.astype(f32)
            normal = stash[(2 + u) * blocks + block, some, :].astype(f32)
            add_sums(0, 1, upstream, normal)
            dz = whiten_back(upstream * gain(0, 1), normal, spreads[own, 0:1])
            stash[6 * blocks + block, some, :] = dz.astype(low)

        by_rows(back_in)

    def attention_backward(u):
        span = slice(u * unit, (u + 1) * unit)
        keys = (u + 1) * unit
        lhs[1, :, span] = stash_read(6).T
        d_context = dot(stash_read(6), weight(3)).astype(low)
        stash_write(6, d_context)
        product = (d_context.astype(f32) * rhs[3, span, :].astype(f32)).astype(low)
        head = lax.broadcasted_iota(jnp.int32, (HEADS, width), 0)
        column = lax.broadcasted_iota(jnp.int32, (HEADS, width), 1)
        inside = (column >= head * HEAD) & (column < (head + 1) * HEAD)
        delta_t[...] = dot_cols(jnp.where(inside, 1.0, 0.0).astype(low), product)
        mask[:keys, :] = mask_of((keys, unit), 1, u * unit, 0)

        def pair(p, carry):
            lanes = pair_lanes(p)
            query = projected(0, lanes, u).astype(f32)
            key = projected(1, lanes, 0, u + 1)
            value = projected(2, lanes, 0, u + 1)
            d_out = stash[pl.ds(6 * blocks, blocks), :, lanes].reshape(unit, LANES).astype(f32)
            key_t = key.T
            d_key = d_value = None
            d_query = []
            for h in range(2):
                query_h = (query * half_lanes(h, score_scale)).astype(low)
                d_out_h = (d_out * half_lanes(h, 1.0)).astype(low)
                scores = dot_cols(key, query_h) + mask[:keys, :]
                prob = jnp.exp(scores - log_t[u, pl.ds(2 * p + h, 1), :])
                d_prob = dot_cols(value, d_out_h)
                d_scores = (prob * (d_prob - delta_t[pl.ds(2 * p + h, 1), :])).astype(low)
                term_v = dot(prob.astype(low), d_out_h)
                term_k = dot(d_scores, query_h)
                d_value = term_v if h == 0 else d_value + term_v
                d_key = term_k if h == 0 else d_key + term_k
                d_query.append(dot(key_t[h * HEAD : (h + 1) * HEAD, :], d_scores))
            d_query = jnp.concatenate(d_query, axis=0) * score_scale
            rhs[0, span, lanes] = d_query.T.astype(low)
            for i, grad in ((0, d_key), (1, d_value)):
                carried = pl.ds(i * blocks, blocks)
                if u == 1:
                    rhs[1 + i, span, lanes] = grad[unit:].astype(low)
                    total[carried, :, lanes] = grad[:unit].reshape(blocks, rows, LANES)
                else:
                    grad = grad + total[carried, :, lanes].reshape(unit, LANES)
                    rhs[1 + i, span, lanes] = grad.astype(low)
            return carry

        lax.fori_loop(0, PAIRS, pair, 0)
        for part in range(3):
            add_branch(dot_cols(rhs[part, span, :], weight(part)), part == 0)

        def back_in(block, some, across):
            normal, spread = whiten(stash[u * blocks + block, some, :].astype(f32))
            d_normed = total[2 * blocks + block, some, :]
            add_sums(0, 0, d_normed, normal)
            d_ln = whiten_back(d_normed * gain(0, 0), normal, spread)
            d_input = grads[1, u, block, some, :].astype(f32) + d_ln
            grads[0, u, block, some, :] = d_input.astype(low)

        by_rows(back_in)

    for u in range(2):

        @pl.when(early)
        def _():
            token_copy(u).wait()

        @pl.when(late)
        def _():
            hop_copy(u).wait_recv()

        attention_forward(u)
        feed_forward(u)

        @pl.when(early)
        def _():
            hop_copy(u).start()

        for copy in out_copies(0, u):
            copy.start()

    for u in (1, 0):

        @pl.when(late)
        def _():
            cotangent_copy(u).wait()

        @pl.when(early)
        def _():
            hop_copy(2 + u).wait_recv()

        feed_backward(u)
        attention_backward(u)

        @pl.when(late)
        def _():
            hop_copy(2 + u).start()

        for copy in out_copies(1, u):
            copy.start()

    for k in range(8):
        (weight_remote(k) if k < 6 else affine_remote(k - 6)).wait_send()
    for ring_end in (left, right):
        pl.semaphore_signal(ready, inc=1, device_id=(ring_end, section), device_id_type=MESH)
    pl.semaphore_signal(ready, inc=1, device_id=(dp, peer), device_id_type=MESH)

    slice_width = width // count
    for j in range(count):
        piece = sums[:, :, j * slice_width : (j + 1) * slice_width]
        small[j, :, :slice_width] = jnp.sum(piece, axis=1)

    @pl.when(late)
    def _():
        for u in range(2):
            hop_copy(2 + u).wait_send()

    def pair_copy(step):
        return to_peer(
            stash.at[pl.ds(6 * lax.rem(step, 2), 6)],
            pool.at[pl.ds(6 * step, 6)],
            pair_ss.at[lax.rem(step, 2)],
            pair_rs.at[step],
        )

    def ring_block(step, stream):
        return 6 * count + 6 * step + stream

    def ring_copy(step, stream):
        return pltpu.make_async_remote_copy(
            src_ref=sends.at[6 * lax.rem(step, 2) + stream],
            dst_ref=pool.at[ring_block(step, stream)],
            send_sem=ring_ss.at[lax.rem(step, 2), stream],
            recv_sem=ring_rs.at[step, stream],
            device_id=(right if stream < 3 else left, section),
            device_id_type=MESH,
        )

    def product(step, stream, part):
        if stream < 3:
            block = lax.rem(place + 2 * count - 1 - step, count)
        else:
            block = lax.rem(place + 1 + step, count)
        block = ring_index(block, count)
        if stream % 3 < 2:
            group = stream % 3 + 2 * (stream // 3)
            side = jnp.where(part == 1, 2, 1 if group == 3 else 0)
            piece = lhs[side, pl.ds(pl.multiple_of(block * rows, rows), rows), :]
            return dot(piece, rhs[part * 4 + group])
        start = part * (2 * width) + block * (2 * rows) + (stream // 3) * rows
        return dot(hidden_t[pl.ds(pl.multiple_of(start, rows), rows), :], dz_down[...])

    def pair_part(step):
        slot = lax.rem(step, 2)
        for stream in range(6):
            stash[6 * slot + stream] = product(step, stream, 1 - core).astype(low)

    def own_part(step):
        for stream in range(6):
            total[stream] = product(step, stream, core)

    gb_pair = to_peer(small, small_pair, small_sems.at[0], small_sems.at[1])

    def gb_copy(step):
        other = lax.rem(dp + step, count)
        return pltpu.make_async_remote_copy(
            src_ref=small_sum.at[other],
            dst_ref=small_recv.at[step],
            send_sem=small_ss.at[step],
            recv_sem=small_rs.at[step],
            device_id=(other, section),
            device_id_type=MESH,
        )

    pair_part(0)
    pl.semaphore_wait(ready, 3)
    pair_copy(0).start()
    gb_pair.start()
    own_part(0)
    gb_pair.wait()
    small_sum[...] = small[...] + small_pair[...]

    def gb_start(step, carry):
        gb_copy(step).start()
        return carry

    lax.fori_loop(1, count, gb_start, 0)

    def ring_step(step, carry):
        pair_copy(step).wait_recv()
        for stream in (0, 3, 1, 4, 2, 5):
            total[stream] += pool[6 * step + stream].astype(f32)

            @pl.when(step >= 1)
            def _():
                ring_copy(step - 1, stream).wait_recv()
                total[stream] += pool[ring_block(step - 1, stream)].astype(f32)

            @pl.when(step >= 2)
            def _():
                ring_copy(step - 2, stream).wait_send()

            sends[6 * lax.rem(step, 2) + stream] = total[stream].astype(low)
            ring_copy(step, stream).start()

        @pl.when(step >= 1)
        def _():
            pair_copy(step - 1).wait_send()

        pair_part(step + 1)
        pair_copy(step + 1).start()
        own_part(step + 1)
        return carry

    lax.fori_loop(0, count - 1, ring_step, 0)

    def grad_copy(stream):
        if stream % 3 < 2:
            group = stream % 3 + 2 * (stream // 3)
            target = first_grad.at[:, pl.ds(group * width, width)]
        else:
            target = down_grad.at[pl.ds((stream // 3) * rows, rows)]
        return pltpu.make_async_copy(total.at[stream], target, grad_ls.at[stream])

    last = count - 1
    pair_copy(last).wait_recv()
    for stream in (0, 3, 1, 4, 2, 5):
        total[stream] += pool[6 * last + stream].astype(f32)
        ring_copy(last - 1, stream).wait_recv()
        total[stream] += pool[ring_block(last - 1, stream)].astype(f32)
        grad_copy(stream).start()

    small_out[...] = small_sum[dp]

    def gb_finish(step, carry):
        gb_copy(step).wait()
        small_out[...] += small_recv[step]
        return carry

    lax.fori_loop(1, count, gb_finish, 0)
    for stream in range(6):
        ring_copy(last - 1, stream).wait_send()
        ring_copy(last - 2, stream).wait_send()
        grad_copy(stream).wait()
    pair_copy(last).wait_send()
    pair_copy(last - 1).wait_send()
    for kind in range(2):
        for u in range(2):
            local_copy, remote_copy = out_copies(kind, u)
            local_copy.wait()
            remote_copy.wait()

    @pl.when(early)
    def _():
        for u in range(2):
            hop_copy(u).wait_send()


def layers(tokens, cotangent, lengths, first, down, gains, biases):
    count = lax.axis_size("dp")
    token_count, width = tokens.shape
    row_len = token_count // lengths.shape[0]
    unit = row_len // 2
    rows = width // count
    blocks = unit // rows
    vmem = pl.BlockSpec(memory_space=pltpu.VMEM)
    anywhere = pl.BlockSpec(memory_space=pl.ANY)
    sem = pltpu.SemaphoreType.DMA
    shape = jax.ShapeDtypeStruct
    buffer = pltpu.VMEM
    cut = (token_count // rows, rows, width)
    small = (count, 8, max(128, width // count))
    outs = pl.pallas_call(
        functools.partial(layers_kernel, count),
        out_shape=(
            shape(cut, low),
            shape(cut, low),
            shape((rows, 4 * width), f32),
            shape((2 * rows, width), f32),
            shape(small[1:], f32),
        ),
        in_specs=[anywhere, anywhere, pl.BlockSpec(memory_space=pltpu.SMEM)] + [anywhere] * 4,
        out_specs=(anywhere, anywhere, anywhere, anywhere, vmem),
        scratch_shapes=[
            buffer((12 * count, rows, width), low),
            buffer((6 * blocks, rows, width), low),
            buffer((7 * blocks, rows, width), low),
            buffer((2, blocks, rows, width), low),
            buffer((row_len, 128), f32),
            buffer((2, 2, blocks, rows, width), low),
            buffer((2, 2, blocks, rows, width), low),
            buffer((row_len, unit), f32),
            buffer((max(6, 3 * blocks), rows, width), f32),
            buffer((3, width, row_len), low),
            buffer((4 * width, row_len), low),
            buffer((8, row_len, width), low),
            buffer((row_len, width), low),
            buffer((2, 2, 2, width), f32),
            buffer((2, HEADS, unit), f32),
            buffer((unit, LANES), f32),
            buffer((HEADS, unit), f32),
            buffer((8, 8, width), f32),
            buffer(small, f32),
            buffer(small, f32),
            buffer(small, f32),
            buffer(small, f32),
            sem((8,)),
            sem((8,)),
            sem((8,)),
            sem((4,)),
            sem((4,)),
            sem((4,)),
            sem((4,)),
            sem((4,)),
            sem((4,)),
            pltpu.SemaphoreType.REGULAR,
            sem((2,)),
            sem((count,)),
            sem((2, 6)),
            sem((count - 1, 6)),
            sem((2,)),
            sem((count,)),
            sem((count,)),
            sem((6,)),
        ],
        compiler_params=pltpu.CompilerParams(
            collective_id=0, has_side_effects=True, vmem_limit_bytes=63 * 1024 * 1024
        ),
        name="layers",
    )(
        tokens.reshape(cut),
        cotangent.reshape(cut),
        lengths,
        first.reshape(count, rows, 4 * width),
        down.reshape(2 * count, rows, width),
        gains,
        biases,
    )
    return outs


def local(tokens, doc_lengths, first_weights, down_weights, norm_gains, norm_biases, cotangent):
    width = tokens.shape[1]
    outputs, input_grads, first_part, down_part, small = layers(
        tokens,
        cotangent,
        doc_lengths,
        first_weights[0],
        down_weights[0],
        norm_gains,
        norm_biases,
    )
    slice_width = width // lax.axis_size("dp")
    for_feed = lax.axis_index("section") % 2 == 1
    small = jnp.where(for_feed, small[4:], small[:4])
    return (
        outputs.reshape((1,) + tokens.shape),
        input_grads.reshape((1,) + tokens.shape),
        first_part[None],
        down_part[None],
        small[None, 0:2, :slice_width],
        small[None, 2:4, :slice_width],
    )


def solution(mesh):
    placed = (
        P("dp", None),
        P("dp", None),
        P("section", None, None),
        P("section", None, None),
        P("section", None, None),
        P("section", None, None),
        P("dp", None),
    )
    return jax.shard_map(
        local,
        mesh=mesh,
        in_specs=placed,
        out_specs=(
            P("section", "dp", None),
            P("section", "dp", None),
            P("section", "dp", None),
            P("section", "dp", None),
            P("section", None, "dp"),
            P("section", None, "dp"),
        ),
        check_vma=False,
    )
```

```python
import functools

import jax
import jax.numpy as jnp
from jax import lax
from jax.experimental import pallas as pl
from jax.experimental.pallas import tpu as pltpu
from jax.sharding import PartitionSpec as P

HEADS = 16
HEAD = 64
PAIRS = HEADS // 2
LANES = 2 * HEAD
eps = 1e-05
masked_value = -1e30
score_scale = HEAD ** (-0.5)
MESH = pl.DeviceIdType.MESH
low = jnp.bfloat16
f32 = jnp.float32
tanh_linear = (2.0 / 3.141592653589793) ** 0.5
tanh_cubic = tanh_linear * 0.044715


def ring_place(index, count):
    return jnp.where(index % 2 == 0, index // 2, count - 1 - index // 2)


def ring_index(place, count):
    return jnp.where(place < count // 2, 2 * place, 2 * (count - 1 - place) + 1)


def dot(left, right):
    return jnp.dot(left, right, preferred_element_type=f32)


def dot_cols(left, right):
    return lax.dot_general(left, right, (((1,), (1,)), ((), ())), preferred_element_type=f32)


def whiten(values):
    average = jnp.mean(values, axis=-1, keepdims=True)
    centered = values - average
    variance = jnp.mean(centered * centered, axis=-1, keepdims=True)
    spread = lax.rsqrt(variance + eps)
    return centered * spread, spread


def whiten_back(grad, normal, spread):
    first = jnp.mean(grad, axis=-1, keepdims=True)
    second = jnp.mean(grad * normal, axis=-1, keepdims=True)
    return spread * (grad - first - normal * second)


def gelu_both(u):
    square = u * u
    half = 0.5 + 0.5 * jnp.tanh(u * (tanh_linear + tanh_cubic * square))
    value = u * half
    slope = half + value * (1.0 - half) * (2.0 * tanh_linear + 6.0 * tanh_cubic * square)
    return value, slope


def layers_kernel(
    count,
    tokens,
    cotangent,
    lengths,
    first,
    down,
    gains,
    biases,
    outputs,
    input_grads,
    first_grad,
    down_grad,
    small_out,
    pool,
    sends,
    stash,
    grad_in,
    spreads,
    kept,
    grads,
    mask,
    total,
    lhs,
    hidden_t,
    rhs,
    dz_down,
    affine,
    log_t,
    log_rows,
    delta_t,
    sums,
    small,
    small_pair,
    small_sum,
    small_recv,
    weight_ls,
    weight_ss,
    weight_rs,
    row_ls,
    hop_ss,
    hop_rs,
    out_ls,
    out_ss,
    out_rs,
    ready,
    pair_ss,
    pair_rs,
    ring_ss,
    ring_rs,
    small_sems,
    small_ss,
    small_rs,
    grad_ls,
):
    rows, width = pool.shape[1:]
    row_len = rhs.shape[1]
    unit = row_len // 2
    blocks = unit // rows
    dp = lax.axis_index("dp")
    section = lax.axis_index("section")
    section_count = lax.axis_size("section")
    core = lax.rem(section, 2)
    peer = section + 1 - 2 * core
    early = section < 2
    late = section >= 2
    partner = lax.rem(section + 2, section_count)
    place = ring_place(dp, count)
    left = ring_index(lax.rem(place + count - 1, count), count)
    right = ring_index(lax.rem(place + 1, count), count)

    barrier = pltpu.get_barrier_semaphore()

    def greet(step, carry):
        other = lax.rem(dp + step, count)
        pl.semaphore_signal(barrier, inc=1, device_id=(other, section), device_id_type=MESH)
        return carry

    lax.fori_loop(1, count, greet, 0)
    for other in (peer, partner):
        pl.semaphore_signal(barrier, inc=1, device_id=(dp, other), device_id_type=MESH)

    def own_chunk(k):
        if k < 4:
            return first.at[:, :, pl.ds(k * width, width)], 4 * core + k
        return down.at[pl.ds((k - 4) * count, count)], 8 + 2 * core + k - 4

    def weight_local(k):
        source, chunk = own_chunk(k)
        target = pool.at[pl.ds(chunk * count, count)]
        return pltpu.make_async_copy(source, target, weight_ls.at[k])

    def to_peer(source, target, send_sem, recv_sem):
        return pltpu.make_async_remote_copy(
            src_ref=source,
            dst_ref=target,
            send_sem=send_sem,
            recv_sem=recv_sem,
            device_id=(dp, peer),
            device_id_type=MESH,
        )

    def weight_remote(k):
        source, chunk = own_chunk(k)
        target = pool.at[pl.ds(chunk * count, count)]
        return to_peer(source, target, weight_ss.at[k], weight_rs.at[k])

    def affine_local(i):
        source = (gains, biases)[i].at[0]
        return pltpu.make_async_copy(source, affine.at[core, i], weight_ls.at[6 + i])

    def affine_remote(i):
        source = (gains, biases)[i].at[0]
        return to_peer(source, affine.at[core, i], weight_ss.at[6 + i], weight_rs.at[6 + i])

    def await_chunk(chunk):
        owner = 1 if 4 <= chunk < 8 or chunk >= 10 else 0
        k = chunk % 4 if chunk < 8 else 4 + chunk % 2

        @pl.when(core == owner)
        def _():
            weight_local(k).wait()

        @pl.when(core != owner)
        def _():
            weight_remote(k).wait_recv()

    def weight(chunk):
        return pool[pl.ds(chunk * count, count)].reshape(width, width)

    def weight_cols(chunk, some):
        return pool[pl.ds(chunk * count, count), :, some].reshape(width, width // 2)

    def weight_rows(chunk, half):
        start = chunk * count + half * (count // 2)
        return pool[pl.ds(start, count // 2)].reshape(width // 2, width)

    def stash_at(place_in):
        return stash.at[pl.ds(place_in * blocks, blocks)]

    def stash_read(place_in):
        return stash[pl.ds(place_in * blocks, blocks)].reshape(unit, width)

    def stash_write(place_in, value):
        stash[pl.ds(place_in * blocks, blocks)] = value.astype(low).reshape(blocks, rows, width)

    def row_copy(u, source, target, sem):
        start = (core * 2 + u) * blocks
        return pltpu.make_async_copy(source.at[pl.ds(start, blocks)], target, sem)

    def token_copy(u):
        return row_copy(u, tokens, stash_at(u), row_ls.at[u])

    def cotangent_copy(u):
        return row_copy(u, cotangent, grad_in.at[u], row_ls.at[2 + u])

    def hop_copy(k):
        u = k % 2
        return pltpu.make_async_remote_copy(
            src_ref=kept.at[1, u] if k < 2 else grads.at[0, u],
            dst_ref=stash_at(u) if k < 2 else grad_in.at[u],
            send_sem=hop_ss.at[k],
            recv_sem=hop_rs.at[k],
            device_id=(dp, partner),
            device_id_type=MESH,
        )

    def out_copies(kind, u):
        source, target = ((kept, outputs), (grads, input_grads))[kind]
        place_out = target.at[pl.ds((core * 2 + u) * blocks, blocks)]
        k = 2 * kind + u
        return (
            pltpu.make_async_copy(source.at[core, u], place_out, out_ls.at[k]),
            to_peer(source.at[1 - core, u], place_out, out_ss.at[k], out_rs.at[k]),
        )

    for k in range(6):
        weight_local(k).start()
    for i in range(2):
        affine_local(i).start()

    @pl.when(early)
    def _():
        for u in range(2):
            token_copy(u).start()

    @pl.when(late)
    def _():
        for u in range(2):
            cotangent_copy(u).start()

    pl.semaphore_wait(barrier, count + 1)
    for i in range(2):
        affine_remote(i).start()
    for k in range(6):
        weight_remote(k).start()

    sums[...] = jnp.zeros_like(sums)
    log_rows[...] = jnp.zeros_like(log_rows)
    small[...] = jnp.zeros_like(small)
    for i in range(2):
        affine_local(i).wait()
        affine_remote(i).wait_recv()

    def gain(sub, which):
        return affine[sub, 0, which : which + 1, :]

    def bias(sub, which):
        return affine[sub, 1, which : which + 1, :]

    ends = [lengths[core, 0]]
    for j in range(1, lengths.shape[1]):
        ends.append(ends[-1] + lengths[core, j])

    def mask_of(shape, query_axis, first_query, first_key):
        query = lax.broadcasted_iota(jnp.int32, shape, query_axis) + first_query
        key = lax.broadcasted_iota(jnp.int32, shape, 1 - query_axis) + first_key
        apart = jnp.zeros(shape, jnp.int32)
        for end in ends:
            apart += (query >= end).astype(jnp.int32) - (key >= end).astype(jnp.int32)
        return jnp.where((apart == 0) & (key <= query), 0.0, masked_value)

    def projected(part, lanes, u=0, halves=1):
        span = pl.ds((2 * part + u) * blocks, halves * blocks)
        return sends[span, :, lanes].reshape(halves * unit, LANES)

    def half_lanes(h, scale):
        lane = lax.broadcasted_iota(jnp.int32, (1, LANES), 1)
        return jnp.where((lane >= h * HEAD) & (lane < (h + 1) * HEAD), scale, 0.0)

    def pair_lanes(p):
        return pl.ds(pl.multiple_of(p * LANES, LANES), LANES)

    def branch():
        return total[pl.ds(2 * blocks, blocks)].reshape(unit, width)

    def add_branch(term, begin):
        value = term if begin else branch() + term
        total[pl.ds(2 * blocks, blocks)] = value.reshape(blocks, rows, width)

    size = min(rows, 64)
    groups = rows // size

    def by_rows(body):
        def step(i, carry):
            block, start = i // groups, pl.multiple_of(lax.rem(i, groups) * size, size)
            body(block, pl.ds(start, size), pl.ds(pl.multiple_of(i * size, size), size))
            return carry

        lax.fori_loop(0, unit // size, step, 0, unroll=True)

    def add_sums(sub, which, grad, normal):
        row = 4 * sub + which
        sums[row] += jnp.sum((grad * normal).reshape(size // 8, 8, width), axis=0)
        sums[row + 2] += jnp.sum(grad.reshape(size // 8, 8, width), axis=0)

    def normed_input(sub, values):
        return (whiten(values)[0] * gain(sub, 0) + bias(sub, 0)).astype(low)

    def attention_forward(u):
        span = slice(u * unit, (u + 1) * unit)

        def norm_in(block, some, _):
            values = stash[u * blocks + block, some, :].astype(f32)
            stash[6 * blocks + block, some, :] = normed_input(0, values)

        by_rows(norm_in)
        for part in range(3):
            if u == 0:
                await_chunk(part)
            value = dot(stash_read(6), weight(part)).astype(low)
            sends[pl.ds((2 * part + u) * blocks, blocks)] = value.reshape(blocks, rows, width)
        lhs[0, :, span] = stash_read(6).T
        for i in range(u + 1):
            mask[i * unit : (i + 1) * unit, :] = mask_of((unit, unit), 0, u * unit, i * unit)
        lane = lax.broadcasted_iota(jnp.int32, (unit, LANES), 1)

        def pair(p, carry):
            lanes = pair_lanes(p)
            query = projected(0, lanes, u).astype(f32)
            key = projected(1, lanes, 0, u + 1)
            value = projected(2, lanes, 0, u + 1)
            added = jnp.concatenate([mask[i * unit : (i + 1) * unit, :] for i in range(u + 1)], 1)
            context = None
            for h in range(2):
                scores = dot_cols((query * half_lanes(h, score_scale)).astype(low), key)
                scores = scores + added
                top = jnp.max(scores, axis=-1, keepdims=True)
                exponent = jnp.exp(scores - top)
                summed = jnp.sum(exponent, axis=-1, keepdims=True)
                part = dot(exponent.astype(low), value) * (1.0 / summed)
                context = part if h == 0 else jnp.where(lane < HEAD, context, part)
                log_total = top + jnp.log(summed)
                log_rows[...] = jnp.where(lane == 2 * p + h, log_total, log_rows[...])
            rhs[3, span, lanes] = context.astype(low)
            return carry

        lax.fori_loop(0, PAIRS, pair, 0, unroll=2)
        log_t[u] = log_rows[...].T[:HEADS]
        if u == 0:
            await_chunk(3)
        add_branch(dot_cols(rhs[3, span, :], weight(3)), True)

        def norm_out(block, some, across):
            normal, spread = whiten(total[2 * blocks + block, some, :])
            stash[(2 + u) * blocks + block, some, :] = normal.astype(low)
            spreads[pl.ds(u * unit + across.start, size), 0:1] = spread
            middle = stash[u * blocks + block, some, :].astype(f32)
            middle = (middle + (normal * gain(0, 1) + bias(0, 1))).astype(low)
            kept[0, u, block, some, :] = middle
            stash[6 * blocks + block, some, :] = normed_input(1, middle.astype(f32))

        by_rows(norm_out)

    def feed_forward(u):
        span = slice(u * unit, (u + 1) * unit)
        lhs[2, :, span] = stash_read(6).T
        for c in range(4):
            if u == 0:
                await_chunk(4 + c)
                await_chunk(8 + c)
            hidden, slope = gelu_both(dot(stash_read(6), weight(4 + c)))
            hidden = hidden.astype(low)
            rhs[4 + c, span, :] = slope.astype(low)
            hidden_t[c * width : (c + 1) * width, span] = hidden.T
            add_branch(dot(hidden, weight(8 + c)), c == 0)

        def norm_out(block, some, across):
            normal, spread = whiten(total[2 * blocks + block, some, :])
            stash[(4 + u) * blocks + block, some, :] = normal.astype(low)
            spreads[pl.ds(u * unit + across.start, size), 1:2] = spread
            middle = kept[0, u, block, some, :].astype(f32)
            output = middle + (normal * gain(1, 1) + bias(1, 1))
            kept[1, u, block, some, :] = output.astype(low)

        by_rows(norm_out)

    def feed_backward(u):
        span = slice(u * unit, (u + 1) * unit)

        def back_out(block, some, across):
            own = pl.ds(u * unit + across.start, size)
            upstream = grad_in[u, block, some, :].astype(f32)
            normal = stash[(4 + u) * blocks + block, some, :].astype(f32)
            add_sums(1, 1, upstream, normal)
            dz = whiten_back(upstream * gain(1, 1), normal, spreads[own, 1:2])
            dz_down[own, :] = dz.astype(low)

        by_rows(back_out)
        for c in range(4):
            d_hidden = dot_cols(dz_down[span, :], weight(8 + c))
            d_pre = (d_hidden * rhs[4 + c, span, :].astype(f32)).astype(low)
            rhs[4 + c, span, :] = d_pre
            add_branch(dot_cols(d_pre, weight(4 + c)), c == 0)

        def back_in(block, some, across):
            own = pl.ds(u * unit + across.start, size)
            normal, spread = whiten(kept[0, u, block, some, :].astype(f32))
            d_normed = total[2 * blocks + block, some, :]
            add_sums(1, 0, d_normed, normal)
            d_ln = whiten_back(d_normed * gain(1, 0), normal, spread)
            d_middle = (grad_in[u, block, some, :].astype(f32) + d_ln).astype(low)
            grads[1, u, block, some, :] = d_middle
            upstream = d_middle.astype(f32)
            normal = stash[(2 + u) * blocks + block, some, :].astype(f32)
            add_sums(0, 1, upstream, normal)
            dz = whiten_back(upstream * gain(0, 1), normal, spreads[own, 0:1])
            stash[6 * blocks + block, some, :] = dz.astype(low)

        by_rows(back_in)

    def attention_backward(u):
        span = slice(u * unit, (u + 1) * unit)
        keys = (u + 1) * unit
        lhs[1, :, span] = stash_read(6).T
        d_context = dot(stash_read(6), weight(3)).astype(low)
        stash_write(6, d_context)
        product = (d_context.astype(f32) * rhs[3, span, :].astype(f32)).astype(low)
        head = lax.broadcasted_iota(jnp.int32, (HEADS, width), 0)
        column = lax.broadcasted_iota(jnp.int32, (HEADS, width), 1)
        inside = (column >= head * HEAD) & (column < (head + 1) * HEAD)
        delta_t[...] = dot_cols(jnp.where(inside, 1.0, 0.0).astype(low), product)
        mask[:keys, :] = mask_of((keys, unit), 1, u * unit, 0)

        def pair(p, carry):
            lanes = pair_lanes(p)
            query = projected(0, lanes, u).astype(f32)
            key = projected(1, lanes, 0, u + 1)
            value = projected(2, lanes, 0, u + 1)
            d_out = stash[pl.ds(6 * blocks, blocks), :, lanes].reshape(unit, LANES).astype(f32)
            key_t = key.T
            d_key = d_value = None
            d_query = []
            for h in range(2):
                query_h = (query * half_lanes(h, score_scale)).astype(low)
                d_out_h = (d_out * half_lanes(h, 1.0)).astype(low)
                scores = dot_cols(key, query_h) + mask[:keys, :]
                prob = jnp.exp(scores - log_t[u, pl.ds(2 * p + h, 1), :])
                d_prob = dot_cols(value, d_out_h)
                d_scores = (prob * (d_prob - delta_t[pl.ds(2 * p + h, 1), :])).astype(low)
                term_v = dot(prob.astype(low), d_out_h)
                term_k = dot(d_scores, query_h)
                d_value = term_v if h == 0 else d_value + term_v
                d_key = term_k if h == 0 else d_key + term_k
                d_query.append(dot(key_t[h * HEAD : (h + 1) * HEAD, :], d_scores))
            d_query = jnp.concatenate(d_query, axis=0) * score_scale
            rhs[0, span, lanes] = d_query.T.astype(low)
            for i, grad in ((0, d_key), (1, d_value)):
                carried = pl.ds(i * blocks, blocks)
                if u == 1:
                    rhs[1 + i, span, lanes] = grad[unit:].astype(low)
                    total[carried, :, lanes] = grad[:unit].reshape(blocks, rows, LANES)
                else:
                    grad = grad + total[carried, :, lanes].reshape(unit, LANES)
                    rhs[1 + i, span, lanes] = grad.astype(low)
            return carry

        lax.fori_loop(0, PAIRS, pair, 0, unroll=2)
        for part in range(3):
            add_branch(dot_cols(rhs[part, span, :], weight(part)), part == 0)

        def back_in(block, some, across):
            normal, spread = whiten(stash[u * blocks + block, some, :].astype(f32))
            d_normed = total[2 * blocks + block, some, :]
            add_sums(0, 0, d_normed, normal)
            d_ln = whiten_back(d_normed * gain(0, 0), normal, spread)
            d_input = grads[1, u, block, some, :].astype(f32) + d_ln
            grads[0, u, block, some, :] = d_input.astype(low)

        by_rows(back_in)

    for u in range(2):

        @pl.when(early)
        def _():
            token_copy(u).wait()

        @pl.when(late)
        def _():
            hop_copy(u).wait_recv()

        attention_forward(u)
        feed_forward(u)

        @pl.when(early)
        def _():
            hop_copy(u).start()

        for copy in out_copies(0, u):
            copy.start()

    for u in (1, 0):

        @pl.when(late)
        def _():
            cotangent_copy(u).wait()

        @pl.when(early)
        def _():
            hop_copy(2 + u).wait_recv()

        feed_backward(u)
        attention_backward(u)

        @pl.when(late)
        def _():
            hop_copy(2 + u).start()

        for copy in out_copies(1, u):
            copy.start()

    for k in range(8):
        (weight_remote(k) if k < 6 else affine_remote(k - 6)).wait_send()
    for ring_end in (left, right):
        pl.semaphore_signal(ready, inc=1, device_id=(ring_end, section), device_id_type=MESH)
    pl.semaphore_signal(ready, inc=1, device_id=(dp, peer), device_id_type=MESH)

    slice_width = width // count
    for j in range(count):
        piece = sums[:, :, j * slice_width : (j + 1) * slice_width]
        small[j, :, :slice_width] = jnp.sum(piece, axis=1)

    @pl.when(late)
    def _():
        for u in range(2):
            hop_copy(2 + u).wait_send()

    def pair_copy(step):
        return to_peer(
            stash.at[pl.ds(6 * lax.rem(step, 2), 6)],
            pool.at[pl.ds(6 * step, 6)],
            pair_ss.at[lax.rem(step, 2)],
            pair_rs.at[step],
        )

    def ring_block(step, stream):
        return 6 * count + 6 * step + stream

    def ring_copy(step, stream):
        return pltpu.make_async_remote_copy(
            src_ref=sends.at[6 * lax.rem(step, 2) + stream],
            dst_ref=pool.at[ring_block(step, stream)],
            send_sem=ring_ss.at[lax.rem(step, 2), stream],
            recv_sem=ring_rs.at[step, stream],
            device_id=(right if stream < 3 else left, section),
            device_id_type=MESH,
        )

    def product(step, stream, part):
        if stream < 3:
            block = lax.rem(place + 2 * count - 1 - step, count)
        else:
            block = lax.rem(place + 1 + step, count)
        block = ring_index(block, count)
        if stream % 3 < 2:
            group = stream % 3 + 2 * (stream // 3)
            side = jnp.where(part == 1, 2, 1 if group == 3 else 0)
            piece = lhs[side, pl.ds(pl.multiple_of(block * rows, rows), rows), :]
            return dot(piece, rhs[part * 4 + group])
        start = part * (2 * width) + block * (2 * rows) + (stream // 3) * rows
        return dot(hidden_t[pl.ds(pl.multiple_of(start, rows), rows), :], dz_down[...])

    def pair_part(step):
        slot = lax.rem(step, 2)
        for stream in range(6):
            stash[6 * slot + stream] = product(step, stream, 1 - core).astype(low)

    def own_part(step):
        for stream in range(6):
            total[stream] = product(step, stream, core)

    gb_pair = to_peer(small, small_pair, small_sems.at[0], small_sems.at[1])

    def gb_copy(step):
        other = lax.rem(dp + step, count)
        return pltpu.make_async_remote_copy(
            src_ref=small_sum.at[other],
            dst_ref=small_recv.at[step],
            send_sem=small_ss.at[step],
            recv_sem=small_rs.at[step],
            device_id=(other, section),
            device_id_type=MESH,
        )

    pair_part(0)
    pl.semaphore_wait(ready, 3)
    pair_copy(0).start()
    gb_pair.start()
    own_part(0)
    gb_pair.wait()
    small_sum[...] = small[...] + small_pair[...]

    def gb_start(step, carry):
        gb_copy(step).start()
        return carry

    lax.fori_loop(1, count, gb_start, 0)

    def ring_step(step, carry):
        pair_copy(step).wait_recv()
        for stream in (0, 3, 1, 4, 2, 5):
            total[stream] += pool[6 * step + stream].astype(f32)

            @pl.when(step >= 1)
            def _():
                ring_copy(step - 1, stream).wait_recv()
                total[stream] += pool[ring_block(step - 1, stream)].astype(f32)

            @pl.when(step >= 2)
            def _():
                ring_copy(step - 2, stream).wait_send()

            sends[6 * lax.rem(step, 2) + stream] = total[stream].astype(low)
            ring_copy(step, stream).start()

        @pl.when(step >= 1)
        def _():
            pair_copy(step - 1).wait_send()

        pair_part(step + 1)
        pair_copy(step + 1).start()
        own_part(step + 1)
        return carry

    lax.fori_loop(0, count - 1, ring_step, 0)

    def grad_copy(stream):
        if stream % 3 < 2:
            group = stream % 3 + 2 * (stream // 3)
            target = first_grad.at[:, pl.ds(group * width, width)]
        else:
            target = down_grad.at[pl.ds((stream // 3) * rows, rows)]
        return pltpu.make_async_copy(total.at[stream], target, grad_ls.at[stream])

    last = count - 1
    pair_copy(last).wait_recv()
    for stream in (0, 3, 1, 4, 2, 5):
        total[stream] += pool[6 * last + stream].astype(f32)
        ring_copy(last - 1, stream).wait_recv()
        total[stream] += pool[ring_block(last - 1, stream)].astype(f32)
        grad_copy(stream).start()

    small_out[...] = small_sum[dp]

    def gb_finish(step, carry):
        gb_copy(step).wait()
        small_out[...] += small_recv[step]
        return carry

    lax.fori_loop(1, count, gb_finish, 0)
    for stream in range(6):
        ring_copy(last - 1, stream).wait_send()
        ring_copy(last - 2, stream).wait_send()
        grad_copy(stream).wait()
    pair_copy(last).wait_send()
    pair_copy(last - 1).wait_send()
    for kind in range(2):
        for u in range(2):
            local_copy, remote_copy = out_copies(kind, u)
            local_copy.wait()
            remote_copy.wait()

    @pl.when(early)
    def _():
        for u in range(2):
            hop_copy(u).wait_send()


def layers(tokens, cotangent, lengths, first, down, gains, biases):
    count = lax.axis_size("dp")
    token_count, width = tokens.shape
    row_len = token_count // lengths.shape[0]
    unit = row_len // 2
    rows = width // count
    blocks = unit // rows
    vmem = pl.BlockSpec(memory_space=pltpu.VMEM)
    anywhere = pl.BlockSpec(memory_space=pl.ANY)
    sem = pltpu.SemaphoreType.DMA
    shape = jax.ShapeDtypeStruct
    buffer = pltpu.VMEM
    cut = (token_count // rows, rows, width)
    small = (count, 8, max(128, width // count))
    outs = pl.pallas_call(
        functools.partial(layers_kernel, count),
        out_shape=(
            shape(cut, low),
            shape(cut, low),
            shape((rows, 4 * width), f32),
            shape((2 * rows, width), f32),
            shape(small[1:], f32),
        ),
        in_specs=[anywhere, anywhere, pl.BlockSpec(memory_space=pltpu.SMEM)] + [anywhere] * 4,
        out_specs=(anywhere, anywhere, anywhere, anywhere, vmem),
        scratch_shapes=[
            buffer((12 * count, rows, width), low),
            buffer((6 * blocks, rows, width), low),
            buffer((7 * blocks, rows, width), low),
            buffer((2, blocks, rows, width), low),
            buffer((row_len, 128), f32),
            buffer((2, 2, blocks, rows, width), low),
            buffer((2, 2, blocks, rows, width), low),
            buffer((row_len, unit), f32),
            buffer((max(6, 3 * blocks), rows, width), f32),
            buffer((3, width, row_len), low),
            buffer((4 * width, row_len), low),
            buffer((8, row_len, width), low),
            buffer((row_len, width), low),
            buffer((2, 2, 2, width), f32),
            buffer((2, HEADS, unit), f32),
            buffer((unit, LANES), f32),
            buffer((HEADS, unit), f32),
            buffer((8, 8, width), f32),
            buffer(small, f32),
            buffer(small, f32),
            buffer(small, f32),
            buffer(small, f32),
            sem((8,)),
            sem((8,)),
            sem((8,)),
            sem((4,)),
            sem((4,)),
            sem((4,)),
            sem((4,)),
            sem((4,)),
            sem((4,)),
            pltpu.SemaphoreType.REGULAR,
            sem((2,)),
            sem((count,)),
            sem((2, 6)),
            sem((count - 1, 6)),
            sem((2,)),
            sem((count,)),
            sem((count,)),
            sem((6,)),
        ],
        compiler_params=pltpu.CompilerParams(
            collective_id=0, has_side_effects=True, vmem_limit_bytes=63 * 1024 * 1024
        ),
        name="layers",
    )(
        tokens.reshape(cut),
        cotangent.reshape(cut),
        lengths,
        first.reshape(count, rows, 4 * width),
        down.reshape(2 * count, rows, width),
        gains,
        biases,
    )
    return outs


def local(tokens, doc_lengths, first_weights, down_weights, norm_gains, norm_biases, cotangent):
    width = tokens.shape[1]
    outputs, input_grads, first_part, down_part, small = layers(
        tokens,
        cotangent,
        doc_lengths,
        first_weights[0],
        down_weights[0],
        norm_gains,
        norm_biases,
    )
    slice_width = width // lax.axis_size("dp")
    for_feed = lax.axis_index("section") % 2 == 1
    small = jnp.where(for_feed, small[4:], small[:4])
    return (
        outputs.reshape((1,) + tokens.shape),
        input_grads.reshape((1,) + tokens.shape),
        first_part[None],
        down_part[None],
        small[None, 0:2, :slice_width],
        small[None, 2:4, :slice_width],
    )


def solution(mesh):
    placed = (
        P("dp", None),
        P("dp", None),
        P("section", None, None),
        P("section", None, None),
        P("section", None, None),
        P("section", None, None),
        P("dp", None),
    )
    return jax.shard_map(
        local,
        mesh=mesh,
        in_specs=placed,
        out_specs=(
            P("section", "dp", None),
            P("section", "dp", None),
            P("section", "dp", None),
            P("section", "dp", None),
            P("section", None, "dp"),
            P("section", None, "dp"),
        ),
        check_vma=False,
    )
```

```python
import functools

import jax
import jax.numpy as jnp
from jax import lax
from jax.experimental import pallas as pl
from jax.experimental.pallas import tpu as pltpu
from jax.sharding import PartitionSpec as P

HEADS = 16
HEAD = 64
PAIRS = HEADS // 2
LANES = 2 * HEAD
eps = 1e-05
masked_value = -1e30
score_scale = HEAD ** (-0.5)
MESH = pl.DeviceIdType.MESH
low = jnp.bfloat16
f32 = jnp.float32
tanh_linear = (2.0 / 3.141592653589793) ** 0.5
tanh_cubic = tanh_linear * 0.044715


def ring_place(index, count):
    return jnp.where(index % 2 == 0, index // 2, count - 1 - index // 2)


def ring_index(place, count):
    return jnp.where(place < count // 2, 2 * place, 2 * (count - 1 - place) + 1)


def dot(left, right):
    return jnp.dot(left, right, preferred_element_type=f32)


def dot_cols(left, right):
    return lax.dot_general(left, right, (((1,), (1,)), ((), ())), preferred_element_type=f32)


def whiten(values):
    average = jnp.mean(values, axis=-1, keepdims=True)
    centered = values - average
    variance = jnp.mean(centered * centered, axis=-1, keepdims=True)
    spread = lax.rsqrt(variance + eps)
    return centered * spread, spread


def whiten_back(grad, normal, spread):
    first = jnp.mean(grad, axis=-1, keepdims=True)
    second = jnp.mean(grad * normal, axis=-1, keepdims=True)
    return spread * (grad - first - normal * second)


def gelu_both(u):
    square = u * u
    half = 0.5 + 0.5 * jnp.tanh(u * (tanh_linear + tanh_cubic * square))
    value = u * half
    slope = half + value * (1.0 - half) * (2.0 * tanh_linear + 6.0 * tanh_cubic * square)
    return value, slope


def layers_kernel(
    count,
    tokens,
    cotangent,
    lengths,
    first,
    down,
    gains,
    biases,
    outputs,
    input_grads,
    first_grad,
    down_grad,
    small_out,
    pool,
    sends,
    stash,
    spreads,
    kept,
    mask,
    total,
    lhs,
    hidden_t,
    rhs,
    dz_down,
    affine,
    log_t,
    log_rows,
    delta_t,
    sums,
    small,
    small_pair,
    small_sum,
    small_recv,
    weight_ls,
    weight_ss,
    weight_rs,
    row_ls,
    hop_ss,
    hop_rs,
    out_ls,
    out_ss,
    out_rs,
    ready,
    pair_ready,
    first_ss,
    first_rs,
    pair_ss,
    pair_rs,
    ring_ss,
    ring_rs,
    small_sems,
    small_ss,
    small_rs,
    grad_ls,
):
    rows, width = pool.shape[1:]
    row_len = rhs.shape[1]
    unit = row_len // 2
    blocks = unit // rows
    dp = lax.axis_index("dp")
    section = lax.axis_index("section")
    section_count = lax.axis_size("section")
    core = lax.rem(section, 2)
    peer = section + 1 - 2 * core
    early = section < 2
    late = section >= 2
    partner = lax.rem(section + 2, section_count)
    place = ring_place(dp, count)
    left = ring_index(lax.rem(place + count - 1, count), count)
    right = ring_index(lax.rem(place + 1, count), count)

    barrier = pltpu.get_barrier_semaphore()

    def greet(step, carry):
        other = lax.rem(dp + step, count)
        pl.semaphore_signal(barrier, inc=1, device_id=(other, section), device_id_type=MESH)
        return carry

    lax.fori_loop(1, count, greet, 0)
    for other in (peer, partner):
        pl.semaphore_signal(barrier, inc=1, device_id=(dp, other), device_id_type=MESH)

    def own_chunk(k):
        if k < 4:
            return first.at[:, :, pl.ds(k * width, width)], 4 * core + k
        return down.at[pl.ds((k - 4) * count, count)], 8 + 2 * core + k - 4

    def weight_local(k):
        source, chunk = own_chunk(k)
        target = pool.at[pl.ds(chunk * count, count)]
        return pltpu.make_async_copy(source, target, weight_ls.at[k])

    def to_peer(source, target, send_sem, recv_sem):
        return pltpu.make_async_remote_copy(
            src_ref=source,
            dst_ref=target,
            send_sem=send_sem,
            recv_sem=recv_sem,
            device_id=(dp, peer),
            device_id_type=MESH,
        )

    def weight_remote(k):
        source, chunk = own_chunk(k)
        target = pool.at[pl.ds(chunk * count, count)]
        return to_peer(source, target, weight_ss.at[k], weight_rs.at[k])

    def affine_local(i):
        source = (gains, biases)[i].at[0]
        return pltpu.make_async_copy(source, affine.at[core, i], weight_ls.at[6 + i])

    def affine_remote(i):
        source = (gains, biases)[i].at[0]
        return to_peer(source, affine.at[core, i], weight_ss.at[6 + i], weight_rs.at[6 + i])

    def await_chunk(chunk):
        owner = 1 if 4 <= chunk < 8 or chunk >= 10 else 0
        k = chunk % 4 if chunk < 8 else 4 + chunk % 2

        @pl.when(core == owner)
        def _():
            weight_local(k).wait()

        @pl.when(core != owner)
        def _():
            weight_remote(k).wait_recv()

    def await_feed(i):
        @pl.when(core == 0)
        def _():
            weight_remote(i).wait_recv()

        @pl.when(core == 1)
        def _():
            weight_local((i + 2) % 4).wait()

        if i < 2:
            weight_local(4 + i).wait()
        else:
            weight_remote(2 + i).wait_recv()

    def weight(chunk):
        return pool[pl.ds(chunk * count, count)].reshape(width, width)

    def weight_cols(chunk, some):
        return pool[pl.ds(chunk * count, count), :, some].reshape(width, width // 2)

    def weight_rows(chunk, half):
        start = chunk * count + half * (count // 2)
        return pool[pl.ds(start, count // 2)].reshape(width // 2, width)

    def stash_at(place_in):
        return stash.at[pl.ds(place_in * blocks, blocks)]

    def stash_read(place_in):
        return stash[pl.ds(place_in * blocks, blocks)].reshape(unit, width)

    def stash_write(place_in, value):
        stash[pl.ds(place_in * blocks, blocks)] = value.astype(low).reshape(blocks, rows, width)

    def row_copy(u, source, target, sem):
        start = (core * 2 + u) * blocks
        return pltpu.make_async_copy(source.at[pl.ds(start, blocks)], target, sem)

    def token_copy(u):
        return row_copy(u, tokens, stash_at(u), row_ls.at[u])

    def cotangent_copy(u):
        return row_copy(u, cotangent, sends.at[pl.ds((6 + u) * blocks, blocks)], row_ls.at[2 + u])

    def hop_copy(k, part):
        u = k % 2
        some = pl.ds(part * (blocks // 2), blocks // 2)
        arriving = pl.ds(u * blocks + part * (blocks // 2), blocks // 2)
        grad_arriving = pl.ds((6 + u) * blocks + part * (blocks // 2), blocks // 2)
        return pltpu.make_async_remote_copy(
            src_ref=kept.at[1, u, some],
            dst_ref=stash.at[arriving] if k < 2 else sends.at[grad_arriving],
            send_sem=hop_ss.at[k, part],
            recv_sem=hop_rs.at[k, part],
            device_id=(dp, partner),
            device_id_type=MESH,
        )

    def out_copies(kind, u):
        target = (outputs, input_grads)[kind]
        place_out = target.at[pl.ds((core * 2 + u) * blocks, blocks)]
        k = 2 * kind + u
        own, other = (core, 1 - core) if kind == 0 else (1 - core, core)
        return (
            pltpu.make_async_copy(kept.at[own, u], place_out, out_ls.at[k]),
            to_peer(kept.at[other, u], place_out, out_ss.at[k], out_rs.at[k]),
        )

    def outputs_sent(u):
        local_copy, remote_copy = out_copies(0, u)
        local_copy.wait()
        remote_copy.wait_send()

        @pl.when(early)
        def _():
            for part in range(2):
                hop_copy(u, part).wait_send()

    for k in range(6):
        weight_local(k).start()
    for i in range(2):
        affine_local(i).start()

    @pl.when(early)
    def _():
        for u in range(2):
            token_copy(u).start()

    @pl.when(late)
    def _():
        for u in range(2):
            cotangent_copy(u).start()

    pl.semaphore_wait(barrier, count + 1)
    for i in range(2):
        affine_remote(i).start()
    for k in range(6):
        weight_remote(k).start()

    sums[...] = jnp.zeros_like(sums)
    log_rows[...] = jnp.zeros_like(log_rows)
    small[...] = jnp.zeros_like(small)
    for i in range(2):
        affine_local(i).wait()
        affine_remote(i).wait_recv()

    def gain(sub, which):
        return affine[sub, 0, which : which + 1, :]

    def bias(sub, which):
        return affine[sub, 1, which : which + 1, :]

    ends = [lengths[core, 0]]
    for j in range(1, lengths.shape[1]):
        ends.append(ends[-1] + lengths[core, j])

    def mask_of(shape, query_axis, first_query, first_key):
        query = lax.broadcasted_iota(jnp.int32, shape, query_axis) + first_query
        key = lax.broadcasted_iota(jnp.int32, shape, 1 - query_axis) + first_key
        apart = jnp.zeros(shape, jnp.int32)
        for end in ends:
            apart += (query >= end).astype(jnp.int32) - (key >= end).astype(jnp.int32)
        return jnp.where((apart == 0) & (key <= query), 0.0, masked_value)

    def projected(part, lanes, u=0, halves=1):
        span = pl.ds((2 * part + u) * blocks, halves * blocks)
        return sends[span, :, lanes].reshape(halves * unit, LANES)

    def half_lanes(h, scale):
        lane = lax.broadcasted_iota(jnp.int32, (1, LANES), 1)
        return jnp.where((lane >= h * HEAD) & (lane < (h + 1) * HEAD), scale, 0.0)

    def pair_lanes(p):
        return pl.ds(pl.multiple_of(p * LANES, LANES), LANES)

    def branch():
        return total[pl.ds(2 * blocks, blocks)].reshape(unit, width)

    def add_branch(term, begin):
        value = term if begin else branch() + term
        total[pl.ds(2 * blocks, blocks)] = value.reshape(blocks, rows, width)

    size = min(rows, 64)
    groups = rows // size

    def by_rows(body, part=None):
        def step(i, carry):
            block, start = i // groups, pl.multiple_of(lax.rem(i, groups) * size, size)
            body(block, pl.ds(start, size), pl.ds(pl.multiple_of(i * size, size), size))
            return carry

        half = unit // size // 2
        begin, end = (0, 2 * half) if part is None else (part * half, (part + 1) * half)
        lax.fori_loop(begin, end, step, 0, unroll=True)

    def add_sums(sub, which, grad, normal):
        row = 4 * sub + which
        sums[row] += jnp.sum((grad * normal).reshape(size // 8, 8, width), axis=0)
        sums[row + 2] += jnp.sum(grad.reshape(size // 8, 8, width), axis=0)

    def normed_input(sub, values):
        return (whiten(values)[0] * gain(sub, 0) + bias(sub, 0)).astype(low)

    def await_input(u, half):
        @pl.when(late)
        def _():
            hop_copy(u, half).wait_recv()

        if half == 0:

            @pl.when(early)
            def _():
                token_copy(u).wait()

    def await_grad(u, half):
        @pl.when(early)
        def _():
            hop_copy(2 + u, half).wait_recv()

        if half == 0:

            @pl.when(late)
            def _():
                cotangent_copy(u).wait()

    def send_part(stage, k, part):
        @pl.when(stage)
        def _():
            hop_copy(k, part).start()

    def attention_forward(u):
        span = slice(u * unit, (u + 1) * unit)

        def norm_in(block, some, _):
            values = stash[u * blocks + block, some, :].astype(f32)
            stash[4 * blocks + block, some, :] = normed_input(0, values)

        for half in range(2):
            await_input(u, half)
            by_rows(norm_in, half)
            if u == 0:
                part_blocks = blocks // 2
                normed = stash[pl.ds(4 * blocks + half * part_blocks, part_blocks)]
                for part in range(3):
                    if half == 0:
                        await_chunk(part)
                    value = dot(normed.reshape(unit // 2, width), weight(part)).astype(low)
                    target = pl.ds(2 * part * blocks + half * part_blocks, part_blocks)
                    sends[target] = value.reshape(part_blocks, rows, width)
        for part in range(3) if u == 1 else ():
            value = dot(stash_read(4), weight(part)).astype(low)
            sends[pl.ds((2 * part + u) * blocks, blocks)] = value.reshape(blocks, rows, width)
        lhs[0, :, span] = stash_read(4).T
        for i in range(u + 1):
            mask[i * unit : (i + 1) * unit, :] = mask_of((unit, unit), 0, u * unit, i * unit)
        lane = lax.broadcasted_iota(jnp.int32, (unit, LANES), 1)

        def pair(p, carry):
            lanes = pair_lanes(p)
            query = projected(0, lanes, u).astype(f32)
            key = projected(1, lanes, 0, u + 1)
            value = projected(2, lanes, 0, u + 1)
            added = jnp.concatenate([mask[i * unit : (i + 1) * unit, :] for i in range(u + 1)], 1)
            context = None
            for h in range(2):
                scores = dot_cols((query * half_lanes(h, score_scale)).astype(low), key)
                scores = scores + added
                top = jnp.max(scores, axis=-1, keepdims=True)
                exponent = jnp.exp(scores - top)
                summed = jnp.sum(exponent, axis=-1, keepdims=True)
                part = dot(exponent.astype(low), value) * (1.0 / summed)
                context = part if h == 0 else jnp.where(lane < HEAD, context, part)
                log_total = top + jnp.log(summed)
                log_rows[...] = jnp.where(lane == 2 * p + h, log_total, log_rows[...])
            rhs[3, span, lanes] = context.astype(low)
            return carry

        lax.fori_loop(0, PAIRS, pair, 0, unroll=2)
        log_t[u] = log_rows[...].T[:HEADS]
        if u == 0:
            await_chunk(3)
        add_branch(dot_cols(rhs[3, span, :], weight(3)), True)

        def norm_out(block, some, across):
            normal, spread = whiten(total[2 * blocks + block, some, :])
            stash[(2 + u) * blocks + block, some, :] = normal.astype(low)
            spreads[pl.ds(u * unit + across.start, size), 0:1] = spread
            middle = stash[u * blocks + block, some, :].astype(f32)
            middle = (middle + (normal * gain(0, 1) + bias(0, 1))).astype(low)
            kept[0, u, block, some, :] = middle
            stash[4 * blocks + block, some, :] = normed_input(1, middle.astype(f32))

        by_rows(norm_out)

    def feed_forward(u):
        span = slice(u * unit, (u + 1) * unit)
        lhs[2, :, span] = stash_read(4).T
        for i in range(4):
            c = lax.rem(2 * core + i, 4) if u == 0 else i
            if u == 0:
                await_feed(i)
            hidden, slope = gelu_both(dot(stash_read(4), weight(4 + c)))
            hidden = hidden.astype(low)
            rhs[4 + c, span, :] = slope.astype(low)
            hidden_t[pl.ds(pl.multiple_of(c * width, width), width), span] = hidden.T
            add_branch(dot(hidden, weight(8 + c)), i == 0)

        def norm_out(block, some, across):
            normal, spread = whiten(total[2 * blocks + block, some, :])
            stash[(5 + u) * blocks + block, some, :] = normal.astype(low)
            spreads[pl.ds(u * unit + across.start, size), 1:2] = spread
            middle = kept[0, u, block, some, :].astype(f32)
            output = middle + (normal * gain(1, 1) + bias(1, 1))
            kept[1, u, block, some, :] = output.astype(low)

        for half in range(2):
            by_rows(norm_out, half)
            send_part(early, u, half)

    def feed_backward(u):
        span = slice(u * unit, (u + 1) * unit)

        def back_out(block, some, across):
            own = pl.ds(u * unit + across.start, size)
            upstream = sends[(6 + u) * blocks + block, some, :].astype(f32)
            normal = stash[(5 + u) * blocks + block, some, :].astype(f32)
            add_sums(1, 1, upstream, normal)
            dz = whiten_back(upstream * gain(1, 1), normal, spreads[own, 1:2])
            dz_down[own, :] = dz.astype(low)

        for half in range(2):
            await_grad(u, half)
            by_rows(back_out, half)
        for c in range(4):
            d_hidden = dot_cols(dz_down[span, :], weight(8 + c))
            d_pre = (d_hidden * rhs[4 + c, span, :].astype(f32)).astype(low)
            rhs[4 + c, span, :] = d_pre
            add_branch(dot_cols(d_pre, weight(4 + c)), c == 0)

        def back_in(block, some, across):
            own = pl.ds(u * unit + across.start, size)
            normal, spread = whiten(kept[0, u, block, some, :].astype(f32))
            d_normed = total[2 * blocks + block, some, :]
            add_sums(1, 0, d_normed, normal)
            d_ln = whiten_back(d_normed * gain(1, 0), normal, spread)
            d_middle = (sends[(6 + u) * blocks + block, some, :].astype(f32) + d_ln).astype(low)
            kept[0, u, block, some, :] = d_middle
            upstream = d_middle.astype(f32)
            normal = stash[(2 + u) * blocks + block, some, :].astype(f32)
            add_sums(0, 1, upstream, normal)
            dz = whiten_back(upstream * gain(0, 1), normal, spreads[own, 0:1])
            stash[4 * blocks + block, some, :] = dz.astype(low)

        outputs_sent(u)
        by_rows(back_in)

    def attention_backward(u):
        span = slice(u * unit, (u + 1) * unit)
        keys = (u + 1) * unit
        lhs[1, :, span] = stash_read(4).T
        d_context = dot(stash_read(4), weight(3)).astype(low)
        stash_write(4, d_context)
        product = (d_context.astype(f32) * rhs[3, span, :].astype(f32)).astype(low)
        head = lax.broadcasted_iota(jnp.int32, (HEADS, width), 0)
        column = lax.broadcasted_iota(jnp.int32, (HEADS, width), 1)
        inside = (column >= head * HEAD) & (column < (head + 1) * HEAD)
        delta_t[...] = dot_cols(jnp.where(inside, 1.0, 0.0).astype(low), product)
        mask[:keys, :] = mask_of((keys, unit), 1, u * unit, 0)

        def pair(p, carry):
            lanes = pair_lanes(p)
            query = projected(0, lanes, u).astype(f32)
            key = projected(1, lanes, 0, u + 1)
            value = projected(2, lanes, 0, u + 1)
            d_out = stash[pl.ds(4 * blocks, blocks), :, lanes].reshape(unit, LANES).astype(f32)
            key_t = key.T
            d_key = d_value = None
            d_query = []
            for h in range(2):
                query_h = (query * half_lanes(h, score_scale)).astype(low)
                d_out_h = (d_out * half_lanes(h, 1.0)).astype(low)
                scores = dot_cols(key, query_h) + mask[:keys, :]
                prob = jnp.exp(scores - log_t[u, pl.ds(2 * p + h, 1), :])
                d_prob = dot_cols(value, d_out_h)
                d_scores = (prob * (d_prob - delta_t[pl.ds(2 * p + h, 1), :])).astype(low)
                term_v = dot(prob.astype(low), d_out_h)
                term_k = dot(d_scores, query_h)
                d_value = term_v if h == 0 else d_value + term_v
                d_key = term_k if h == 0 else d_key + term_k
                d_query.append(dot(key_t[h * HEAD : (h + 1) * HEAD, :], d_scores))
            d_query = jnp.concatenate(d_query, axis=0) * score_scale
            rhs[0, span, lanes] = d_query.T.astype(low)
            for i, grad in ((0, d_key), (1, d_value)):
                carried = pl.ds(i * blocks, blocks)
                if u == 1:
                    rhs[1 + i, span, lanes] = grad[unit:].astype(low)
                    total[carried, :, lanes] = grad[:unit].reshape(blocks, rows, LANES)
                else:
                    grad = grad + total[carried, :, lanes].reshape(unit, LANES)
                    rhs[1 + i, span, lanes] = grad.astype(low)
            return carry

        lax.fori_loop(0, PAIRS, pair, 0, unroll=2)
        for part in range(3):
            add_branch(dot_cols(rhs[part, span, :], weight(part)), part == 0)

        def back_in(block, some, across):
            normal, spread = whiten(stash[u * blocks + block, some, :].astype(f32))
            d_normed = total[2 * blocks + block, some, :]
            add_sums(0, 0, d_normed, normal)
            d_ln = whiten_back(d_normed * gain(0, 0), normal, spread)
            d_input = kept[0, u, block, some, :].astype(f32) + d_ln
            kept[1, u, block, some, :] = d_input.astype(low)

        for half in range(2):
            by_rows(back_in, half)
            send_part(late, 2 + u, half)

    def pair_block(step, stream=0):
        return jnp.where(step == 0, 6 * count, 6 * (step - 1)) + stream

    def ring_block(step, stream):
        return 12 * count - 6 * (step + 1) + stream

    def pair_slot(step):
        return jnp.where(lax.rem(step, 2) == 0, 5 * blocks, 0)

    def ring_slot(step):
        return jnp.where(lax.rem(step, 2) == 0, 6 * blocks, 0)

    def pair_copy(step):
        return to_peer(
            stash.at[pl.ds(pair_slot(step), 6)],
            pool.at[pl.ds(pair_block(step), 6)],
            pair_ss.at[lax.rem(step, 2)],
            pair_rs.at[step],
        )

    def pair_first(stream):
        return to_peer(
            stash.at[5 * blocks + stream],
            pool.at[6 * count + stream],
            first_ss.at[stream],
            first_rs.at[stream],
        )

    def ring_copy(step, stream):
        return pltpu.make_async_remote_copy(
            src_ref=sends.at[ring_slot(step) + stream],
            dst_ref=pool.at[ring_block(step, stream)],
            send_sem=ring_ss.at[lax.rem(step, 2), stream],
            recv_sem=ring_rs.at[step, stream],
            device_id=(jnp.where(stream < 3, right, left), section),
            device_id_type=MESH,
        )

    def ring_row(step, stream):
        behind = lax.rem(place + 2 * count - 1 - step, count)
        ahead = lax.rem(place + 1 + step, count)
        return ring_index(jnp.where(stream < 3, behind, ahead), count)

    def stream_of(group):
        return group + group // 2

    def product(step, group, part):
        block = ring_row(step, stream_of(group))
        side = jnp.where(part == 1, 2, jnp.where(group == 3, 1, 0))
        piece = lhs[side, pl.ds(pl.multiple_of(block * rows, rows), rows), :]
        return dot(piece, rhs[part * 4 + group])

    def down_product(step, turn, part):
        block = ring_row(step, 2 + 3 * turn)
        start = part * (2 * width) + block * (2 * rows) + turn * rows
        return dot(hidden_t[pl.ds(pl.multiple_of(start, rows), rows), :], dz_down[...])

    def each(count_of, action):
        def step(i, carry):
            action(i)
            return carry

        lax.fori_loop(0, count_of, step, 0)

    def pair_part(step):
        slot = pair_slot(step)

        def group_part(group):
            value = product(step, group, 1 - core)
            stash[slot + stream_of(group)] = value.astype(low)

        def down_part(turn):
            stash[slot + 2 + 3 * turn] = down_product(step, turn, 1 - core).astype(low)

        each(4, group_part)
        each(2, down_part)

    def own_part(step):
        def group_part(group):
            total[stream_of(group)] = product(step, group, core)

        def down_part(turn):
            total[2 + 3 * turn] = down_product(step, turn, core)

        each(4, group_part)
        each(2, down_part)

    def first_pair_group(group):
        stream = stream_of(group)
        stash[5 * blocks + stream] = product(0, group, 1 - core).astype(low)

    def first_pair_down(turn):
        stash[5 * blocks + 2 + 3 * turn] = down_product(0, turn, 1 - core).astype(low)

    def first_own_group(group):
        stream = stream_of(group)
        sends[6 * blocks + stream] = product(0, group, core).astype(low)

    def first_own_down(turn):
        sends[6 * blocks + 2 + 3 * turn] = down_product(0, turn, core).astype(low)

    def first_ring(stream):
        pair_first(stream).wait_recv()
        value = sends[6 * blocks + stream].astype(f32) + pool[6 * count + stream].astype(f32)
        sends[6 * blocks + stream] = value.astype(low)
        ring_copy(0, stream).start()

    def feed_first():
        for other in (left, right):
            pl.semaphore_signal(ready, inc=1, device_id=(other, section), device_id_type=MESH)
        pl.semaphore_signal(ready, inc=1, device_id=(dp, peer), device_id_type=MESH)
        each(2, first_pair_down)

        @pl.when(core == 0)
        def _():
            each(4, first_pair_group)

        pl.semaphore_wait(ready, 3)
        each(2, lambda turn: pair_first(2 + 3 * turn).start())

        @pl.when(core == 0)
        def _():
            each(4, lambda group: pair_first(stream_of(group)).start())

        each(2, first_own_down)

        @pl.when(core == 1)
        def _():
            each(4, first_own_group)

        each(2, lambda turn: first_ring(2 + 3 * turn))

        @pl.when(core == 1)
        def _():
            each(4, lambda group: first_ring(stream_of(group)))

    for u in range(2):
        attention_forward(u)
        feed_forward(u)
        for copy in out_copies(0, u):
            copy.start()

    feed_backward(1)
    attention_backward(1)
    for copy in out_copies(1, 1):
        copy.start()
    feed_backward(0)

    def last_attention(turn):
        pl.when(turn == jnp.where(early, 0, 1))(feed_first)

        @pl.when(turn == 0)
        def _():
            attention_backward(0)

    each(2, last_attention)
    for copy in out_copies(1, 0):
        copy.start()
    for k in range(8):
        (weight_remote(k) if k < 6 else affine_remote(k - 6)).wait_send()
    pl.semaphore_signal(pair_ready, inc=1, device_id=(dp, peer), device_id_type=MESH)

    @pl.when(core == 1)
    def _():
        each(4, first_pair_group)
        each(4, lambda group: pair_first(stream_of(group)).start())

    @pl.when(core == 0)
    def _():
        each(4, first_own_group)
        each(4, lambda group: first_ring(stream_of(group)))

    @pl.when(late)
    def _():
        for k in (2, 3):
            for half in range(2):
                hop_copy(k, half).wait_send()

    pair_part(1)
    pl.semaphore_wait(pair_ready, 1)
    pair_copy(1).start()
    own_part(1)

    slice_width = width // count
    for j in range(count):
        piece = sums[:, :, j * slice_width : (j + 1) * slice_width]
        small[j, :, :slice_width] = jnp.sum(piece, axis=1)

    gb_pair = to_peer(small, small_pair, small_sems.at[0], small_sems.at[1])

    def gb_copy(step):
        other = lax.rem(dp + step, count)
        return pltpu.make_async_remote_copy(
            src_ref=small_sum.at[other],
            dst_ref=small_recv.at[step],
            send_sem=small_ss.at[step],
            recv_sem=small_rs.at[step],
            device_id=(other, section),
            device_id_type=MESH,
        )

    gb_pair.start()
    gb_pair.wait()
    small_sum[...] = small[...] + small_pair[...]

    def gb_start(step, carry):
        gb_copy(step).start()
        return carry

    lax.fori_loop(1, count, gb_start, 0)

    for stream in range(6):
        pair_first(stream).wait_send()

    def ring_step(step, carry):
        pair_copy(step).wait_recv()

        def forward(i):
            turn = i // 2
            stream = 3 * lax.rem(i, 2) + jnp.where(turn == 0, 2, turn - 1)
            ring_copy(step - 1, stream).wait_recv()
            value = total[stream] + pool[pair_block(step, stream)].astype(f32)
            value = value + pool[ring_block(step - 1, stream)].astype(f32)

            @pl.when(step >= 2)
            def _():
                ring_copy(step - 2, stream).wait_send()

            sends[ring_slot(step) + stream] = value.astype(low)
            ring_copy(step, stream).start()

        each(6, forward)

        @pl.when(step >= 2)
        def _():
            pair_copy(step - 1).wait_send()

        pair_part(step + 1)
        pair_copy(step + 1).start()
        own_part(step + 1)
        return carry

    lax.fori_loop(1, count - 1, ring_step, 0)

    def grad_copy(stream):
        if stream % 3 < 2:
            group = stream % 3 + 2 * (stream // 3)
            target = first_grad.at[:, pl.ds(group * width, width)]
        else:
            target = down_grad.at[pl.ds((stream // 3) * rows, rows)]
        return pltpu.make_async_copy(total.at[stream], target, grad_ls.at[stream])

    last = count - 1
    pair_copy(last).wait_recv()
    for stream in (2, 5, 0, 3, 1, 4):
        total[stream] += pool[pair_block(last, stream)].astype(f32)
        ring_copy(last - 1, stream).wait_recv()
        total[stream] += pool[ring_block(last - 1, stream)].astype(f32)
        grad_copy(stream).start()

    small_out[...] = small_sum[dp]

    def gb_finish(step, carry):
        gb_copy(step).wait()
        small_out[...] += small_recv[step]
        return carry

    lax.fori_loop(1, count, gb_finish, 0)
    for stream in range(6):
        ring_copy(last - 1, stream).wait_send()
        ring_copy(last - 2, stream).wait_send()
        grad_copy(stream).wait()
    pair_copy(last).wait_send()
    pair_copy(last - 1).wait_send()
    for u in range(2):
        out_copies(0, u)[1].wait_recv()
        local_copy, remote_copy = out_copies(1, u)
        local_copy.wait()
        remote_copy.wait()


def layers(tokens, cotangent, lengths, first, down, gains, biases):
    count = lax.axis_size("dp")
    token_count, width = tokens.shape
    row_len = token_count // lengths.shape[0]
    unit = row_len // 2
    rows = width // count
    blocks = unit // rows
    vmem = pl.BlockSpec(memory_space=pltpu.VMEM)
    anywhere = pl.BlockSpec(memory_space=pl.ANY)
    sem = pltpu.SemaphoreType.DMA
    shape = jax.ShapeDtypeStruct
    buffer = pltpu.VMEM
    cut = (token_count // rows, rows, width)
    small = (count, 8, max(128, width // count))
    outs = pl.pallas_call(
        functools.partial(layers_kernel, count),
        out_shape=(
            shape(cut, low),
            shape(cut, low),
            shape((rows, 4 * width), f32),
            shape((2 * rows, width), f32),
            shape(small[1:], f32),
        ),
        in_specs=[anywhere, anywhere, pl.BlockSpec(memory_space=pltpu.SMEM)] + [anywhere] * 4,
        out_specs=(anywhere, anywhere, anywhere, anywhere, vmem),
        scratch_shapes=[
            buffer((12 * count, rows, width), low),
            buffer((8 * blocks + max(0, 6 - 2 * blocks), rows, width), low),
            buffer((7 * blocks + max(0, 6 - 2 * blocks), rows, width), low),
            buffer((row_len, 128), f32),
            buffer((2, 2, blocks, rows, width), low),
            buffer((row_len, unit), f32),
            buffer((max(6, 3 * blocks), rows, width), f32),
            buffer((3, width, row_len), low),
            buffer((4 * width, row_len), low),
            buffer((8, row_len, width), low),
            buffer((row_len, width), low),
            buffer((2, 2, 2, width), f32),
            buffer((2, HEADS, unit), f32),
            buffer((unit, LANES), f32),
            buffer((HEADS, unit), f32),
            buffer((8, 8, width), f32),
            buffer(small, f32),
            buffer(small, f32),
            buffer(small, f32),
            buffer(small, f32),
            sem((8,)),
            sem((8,)),
            sem((8,)),
            sem((4,)),
            sem((4, 2)),
            sem((4, 2)),
            sem((4,)),
            sem((4,)),
            sem((4,)),
            pltpu.SemaphoreType.REGULAR,
            pltpu.SemaphoreType.REGULAR,
            sem((6,)),
            sem((6,)),
            sem((2,)),
            sem((count,)),
            sem((2, 6)),
            sem((count - 1, 6)),
            sem((2,)),
            sem((count,)),
            sem((count,)),
            sem((6,)),
        ],
        compiler_params=pltpu.CompilerParams(
            collective_id=0, has_side_effects=True, vmem_limit_bytes=63 * 1024 * 1024
        ),
        name="layers",
    )(
        tokens.reshape(cut),
        cotangent.reshape(cut),
        lengths,
        first.reshape(count, rows, 4 * width),
        down.reshape(2 * count, rows, width),
        gains,
        biases,
    )
    return outs


def place_kernel(*refs):
    sources, small, targets, (gain_grad, bias_grad) = refs[:4], refs[4], refs[5:9], refs[9:11]
    buffers, (arrived, written) = refs[11:15], refs[15:]
    reads, writes = [], []
    for j in range(4):
        for i, (source, target, buffer) in enumerate(zip(sources, targets, buffers)):
            size = max(16, source.shape[0] // 4)
            if j * size >= source.shape[0]:
                continue
            some = pl.ds(j * size, size)
            reads.append(
                pltpu.make_async_copy(source.at[some], buffer.at[some], arrived.at[i, j])
            )
            writes.append(
                pltpu.make_async_copy(buffer.at[some], target.at[0, some], written.at[i, j])
            )
    for read in reads:
        read.start()
    feed = lax.axis_index("section") % 2 == 1
    width = gain_grad.shape[2]
    gain_grad[0] = jnp.where(feed, small[4:6, :width], small[0:2, :width])
    bias_grad[0] = jnp.where(feed, small[6:8, :width], small[2:4, :width])
    for read, write in zip(reads, writes):
        read.wait()
        write.start()
    for write in writes:
        write.wait()


def local(tokens, doc_lengths, first_weights, down_weights, norm_gains, norm_biases, cotangent):
    width = tokens.shape[1]
    outputs, input_grads, first_part, down_part, small = layers(
        tokens,
        cotangent,
        doc_lengths,
        first_weights[0],
        down_weights[0],
        norm_gains,
        norm_biases,
    )
    slice_width = width // lax.axis_size("dp")
    results = [outputs.reshape(tokens.shape), input_grads.reshape(tokens.shape)]
    results += [first_part, down_part]
    norm_part = jax.ShapeDtypeStruct((1, 2, slice_width), f32)
    anywhere = pl.BlockSpec(memory_space=pl.ANY)
    vmem = pl.BlockSpec(memory_space=pltpu.VMEM)
    return pl.pallas_call(
        place_kernel,
        out_shape=[jax.ShapeDtypeStruct((1,) + r.shape, r.dtype) for r in results]
        + [norm_part, norm_part],
        in_specs=[anywhere] * 4 + [vmem],
        out_specs=[anywhere] * 4 + [vmem] * 2,
        scratch_shapes=[pltpu.VMEM(r.shape, r.dtype) for r in results]
        + [pltpu.SemaphoreType.DMA((4, 4))] * 2,
        name="place",
    )(*results, small)


def solution(mesh):
    placed = (
        P("dp", None),
        P("dp", None),
        P("section", None, None),
        P("section", None, None),
        P("section", None, None),
        P("section", None, None),
        P("dp", None),
    )
    return jax.shard_map(
        local,
        mesh=mesh,
        in_specs=placed,
        out_specs=(
            P("section", "dp", None),
            P("section", "dp", None),
            P("section", "dp", None),
            P("section", "dp", None),
            P("section", None, "dp"),
            P("section", None, "dp"),
        ),
        check_vma=False,
    )
```

```python
import functools

import jax
import jax.numpy as jnp
from jax import lax
from jax.experimental import pallas as pl
from jax.experimental.pallas import tpu as pltpu
from jax.sharding import PartitionSpec as P

HEADS = 16
HEAD = 64
PAIRS = HEADS // 2
LANES = 2 * HEAD
eps = 1e-05
masked_value = -1e30
score_scale = HEAD ** (-0.5)
MESH = pl.DeviceIdType.MESH
low = jnp.bfloat16
f32 = jnp.float32
tanh_linear = (2.0 / 3.141592653589793) ** 0.5
tanh_cubic = tanh_linear * 0.044715


def ring_place(index, count):
    return jnp.where(index % 2 == 0, index // 2, count - 1 - index // 2)


def ring_index(place, count):
    return jnp.where(place < count // 2, 2 * place, 2 * (count - 1 - place) + 1)


def dot(left, right):
    return jnp.dot(left, right, preferred_element_type=f32)


def dot_cols(left, right):
    return lax.dot_general(left, right, (((1,), (1,)), ((), ())), preferred_element_type=f32)


def whiten(values):
    average = jnp.mean(values, axis=-1, keepdims=True)
    centered = values - average
    variance = jnp.mean(centered * centered, axis=-1, keepdims=True)
    spread = lax.rsqrt(variance + eps)
    return centered * spread, spread


def whiten_back(grad, normal, spread):
    first = jnp.mean(grad, axis=-1, keepdims=True)
    second = jnp.mean(grad * normal, axis=-1, keepdims=True)
    return spread * (grad - first - normal * second)


def gelu_both(u):
    square = u * u
    half = 0.5 + 0.5 * jnp.tanh(u * (tanh_linear + tanh_cubic * square))
    value = u * half
    slope = half + value * (1.0 - half) * (2.0 * tanh_linear + 6.0 * tanh_cubic * square)
    return value, slope


def layers_kernel(
    count,
    tokens,
    cotangent,
    lengths,
    first,
    down,
    gains,
    biases,
    outputs,
    input_grads,
    first_grad,
    down_grad,
    small_out,
    pool,
    sends,
    stash,
    spreads,
    kept,
    mask,
    total,
    lhs,
    hidden_t,
    rhs,
    dz_down,
    affine,
    log_t,
    log_rows,
    delta_t,
    sums,
    small,
    small_pair,
    small_sum,
    small_recv,
    weight_ls,
    weight_ss,
    weight_rs,
    row_ls,
    hop_ss,
    hop_rs,
    out_ls,
    out_ss,
    out_rs,
    ready,
    pair_ready,
    first_ss,
    first_rs,
    pair_ss,
    pair_rs,
    ring_ss,
    ring_rs,
    small_sems,
    small_ss,
    small_rs,
    grad_ls,
):
    rows, width = pool.shape[1:]
    row_len = rhs.shape[1]
    unit = row_len // 2
    blocks = unit // rows
    dp = lax.axis_index("dp")
    section = lax.axis_index("section")
    section_count = lax.axis_size("section")
    core = lax.rem(section, 2)
    peer = section + 1 - 2 * core
    early = section < 2
    late = section >= 2
    partner = lax.rem(section + 2, section_count)
    place = ring_place(dp, count)
    left = ring_index(lax.rem(place + count - 1, count), count)
    right = ring_index(lax.rem(place + 1, count), count)

    barrier = pltpu.get_barrier_semaphore()

    def greet(step, carry):
        other = lax.rem(dp + step, count)
        pl.semaphore_signal(barrier, inc=1, device_id=(other, section), device_id_type=MESH)
        return carry

    lax.fori_loop(1, count, greet, 0)
    for other in (peer, partner):
        pl.semaphore_signal(barrier, inc=1, device_id=(dp, other), device_id_type=MESH)

    def own_chunk(k):
        if k < 4:
            return first.at[:, :, pl.ds(k * width, width)], 4 * core + k
        return down.at[pl.ds((k - 4) * count, count)], 8 + 2 * core + k - 4

    def weight_local(k):
        source, chunk = own_chunk(k)
        target = pool.at[pl.ds(chunk * count, count)]
        return pltpu.make_async_copy(source, target, weight_ls.at[k])

    def to_peer(source, target, send_sem, recv_sem):
        return pltpu.make_async_remote_copy(
            src_ref=source,
            dst_ref=target,
            send_sem=send_sem,
            recv_sem=recv_sem,
            device_id=(dp, peer),
            device_id_type=MESH,
        )

    def weight_remote(k):
        source, chunk = own_chunk(k)
        target = pool.at[pl.ds(chunk * count, count)]
        return to_peer(source, target, weight_ss.at[k], weight_rs.at[k])

    def affine_local(i):
        source = (gains, biases)[i].at[0]
        return pltpu.make_async_copy(source, affine.at[core, i], weight_ls.at[6 + i])

    def affine_remote(i):
        source = (gains, biases)[i].at[0]
        return to_peer(source, affine.at[core, i], weight_ss.at[6 + i], weight_rs.at[6 + i])

    def await_chunk(chunk):
        owner = 1 if 4 <= chunk < 8 or chunk >= 10 else 0
        k = chunk % 4 if chunk < 8 else 4 + chunk % 2

        @pl.when(core == owner)
        def _():
            weight_local(k).wait()

        @pl.when(core != owner)
        def _():
            weight_remote(k).wait_recv()

    def await_feed(i):
        @pl.when(core == 0)
        def _():
            weight_remote(i).wait_recv()

        @pl.when(core == 1)
        def _():
            weight_local((i + 2) % 4).wait()

        if i < 2:
            weight_local(4 + i).wait()
        else:
            weight_remote(2 + i).wait_recv()

    def weight(chunk):
        return pool[pl.ds(chunk * count, count)].reshape(width, width)

    def weight_cols(chunk, some):
        return pool[pl.ds(chunk * count, count), :, some].reshape(width, width // 2)

    def weight_rows(chunk, half):
        start = chunk * count + half * (count // 2)
        return pool[pl.ds(start, count // 2)].reshape(width // 2, width)

    def stash_at(place_in):
        return stash.at[pl.ds(place_in * blocks, blocks)]

    def stash_read(place_in):
        return stash[pl.ds(place_in * blocks, blocks)].reshape(unit, width)

    def stash_write(place_in, value):
        stash[pl.ds(place_in * blocks, blocks)] = value.astype(low).reshape(blocks, rows, width)

    def row_copy(u, source, target, sem):
        start = (core * 2 + u) * blocks
        return pltpu.make_async_copy(source.at[pl.ds(start, blocks)], target, sem)

    def token_copy(u):
        return row_copy(u, tokens, stash_at(u), row_ls.at[u])

    def cotangent_copy(u):
        return row_copy(u, cotangent, sends.at[pl.ds((6 + u) * blocks, blocks)], row_ls.at[2 + u])

    def hop_copy(k, part):
        u = k % 2
        some = pl.ds(part * (blocks // 2), blocks // 2)
        arriving = pl.ds(u * blocks + part * (blocks // 2), blocks // 2)
        grad_arriving = pl.ds((6 + u) * blocks + part * (blocks // 2), blocks // 2)
        return pltpu.make_async_remote_copy(
            src_ref=kept.at[1, u, some],
            dst_ref=stash.at[arriving] if k < 2 else sends.at[grad_arriving],
            send_sem=hop_ss.at[k, part],
            recv_sem=hop_rs.at[k, part],
            device_id=(dp, partner),
            device_id_type=MESH,
        )

    def out_copies(kind, u):
        target = (outputs, input_grads)[kind]
        place_out = target.at[pl.ds((core * 2 + u) * blocks, blocks)]
        k = 2 * kind + u
        own, other = (core, 1 - core) if kind == 0 else (1 - core, core)
        return (
            pltpu.make_async_copy(kept.at[own, u], place_out, out_ls.at[k]),
            to_peer(kept.at[other, u], place_out, out_ss.at[k], out_rs.at[k]),
        )

    def outputs_sent(u):
        local_copy, remote_copy = out_copies(0, u)
        local_copy.wait()
        remote_copy.wait_send()

        @pl.when(early)
        def _():
            for part in range(2):
                hop_copy(u, part).wait_send()

    for k in range(6):
        weight_local(k).start()
    for i in range(2):
        affine_local(i).start()

    @pl.when(early)
    def _():
        for u in range(2):
            token_copy(u).start()

    @pl.when(late)
    def _():
        for u in range(2):
            cotangent_copy(u).start()

    pl.semaphore_wait(barrier, count + 1)
    for i in range(2):
        affine_remote(i).start()
    for k in range(6):
        weight_remote(k).start()

    sums[...] = jnp.zeros_like(sums)
    log_rows[...] = jnp.zeros_like(log_rows)
    small[...] = jnp.zeros_like(small)
    for i in range(2):
        affine_local(i).wait()
        affine_remote(i).wait_recv()

    def gain(sub, which):
        return affine[sub, 0, which : which + 1, :]

    def bias(sub, which):
        return affine[sub, 1, which : which + 1, :]

    ends = [lengths[core, 0]]
    for j in range(1, lengths.shape[1]):
        ends.append(ends[-1] + lengths[core, j])

    def mask_of(shape, query_axis, first_query, first_key):
        query = lax.broadcasted_iota(jnp.int32, shape, query_axis) + first_query
        key = lax.broadcasted_iota(jnp.int32, shape, 1 - query_axis) + first_key
        apart = jnp.zeros(shape, jnp.int32)
        for end in ends:
            apart += (query >= end).astype(jnp.int32) - (key >= end).astype(jnp.int32)
        return jnp.where((apart == 0) & (key <= query), 0.0, masked_value)

    def projected(part, lanes, u=0, halves=1):
        span = pl.ds((2 * part + u) * blocks, halves * blocks)
        return sends[span, :, lanes].reshape(halves * unit, LANES)

    def half_lanes(h, scale):
        lane = lax.broadcasted_iota(jnp.int32, (1, LANES), 1)
        return jnp.where((lane >= h * HEAD) & (lane < (h + 1) * HEAD), scale, 0.0)

    def pair_lanes(p):
        return pl.ds(pl.multiple_of(p * LANES, LANES), LANES)

    def branch():
        return total[pl.ds(2 * blocks, blocks)].reshape(unit, width)

    def add_branch(term, begin):
        value = term if begin else branch() + term
        total[pl.ds(2 * blocks, blocks)] = value.reshape(blocks, rows, width)

    size = min(rows, 64)
    groups = rows // size

    def by_rows(body, part=None):
        def step(i, carry):
            block, start = i // groups, pl.multiple_of(lax.rem(i, groups) * size, size)
            body(block, pl.ds(start, size), pl.ds(pl.multiple_of(i * size, size), size))
            return carry

        half = unit // size // 2
        begin, end = (0, 2 * half) if part is None else (part * half, (part + 1) * half)
        lax.fori_loop(begin, end, step, 0, unroll=True)

    def add_sums(sub, which, grad, normal):
        row = 4 * sub + which
        sums[row] += jnp.sum((grad * normal).reshape(size // 8, 8, width), axis=0)
        sums[row + 2] += jnp.sum(grad.reshape(size // 8, 8, width), axis=0)

    def normed_input(sub, values):
        return (whiten(values)[0] * gain(sub, 0) + bias(sub, 0)).astype(low)

    def await_input(u, half):
        @pl.when(late)
        def _():
            hop_copy(u, half).wait_recv()

        if half == 0:

            @pl.when(early)
            def _():
                token_copy(u).wait()

    def await_grad(u, half):
        @pl.when(early)
        def _():
            hop_copy(2 + u, half).wait_recv()

        if half == 0:

            @pl.when(late)
            def _():
                cotangent_copy(u).wait()

    def send_part(stage, k, part):
        @pl.when(stage)
        def _():
            hop_copy(k, part).start()

    def attention_forward(u):
        span = slice(u * unit, (u + 1) * unit)

        def norm_in(block, some, _):
            values = stash[u * blocks + block, some, :].astype(f32)
            stash[4 * blocks + block, some, :] = normed_input(0, values)

        for i in range(u + 1):
            mask[i * unit : (i + 1) * unit, :] = mask_of((unit, unit), 0, u * unit, i * unit)

        def project_all(stage_weights):
            for part in range(3):
                if stage_weights:
                    await_chunk(part)
                value = dot(stash_read(4), weight(part)).astype(low)
                target = pl.ds((2 * part + u) * blocks, blocks)
                sends[target] = value.reshape(blocks, rows, width)

        if u == 1:
            for half in range(2):
                await_input(u, half)
                by_rows(norm_in, half)
            project_all(False)
        else:

            @pl.when(early)
            def _():
                token_copy(u).wait()
                by_rows(norm_in)
                project_all(True)

            @pl.when(late)
            def _():
                for part in range(3):
                    await_chunk(part)
                part_blocks = blocks // 2
                for half in range(2):
                    hop_copy(u, half).wait_recv()
                    by_rows(norm_in, half)
                    normed = stash[pl.ds(4 * blocks + half * part_blocks, part_blocks)]
                    normed = normed.reshape(unit // 2, width)
                    for part in range(3):
                        value = dot(normed, weight(part)).astype(low)
                        target = pl.ds(2 * part * blocks + half * part_blocks, part_blocks)
                        sends[target] = value.reshape(part_blocks, rows, width)

        lhs[0, :, span] = stash_read(4).T
        lane = lax.broadcasted_iota(jnp.int32, (unit, LANES), 1)

        def pair(p, carry):
            lanes = pair_lanes(p)
            query = projected(0, lanes, u).astype(f32)
            key = projected(1, lanes, 0, u + 1)
            value = projected(2, lanes, 0, u + 1)
            added = jnp.concatenate([mask[i * unit : (i + 1) * unit, :] for i in range(u + 1)], 1)
            both = [(query * half_lanes(h, score_scale)).astype(low) for h in range(2)]
            scores = dot_cols(jnp.concatenate(both, axis=0), key)
            scores = scores + jnp.concatenate([added, added], axis=0)
            top = jnp.max(scores, axis=-1, keepdims=True)
            exponent = jnp.exp(scores - top)
            summed = jnp.sum(exponent, axis=-1, keepdims=True)
            context = dot(exponent.astype(low), value) * (1.0 / summed)
            log_total = top + jnp.log(summed)
            logs = jnp.where(lane == 2 * p, log_total[:unit], log_rows[...])
            log_rows[...] = jnp.where(lane == 2 * p + 1, log_total[unit:], logs)
            context = jnp.where(lane < HEAD, context[:unit], context[unit:])
            rhs[3, span, lanes] = context.astype(low)
            return carry

        lax.fori_loop(0, PAIRS, pair, 0, unroll=4)
        log_t[u] = log_rows[...].T[:HEADS]
        if u == 0:
            await_chunk(3)
        add_branch(dot_cols(rhs[3, span, :], weight(3)), True)

        def norm_out(block, some, across):
            normal, spread = whiten(total[2 * blocks + block, some, :])
            stash[(2 + u) * blocks + block, some, :] = normal.astype(low)
            spreads[pl.ds(u * unit + across.start, size), 0:1] = spread
            middle = stash[u * blocks + block, some, :].astype(f32)
            middle = (middle + (normal * gain(0, 1) + bias(0, 1))).astype(low)
            kept[0, u, block, some, :] = middle
            stash[4 * blocks + block, some, :] = normed_input(1, middle.astype(f32))

        by_rows(norm_out)

    def feed_forward(u):
        span = slice(u * unit, (u + 1) * unit)
        lhs[2, :, span] = stash_read(4).T
        for i in range(4):
            c = lax.rem(2 * core + i, 4) if u == 0 else i
            if u == 0:
                await_feed(i)
            hidden, slope = gelu_both(dot(stash_read(4), weight(4 + c)))
            hidden = hidden.astype(low)
            rhs[4 + c, span, :] = slope.astype(low)
            hidden_t[pl.ds(pl.multiple_of(c * width, width), width), span] = hidden.T
            add_branch(dot(hidden, weight(8 + c)), i == 0)

        def norm_out(block, some, across):
            normal, spread = whiten(total[2 * blocks + block, some, :])
            stash[(5 + u) * blocks + block, some, :] = normal.astype(low)
            spreads[pl.ds(u * unit + across.start, size), 1:2] = spread
            middle = kept[0, u, block, some, :].astype(f32)
            output = middle + (normal * gain(1, 1) + bias(1, 1))
            kept[1, u, block, some, :] = output.astype(low)

        for half in range(2):
            by_rows(norm_out, half)
            send_part(early, u, half)

    def feed_backward(u):
        span = slice(u * unit, (u + 1) * unit)

        def back_out(block, some, across):
            own = pl.ds(u * unit + across.start, size)
            upstream = sends[(6 + u) * blocks + block, some, :].astype(f32)
            normal = stash[(5 + u) * blocks + block, some, :].astype(f32)
            add_sums(1, 1, upstream, normal)
            dz = whiten_back(upstream * gain(1, 1), normal, spreads[own, 1:2])
            dz_down[own, :] = dz.astype(low)

        for half in range(2):
            await_grad(u, half)
            by_rows(back_out, half)
        for c in range(4):
            d_hidden = dot_cols(dz_down[span, :], weight(8 + c))
            d_pre = (d_hidden * rhs[4 + c, span, :].astype(f32)).astype(low)
            rhs[4 + c, span, :] = d_pre
            add_branch(dot_cols(d_pre, weight(4 + c)), c == 0)

        def back_in(block, some, across):
            own = pl.ds(u * unit + across.start, size)
            normal, spread = whiten(kept[0, u, block, some, :].astype(f32))
            d_normed = total[2 * blocks + block, some, :]
            add_sums(1, 0, d_normed, normal)
            d_ln = whiten_back(d_normed * gain(1, 0), normal, spread)
            d_middle = (sends[(6 + u) * blocks + block, some, :].astype(f32) + d_ln).astype(low)
            kept[0, u, block, some, :] = d_middle
            upstream = d_middle.astype(f32)
            normal = stash[(2 + u) * blocks + block, some, :].astype(f32)
            add_sums(0, 1, upstream, normal)
            dz = whiten_back(upstream * gain(0, 1), normal, spreads[own, 0:1])
            stash[4 * blocks + block, some, :] = dz.astype(low)

        outputs_sent(u)
        if u == 0:
            for other in (left, right):
                pl.semaphore_signal(
                    ready, inc=1, device_id=(other, section), device_id_type=MESH
                )
            pl.semaphore_signal(ready, inc=1, device_id=(dp, peer), device_id_type=MESH)
        by_rows(back_in)

    def attention_backward(u):
        span = slice(u * unit, (u + 1) * unit)
        keys = (u + 1) * unit
        lhs[1, :, span] = stash_read(4).T
        d_context = dot(stash_read(4), weight(3)).astype(low)
        stash_write(4, d_context)
        product = (d_context.astype(f32) * rhs[3, span, :].astype(f32)).astype(low)
        head = lax.broadcasted_iota(jnp.int32, (HEADS, width), 0)
        column = lax.broadcasted_iota(jnp.int32, (HEADS, width), 1)
        inside = (column >= head * HEAD) & (column < (head + 1) * HEAD)
        delta_t[...] = dot_cols(jnp.where(inside, 1.0, 0.0).astype(low), product)
        mask[:keys, :] = mask_of((keys, unit), 1, u * unit, 0)

        def pair(p, carry):
            lanes = pair_lanes(p)
            query = projected(0, lanes, u).astype(f32)
            key = projected(1, lanes, 0, u + 1)
            value = projected(2, lanes, 0, u + 1)
            d_out = stash[pl.ds(4 * blocks, blocks), :, lanes].reshape(unit, LANES).astype(f32)
            key_t = key.T
            heads = range(2)
            query_both = [(query * half_lanes(h, score_scale)).astype(low) for h in heads]
            query_both = jnp.concatenate(query_both, axis=0)
            d_out_both = [(d_out * half_lanes(h, 1.0)).astype(low) for h in heads]
            d_out_both = jnp.concatenate(d_out_both, axis=0)
            logs = jnp.concatenate([log_t[u, pl.ds(2 * p + h, 1), :] for h in heads], axis=1)
            delta = jnp.concatenate([delta_t[pl.ds(2 * p + h, 1), :] for h in heads], axis=1)
            added = mask[:keys, :]
            scores = dot_cols(key, query_both) + jnp.concatenate([added, added], axis=1)
            prob = jnp.exp(scores - logs)
            d_prob = dot_cols(value, d_out_both)
            d_scores = (prob * (d_prob - delta)).astype(low)
            d_value = dot(prob.astype(low), d_out_both)
            d_key = dot(d_scores, query_both)
            d_query = [
                dot(key_t[h * HEAD : (h + 1) * HEAD, :], d_scores[:, h * unit : (h + 1) * unit])
                for h in heads
            ]
            d_query = jnp.concatenate(d_query, axis=0) * score_scale
            rhs[0, span, lanes] = d_query.T.astype(low)
            for i, grad in ((0, d_key), (1, d_value)):
                carried = pl.ds(i * blocks, blocks)
                if u == 1:
                    rhs[1 + i, span, lanes] = grad[unit:].astype(low)
                    total[carried, :, lanes] = grad[:unit].reshape(blocks, rows, LANES)
                else:
                    grad = grad + total[carried, :, lanes].reshape(unit, LANES)
                    rhs[1 + i, span, lanes] = grad.astype(low)
            return carry

        lax.fori_loop(0, PAIRS, pair, 0, unroll=4)
        for part in range(3):
            add_branch(dot_cols(rhs[part, span, :], weight(part)), part == 0)

        def back_in(block, some, across):
            normal, spread = whiten(stash[u * blocks + block, some, :].astype(f32))
            d_normed = total[2 * blocks + block, some, :]
            add_sums(0, 0, d_normed, normal)
            d_ln = whiten_back(d_normed * gain(0, 0), normal, spread)
            d_input = kept[0, u, block, some, :].astype(f32) + d_ln
            kept[1, u, block, some, :] = d_input.astype(low)

        for half in range(2):
            by_rows(back_in, half)
            send_part(late, 2 + u, half)

    def pair_block(step, stream=0):
        return jnp.where(step == 0, 6 * count, 6 * (step - 1)) + stream

    def ring_block(step, stream):
        return 12 * count - 6 * (step + 1) + stream

    def pair_slot(step):
        return jnp.where(lax.rem(step, 2) == 0, 5 * blocks, 0)

    def ring_slot(step):
        return jnp.where(lax.rem(step, 2) == 0, 6 * blocks, 0)

    def pair_copy(step):
        return to_peer(
            stash.at[pl.ds(pair_slot(step), 6)],
            pool.at[pl.ds(pair_block(step), 6)],
            pair_ss.at[lax.rem(step, 2)],
            pair_rs.at[step],
        )

    def pair_first(stream):
        return to_peer(
            stash.at[5 * blocks + stream],
            pool.at[6 * count + stream],
            first_ss.at[stream],
            first_rs.at[stream],
        )

    def ring_copy(step, stream):
        return pltpu.make_async_remote_copy(
            src_ref=sends.at[ring_slot(step) + stream],
            dst_ref=pool.at[ring_block(step, stream)],
            send_sem=ring_ss.at[lax.rem(step, 2), stream],
            recv_sem=ring_rs.at[step, stream],
            device_id=(jnp.where(stream < 3, right, left), section),
            device_id_type=MESH,
        )

    def ring_row(step, stream):
        behind = lax.rem(place + 2 * count - 1 - step, count)
        ahead = lax.rem(place + 1 + step, count)
        return ring_index(jnp.where(stream < 3, behind, ahead), count)

    def stream_of(group):
        return group + group // 2

    def product(step, group, part):
        block = ring_row(step, stream_of(group))
        side = jnp.where(part == 1, 2, jnp.where(group == 3, 1, 0))
        piece = lhs[side, pl.ds(pl.multiple_of(block * rows, rows), rows), :]
        return dot(piece, rhs[part * 4 + group])

    def down_product(step, turn, part):
        block = ring_row(step, 2 + 3 * turn)
        start = part * (2 * width) + block * (2 * rows) + turn * rows
        return dot(hidden_t[pl.ds(pl.multiple_of(start, rows), rows), :], dz_down[...])

    def each(count_of, action):
        def step(i, carry):
            action(i)
            return carry

        lax.fori_loop(0, count_of, step, 0)

    def pair_part(step):
        slot = pair_slot(step)

        def group_part(group):
            value = product(step, group, 1 - core)
            stash[slot + stream_of(group)] = value.astype(low)

        def down_part(turn):
            stash[slot + 2 + 3 * turn] = down_product(step, turn, 1 - core).astype(low)

        each(4, group_part)
        each(2, down_part)

    def own_part(step):
        def group_part(group):
            total[stream_of(group)] = product(step, group, core)

        def down_part(turn):
            total[2 + 3 * turn] = down_product(step, turn, core)

        each(4, group_part)
        each(2, down_part)

    def turn_about(i):
        return i // 2 + 2 * lax.rem(i, 2)

    def first_pair_group(i):
        group = turn_about(i)
        stream = stream_of(group)
        stash[5 * blocks + stream] = product(0, group, 1 - core).astype(low)
        pair_first(stream).start()

    def first_pair_down(turn):
        stash[5 * blocks + 2 + 3 * turn] = down_product(0, turn, 1 - core).astype(low)

    def first_own_group(group):
        stream = stream_of(group)
        sends[6 * blocks + stream] = product(0, group, core).astype(low)

    def first_own_down(turn):
        sends[6 * blocks + 2 + 3 * turn] = down_product(0, turn, core).astype(low)

    def first_ring_group(i):
        first_ring(stream_of(turn_about(i)))

    def first_ring(stream):
        pair_first(stream).wait_recv()
        value = sends[6 * blocks + stream].astype(f32) + pool[6 * count + stream].astype(f32)
        sends[6 * blocks + stream] = value.astype(low)
        ring_copy(0, stream).start()

    def feed_first():
        each(2, first_pair_down)
        pl.semaphore_wait(ready, 3)
        each(2, lambda turn: pair_first(2 + 3 * turn).start())
        each(2, first_own_down)

        @pl.when(core == 0)
        def _():
            each(4, first_pair_group)

        @pl.when(core == 1)
        def _():
            each(4, first_own_group)

        each(2, lambda turn: first_ring(2 + 3 * turn))

        @pl.when(core == 1)
        def _():
            each(4, first_ring_group)

    for u in range(2):
        attention_forward(u)
        feed_forward(u)
        for copy in out_copies(0, u):
            copy.start()

    feed_backward(1)
    attention_backward(1)
    for copy in out_copies(1, 1):
        copy.start()
    feed_backward(0)

    def last_attention(turn):
        pl.when(turn == jnp.where(early, 0, 1))(feed_first)

        @pl.when(turn == 0)
        def _():
            attention_backward(0)

    each(2, last_attention)
    for copy in out_copies(1, 0):
        copy.start()
    for k in range(8):
        (weight_remote(k) if k < 6 else affine_remote(k - 6)).wait_send()
    pl.semaphore_signal(pair_ready, inc=1, device_id=(dp, peer), device_id_type=MESH)

    @pl.when(core == 1)
    def _():
        each(4, first_pair_group)

    @pl.when(core == 0)
    def _():
        each(4, first_own_group)
        each(4, first_ring_group)

    @pl.when(late)
    def _():
        for k in (2, 3):
            for half in range(2):
                hop_copy(k, half).wait_send()

    pair_part(1)
    pl.semaphore_wait(pair_ready, 1)
    pair_copy(1).start()
    own_part(1)

    slice_width = width // count
    for j in range(count):
        piece = sums[:, :, j * slice_width : (j + 1) * slice_width]
        small[j, :, :slice_width] = jnp.sum(piece, axis=1)

    gb_pair = to_peer(small, small_pair, small_sems.at[0], small_sems.at[1])

    def gb_copy(step):
        other = lax.rem(dp + step, count)
        return pltpu.make_async_remote_copy(
            src_ref=small_sum.at[other],
            dst_ref=small_recv.at[step],
            send_sem=small_ss.at[step],
            recv_sem=small_rs.at[step],
            device_id=(other, section),
            device_id_type=MESH,
        )

    gb_pair.start()
    gb_pair.wait()
    small_sum[...] = small[...] + small_pair[...]

    def gb_start(step, carry):
        gb_copy(step).start()
        return carry

    lax.fori_loop(1, count, gb_start, 0)

    for stream in range(6):
        pair_first(stream).wait_send()

    def ring_step(step, carry):
        pair_copy(step).wait_recv()

        def forward(i):
            turn = i // 2
            stream = 3 * lax.rem(i, 2) + jnp.where(turn == 0, 2, turn - 1)
            ring_copy(step - 1, stream).wait_recv()
            value = total[stream] + pool[pair_block(step, stream)].astype(f32)
            value = value + pool[ring_block(step - 1, stream)].astype(f32)

            @pl.when(step >= 2)
            def _():
                ring_copy(step - 2, stream).wait_send()

            sends[ring_slot(step) + stream] = value.astype(low)
            ring_copy(step, stream).start()

        each(6, forward)

        @pl.when(step >= 2)
        def _():
            pair_copy(step - 1).wait_send()

        pair_part(step + 1)
        pair_copy(step + 1).start()
        own_part(step + 1)
        return carry

    lax.fori_loop(1, count - 1, ring_step, 0)

    def grad_copy(stream):
        if stream % 3 < 2:
            group = stream % 3 + 2 * (stream // 3)
            target = first_grad.at[:, pl.ds(group * width, width)]
        else:
            target = down_grad.at[pl.ds((stream // 3) * rows, rows)]
        return pltpu.make_async_copy(total.at[stream], target, grad_ls.at[stream])

    last = count - 1
    pair_copy(last).wait_recv()
    for stream in (2, 5, 0, 3, 1, 4):
        total[stream] += pool[pair_block(last, stream)].astype(f32)
        ring_copy(last - 1, stream).wait_recv()
        total[stream] += pool[ring_block(last - 1, stream)].astype(f32)
        grad_copy(stream).start()

    small_out[...] = small_sum[dp]

    def gb_finish(step, carry):
        gb_copy(step).wait()
        small_out[...] += small_recv[step]
        return carry

    lax.fori_loop(1, count, gb_finish, 0)
    for stream in range(6):
        ring_copy(last - 1, stream).wait_send()
        ring_copy(last - 2, stream).wait_send()
        grad_copy(stream).wait()
    pair_copy(last).wait_send()
    pair_copy(last - 1).wait_send()
    for u in range(2):
        out_copies(0, u)[1].wait_recv()
        local_copy, remote_copy = out_copies(1, u)
        local_copy.wait()
        remote_copy.wait()


def layers(tokens, cotangent, lengths, first, down, gains, biases):
    count = lax.axis_size("dp")
    token_count, width = tokens.shape
    row_len = token_count // lengths.shape[0]
    unit = row_len // 2
    rows = width // count
    blocks = unit // rows
    vmem = pl.BlockSpec(memory_space=pltpu.VMEM)
    anywhere = pl.BlockSpec(memory_space=pl.ANY)
    sem = pltpu.SemaphoreType.DMA
    shape = jax.ShapeDtypeStruct
    buffer = pltpu.VMEM
    cut = (token_count // rows, rows, width)
    small = (count, 8, max(128, width // count))
    outs = pl.pallas_call(
        functools.partial(layers_kernel, count),
        out_shape=(
            shape(cut, low),
            shape(cut, low),
            shape((rows, 4 * width), f32),
            shape((2 * rows, width), f32),
            shape(small[1:], f32),
        ),
        in_specs=[anywhere, anywhere, pl.BlockSpec(memory_space=pltpu.SMEM)] + [anywhere] * 4,
        out_specs=(anywhere, anywhere, anywhere, anywhere, vmem),
        scratch_shapes=[
            buffer((12 * count, rows, width), low),
            buffer((8 * blocks + max(0, 6 - 2 * blocks), rows, width), low),
            buffer((7 * blocks + max(0, 6 - 2 * blocks), rows, width), low),
            buffer((row_len, 128), f32),
            buffer((2, 2, blocks, rows, width), low),
            buffer((row_len, unit), f32),
            buffer((max(6, 3 * blocks), rows, width), f32),
            buffer((3, width, row_len), low),
            buffer((4 * width, row_len), low),
            buffer((8, row_len, width), low),
            buffer((row_len, width), low),
            buffer((2, 2, 2, width), f32),
            buffer((2, HEADS, unit), f32),
            buffer((unit, LANES), f32),
            buffer((HEADS, unit), f32),
            buffer((8, 8, width), f32),
            buffer(small, f32),
            buffer(small, f32),
            buffer(small, f32),
            buffer(small, f32),
            sem((8,)),
            sem((8,)),
            sem((8,)),
            sem((4,)),
            sem((4, 2)),
            sem((4, 2)),
            sem((4,)),
            sem((4,)),
            sem((4,)),
            pltpu.SemaphoreType.REGULAR,
            pltpu.SemaphoreType.REGULAR,
            sem((6,)),
            sem((6,)),
            sem((2,)),
            sem((count,)),
            sem((2, 6)),
            sem((count - 1, 6)),
            sem((2,)),
            sem((count,)),
            sem((count,)),
            sem((6,)),
        ],
        compiler_params=pltpu.CompilerParams(
            collective_id=0, has_side_effects=True, vmem_limit_bytes=63 * 1024 * 1024
        ),
        name="layers",
    )(
        tokens.reshape(cut),
        cotangent.reshape(cut),
        lengths,
        first.reshape(count, rows, 4 * width),
        down.reshape(2 * count, rows, width),
        gains,
        biases,
    )
    return outs


def place_kernel(*refs):
    sources, small, targets, (gain_grad, bias_grad) = refs[:4], refs[4], refs[5:9], refs[9:11]
    buffers, (arrived, written) = refs[11:15], refs[15:]
    reads, writes = [], []
    for i, (source, target, buffer) in enumerate(zip(sources, targets, buffers)):
        reads.append(pltpu.make_async_copy(source, buffer, arrived.at[i]))
        writes.append(pltpu.make_async_copy(buffer, target.at[0], written.at[i]))
    for read in reads:
        read.start()
    feed = lax.axis_index("section") % 2 == 1
    width = gain_grad.shape[2]
    gain_grad[0] = jnp.where(feed, small[4:6, :width], small[0:2, :width])
    bias_grad[0] = jnp.where(feed, small[6:8, :width], small[2:4, :width])
    for read, write in zip(reads, writes):
        read.wait()
        write.start()
    for write in writes:
        write.wait()


def local(tokens, doc_lengths, first_weights, down_weights, norm_gains, norm_biases, cotangent):
    width = tokens.shape[1]
    outputs, input_grads, first_part, down_part, small = layers(
        tokens,
        cotangent,
        doc_lengths,
        first_weights[0],
        down_weights[0],
        norm_gains,
        norm_biases,
    )
    slice_width = width // lax.axis_size("dp")
    results = [outputs.reshape(tokens.shape), input_grads.reshape(tokens.shape)]
    results += [first_part, down_part]
    norm_part = jax.ShapeDtypeStruct((1, 2, slice_width), f32)
    anywhere = pl.BlockSpec(memory_space=pl.ANY)
    vmem = pl.BlockSpec(memory_space=pltpu.VMEM)
    return pl.pallas_call(
        place_kernel,
        out_shape=[jax.ShapeDtypeStruct((1,) + r.shape, r.dtype) for r in results]
        + [norm_part, norm_part],
        in_specs=[anywhere] * 4 + [vmem],
        out_specs=[anywhere] * 4 + [vmem] * 2,
        scratch_shapes=[pltpu.VMEM(r.shape, r.dtype) for r in results]
        + [pltpu.SemaphoreType.DMA((4,))] * 2,
        name="place",
    )(*results, small)


def solution(mesh):
    placed = (
        P("dp", None),
        P("dp", None),
        P("section", None, None),
        P("section", None, None),
        P("section", None, None),
        P("section", None, None),
        P("dp", None),
    )
    return jax.shard_map(
        local,
        mesh=mesh,
        in_specs=placed,
        out_specs=(
            P("section", "dp", None),
            P("section", "dp", None),
            P("section", "dp", None),
            P("section", "dp", None),
            P("section", None, "dp"),
            P("section", None, "dp"),
        ),
        check_vma=False,
    )
```

```python
import functools

import jax
import jax.numpy as jnp
from jax import lax
from jax.experimental import pallas as pl
from jax.experimental.pallas import tpu as pltpu
from jax.sharding import PartitionSpec as P

HEADS = 16
HEAD = 64
PAIRS = HEADS // 2
LANES = 2 * HEAD
eps = 1e-05
masked_value = -1e30
score_scale = HEAD ** (-0.5)
MESH = pl.DeviceIdType.MESH
low = jnp.bfloat16
f32 = jnp.float32
tanh_linear = (2.0 / 3.141592653589793) ** 0.5
tanh_cubic = tanh_linear * 0.044715


def ring_place(index, count):
    return jnp.where(index % 2 == 0, index // 2, count - 1 - index // 2)


def ring_index(place, count):
    return jnp.where(place < count // 2, 2 * place, 2 * (count - 1 - place) + 1)


def dot(left, right):
    return jnp.dot(left, right, preferred_element_type=f32)


def dot_cols(left, right):
    return lax.dot_general(left, right, (((1,), (1,)), ((), ())), preferred_element_type=f32)


def whiten(values):
    average = jnp.mean(values, axis=-1, keepdims=True)
    centered = values - average
    variance = jnp.mean(centered * centered, axis=-1, keepdims=True)
    spread = lax.rsqrt(variance + eps)
    return centered * spread, spread


def whiten_back(grad, normal, spread):
    first = jnp.mean(grad, axis=-1, keepdims=True)
    second = jnp.mean(grad * normal, axis=-1, keepdims=True)
    return spread * (grad - first - normal * second)


def gelu_both(u):
    square = u * u
    half = 0.5 + 0.5 * jnp.tanh(u * (tanh_linear + tanh_cubic * square))
    value = u * half
    slope = half + value * (1.0 - half) * (2.0 * tanh_linear + 6.0 * tanh_cubic * square)
    return value, slope


def layers_kernel(
    count,
    tokens,
    cotangent,
    lengths,
    first,
    down,
    gains,
    biases,
    outputs,
    input_grads,
    first_grad,
    down_grad,
    small_out,
    pool,
    sends,
    stash,
    spreads,
    kept,
    mask,
    total,
    lhs,
    hidden_t,
    rhs,
    dz_down,
    affine,
    log_t,
    log_rows,
    delta_t,
    sums,
    small,
    small_pair,
    small_sum,
    small_recv,
    weight_ls,
    weight_ss,
    weight_rs,
    row_ls,
    hop_ss,
    hop_rs,
    out_ls,
    out_ss,
    out_rs,
    ready,
    pair_ready,
    first_ss,
    first_rs,
    pair_ss,
    pair_rs,
    ring_ss,
    ring_rs,
    small_sems,
    small_ss,
    small_rs,
    grad_ls,
):
    rows, width = pool.shape[1:]
    row_len = rhs.shape[1]
    unit = row_len // 2
    blocks = unit // rows
    dp = lax.axis_index("dp")
    section = lax.axis_index("section")
    section_count = lax.axis_size("section")
    core = lax.rem(section, 2)
    peer = section + 1 - 2 * core
    early = section < 2
    late = section >= 2
    partner = lax.rem(section + 2, section_count)
    place = ring_place(dp, count)
    left = ring_index(lax.rem(place + count - 1, count), count)
    right = ring_index(lax.rem(place + 1, count), count)

    barrier = pltpu.get_barrier_semaphore()

    def greet(step, carry):
        other = lax.rem(dp + step, count)
        pl.semaphore_signal(barrier, inc=1, device_id=(other, section), device_id_type=MESH)
        return carry

    lax.fori_loop(1, count, greet, 0)
    for other in (peer, partner):
        pl.semaphore_signal(barrier, inc=1, device_id=(dp, other), device_id_type=MESH)

    def own_chunk(k):
        if k < 4:
            return first.at[:, :, pl.ds(k * width, width)], 4 * core + k
        return down.at[pl.ds((k - 4) * count, count)], 8 + 2 * core + k - 4

    def weight_local(k):
        source, chunk = own_chunk(k)
        target = pool.at[pl.ds(chunk * count, count)]
        return pltpu.make_async_copy(source, target, weight_ls.at[k])

    def to_peer(source, target, send_sem, recv_sem):
        return pltpu.make_async_remote_copy(
            src_ref=source,
            dst_ref=target,
            send_sem=send_sem,
            recv_sem=recv_sem,
            device_id=(dp, peer),
            device_id_type=MESH,
        )

    def weight_remote(k):
        source, chunk = own_chunk(k)
        target = pool.at[pl.ds(chunk * count, count)]
        return to_peer(source, target, weight_ss.at[k], weight_rs.at[k])

    def affine_local(i):
        source = (gains, biases)[i].at[0]
        return pltpu.make_async_copy(source, affine.at[core, i], weight_ls.at[6 + i])

    def affine_remote(i):
        source = (gains, biases)[i].at[0]
        return to_peer(source, affine.at[core, i], weight_ss.at[6 + i], weight_rs.at[6 + i])

    def await_chunk(chunk):
        owner = 1 if 4 <= chunk < 8 or chunk >= 10 else 0
        k = chunk % 4 if chunk < 8 else 4 + chunk % 2

        @pl.when(core == owner)
        def _():
            weight_local(k).wait()

        @pl.when(core != owner)
        def _():
            weight_remote(k).wait_recv()

    def await_feed(i):
        @pl.when(core == 0)
        def _():
            weight_remote(i).wait_recv()

        @pl.when(core == 1)
        def _():
            weight_local((i + 2) % 4).wait()

    def await_down(i):
        if i < 2:
            weight_local(4 + i).wait()
        else:
            weight_remote(2 + i).wait_recv()

    def weight(chunk):
        return pool[pl.ds(chunk * count, count)].reshape(width, width)

    def weight_cols(chunk, some):
        return pool[pl.ds(chunk * count, count), :, some].reshape(width, width // 2)

    def weight_rows(chunk, half):
        start = chunk * count + half * (count // 2)
        return pool[pl.ds(start, count // 2)].reshape(width // 2, width)

    def stash_at(place_in):
        return stash.at[pl.ds(place_in * blocks, blocks)]

    def stash_read(place_in):
        return stash[pl.ds(place_in * blocks, blocks)].reshape(unit, width)

    def stash_write(place_in, value):
        stash[pl.ds(place_in * blocks, blocks)] = value.astype(low).reshape(blocks, rows, width)

    def row_copy(u, source, target, sem):
        start = (core * 2 + u) * blocks
        return pltpu.make_async_copy(source.at[pl.ds(start, blocks)], target, sem)

    def token_copy(u):
        return row_copy(u, tokens, stash_at(u), row_ls.at[u])

    def cotangent_copy(u):
        return row_copy(u, cotangent, sends.at[pl.ds((6 + u) * blocks, blocks)], row_ls.at[2 + u])

    def hop_copy(k, part):
        u = k % 2
        some = pl.ds(part * (blocks // 2), blocks // 2)
        arriving = pl.ds(u * blocks + part * (blocks // 2), blocks // 2)
        grad_arriving = pl.ds((6 + u) * blocks + part * (blocks // 2), blocks // 2)
        return pltpu.make_async_remote_copy(
            src_ref=kept.at[1, u, some],
            dst_ref=stash.at[arriving] if k < 2 else sends.at[grad_arriving],
            send_sem=hop_ss.at[k, part],
            recv_sem=hop_rs.at[k, part],
            device_id=(dp, partner),
            device_id_type=MESH,
        )

    def out_copies(kind, u):
        target = (outputs, input_grads)[kind]
        place_out = target.at[pl.ds((core * 2 + u) * blocks, blocks)]
        k = 2 * kind + u
        own, other = (core, 1 - core) if kind == 0 else (1 - core, core)
        return (
            pltpu.make_async_copy(kept.at[own, u], place_out, out_ls.at[k]),
            to_peer(kept.at[other, u], place_out, out_ss.at[k], out_rs.at[k]),
        )

    def outputs_sent(u):
        local_copy, remote_copy = out_copies(0, u)
        local_copy.wait()
        remote_copy.wait_send()

        @pl.when(early)
        def _():
            for part in range(2):
                hop_copy(u, part).wait_send()

    for k in range(6):
        weight_local(k).start()
    for i in range(2):
        affine_local(i).start()

    @pl.when(early)
    def _():
        for u in range(2):
            token_copy(u).start()

    @pl.when(late)
    def _():
        for u in range(2):
            cotangent_copy(u).start()

    pl.semaphore_wait(barrier, count + 1)
    for i in range(2):
        affine_remote(i).start()
    for k in range(6):
        weight_remote(k).start()

    sums[...] = jnp.zeros_like(sums)
    log_rows[...] = jnp.zeros_like(log_rows)
    small[...] = jnp.zeros_like(small)
    for i in range(2):
        affine_local(i).wait()
        affine_remote(i).wait_recv()

    def gain(sub, which):
        return affine[sub, 0, which : which + 1, :]

    def bias(sub, which):
        return affine[sub, 1, which : which + 1, :]

    ends = [lengths[core, 0]]
    for j in range(1, lengths.shape[1]):
        ends.append(ends[-1] + lengths[core, j])

    def mask_of(shape, query_axis, first_query, first_key):
        query = lax.broadcasted_iota(jnp.int32, shape, query_axis) + first_query
        key = lax.broadcasted_iota(jnp.int32, shape, 1 - query_axis) + first_key
        apart = jnp.zeros(shape, jnp.int32)
        for end in ends:
            apart += (query >= end).astype(jnp.int32) - (key >= end).astype(jnp.int32)
        return jnp.where((apart == 0) & (key <= query), 0.0, masked_value)

    def projected(part, lanes, u=0, halves=1):
        span = pl.ds((2 * part + u) * blocks, halves * blocks)
        return sends[span, :, lanes].reshape(halves * unit, LANES)

    def half_lanes(h, scale):
        lane = lax.broadcasted_iota(jnp.int32, (1, LANES), 1)
        return jnp.where((lane >= h * HEAD) & (lane < (h + 1) * HEAD), scale, 0.0)

    def pair_lanes(p):
        return pl.ds(pl.multiple_of(p * LANES, LANES), LANES)

    def branch():
        return total[pl.ds(2 * blocks, blocks)].reshape(unit, width)

    def add_branch(term, begin):
        value = term if begin else branch() + term
        total[pl.ds(2 * blocks, blocks)] = value.reshape(blocks, rows, width)

    size = min(rows, 64)
    groups = rows // size

    def by_rows(body, part=None):
        def step(i, carry):
            block, start = i // groups, pl.multiple_of(lax.rem(i, groups) * size, size)
            body(block, pl.ds(start, size), pl.ds(pl.multiple_of(i * size, size), size))
            return carry

        half = unit // size // 2
        begin, end = (0, 2 * half) if part is None else (part * half, (part + 1) * half)
        lax.fori_loop(begin, end, step, 0, unroll=True)

    def add_sums(sub, which, grad, normal):
        row = 4 * sub + which
        sums[row] += jnp.sum((grad * normal).reshape(size // 8, 8, width), axis=0)
        sums[row + 2] += jnp.sum(grad.reshape(size // 8, 8, width), axis=0)

    def normed_input(sub, values):
        return (whiten(values)[0] * gain(sub, 0) + bias(sub, 0)).astype(low)

    def await_input(u, half):
        @pl.when(late)
        def _():
            hop_copy(u, half).wait_recv()

        if half == 0:

            @pl.when(early)
            def _():
                token_copy(u).wait()

    def await_grad(u, half):
        @pl.when(early)
        def _():
            hop_copy(2 + u, half).wait_recv()

        if half == 0:

            @pl.when(late)
            def _():
                cotangent_copy(u).wait()

    def send_part(stage, k, part):
        @pl.when(stage)
        def _():
            hop_copy(k, part).start()

    def attention_forward(u):
        span = slice(u * unit, (u + 1) * unit)

        def norm_in(block, some, _):
            values = stash[u * blocks + block, some, :].astype(f32)
            stash[4 * blocks + block, some, :] = normed_input(0, values)

        for i in range(u + 1):
            mask[i * unit : (i + 1) * unit, :] = mask_of((unit, unit), 0, u * unit, i * unit)

        def project_all(stage_weights):
            for part in range(3):
                if stage_weights:
                    await_chunk(part)
                value = dot(stash_read(4), weight(part)).astype(low)
                target = pl.ds((2 * part + u) * blocks, blocks)
                sends[target] = value.reshape(blocks, rows, width)

        if u == 1:
            for half in range(2):
                await_input(u, half)
                by_rows(norm_in, half)
            project_all(False)
        else:

            @pl.when(early)
            def _():
                token_copy(u).wait()
                by_rows(norm_in)
                project_all(True)

            @pl.when(late)
            def _():
                for part in range(3):
                    await_chunk(part)
                part_blocks = blocks // 2
                for half in range(2):
                    hop_copy(u, half).wait_recv()
                    by_rows(norm_in, half)
                    normed = stash[pl.ds(4 * blocks + half * part_blocks, part_blocks)]
                    normed = normed.reshape(unit // 2, width)
                    for part in range(3):
                        value = dot(normed, weight(part)).astype(low)
                        target = pl.ds(2 * part * blocks + half * part_blocks, part_blocks)
                        sends[target] = value.reshape(part_blocks, rows, width)

        lhs[0, :, span] = stash_read(4).T
        lane = lax.broadcasted_iota(jnp.int32, (unit, LANES), 1)

        def pair(p, carry):
            lanes = pair_lanes(p)
            query = projected(0, lanes, u).astype(f32)
            key = projected(1, lanes, 0, u + 1)
            value = projected(2, lanes, 0, u + 1)
            added = jnp.concatenate([mask[i * unit : (i + 1) * unit, :] for i in range(u + 1)], 1)
            both = [(query * half_lanes(h, score_scale)).astype(low) for h in range(2)]
            scores = dot_cols(jnp.concatenate(both, axis=0), key)
            scores = scores + jnp.concatenate([added, added], axis=0)
            top = jnp.max(scores, axis=-1, keepdims=True)
            exponent = jnp.exp(scores - top)
            summed = jnp.sum(exponent, axis=-1, keepdims=True)
            context = dot(exponent.astype(low), value) * (1.0 / summed)
            log_total = top + jnp.log(summed)
            logs = jnp.where(lane == 2 * p, log_total[:unit], log_rows[...])
            log_rows[...] = jnp.where(lane == 2 * p + 1, log_total[unit:], logs)
            context = jnp.where(lane < HEAD, context[:unit], context[unit:])
            rhs[3, span, lanes] = context.astype(low)
            return carry

        lax.fori_loop(0, PAIRS, pair, 0, unroll=4)
        log_t[u] = log_rows[...].T[:HEADS]
        if u == 0:
            await_chunk(3)
        add_branch(dot_cols(rhs[3, span, :], weight(3)), True)

        def norm_out(block, some, across):
            normal, spread = whiten(total[2 * blocks + block, some, :])
            stash[(2 + u) * blocks + block, some, :] = normal.astype(low)
            spreads[pl.ds(u * unit + across.start, size), 0:1] = spread
            middle = stash[u * blocks + block, some, :].astype(f32)
            middle = (middle + (normal * gain(0, 1) + bias(0, 1))).astype(low)
            kept[0, u, block, some, :] = middle
            stash[4 * blocks + block, some, :] = normed_input(1, middle.astype(f32))

        by_rows(norm_out)

    def feed_forward(u):
        span = slice(u * unit, (u + 1) * unit)
        lhs[2, :, span] = stash_read(4).T
        def norm_out(block, some, across):
            normal, spread = whiten(total[2 * blocks + block, some, :])
            stash[(5 + u) * blocks + block, some, :] = normal.astype(low)
            spreads[pl.ds(u * unit + across.start, size), 1:2] = spread
            middle = kept[0, u, block, some, :].astype(f32)
            output = middle + (normal * gain(1, 1) + bias(1, 1))
            kept[1, u, block, some, :] = output.astype(low)

        def whole():
            for i in range(4):
                c = lax.rem(2 * core + i, 4) if u == 0 else i
                if u == 0:
                    await_feed(i)
                hidden, slope = gelu_both(dot(stash_read(4), weight(4 + c)))
                hidden = hidden.astype(low)
                rhs[4 + c, span, :] = slope.astype(low)
                hidden_t[pl.ds(pl.multiple_of(c * width, width), width), span] = hidden.T
                if u == 0:
                    await_down(i)
                add_branch(dot(hidden, weight(8 + c)), i == 0)
            for half in range(2):
                by_rows(norm_out, half)
                send_part(early, u, half)

        def by_halves():
            part_blocks, part_rows = blocks // 2, unit // 2
            for half in range(2):
                some = slice(u * unit + half * part_rows, u * unit + (half + 1) * part_rows)
                sum_at = pl.ds(2 * blocks + half * part_blocks, part_blocks)
                normed = stash[pl.ds(4 * blocks + half * part_blocks, part_blocks)]
                normed = normed.reshape(part_rows, width)
                for c in range(4):
                    hidden, slope = gelu_both(dot(normed, weight(4 + c)))
                    hidden = hidden.astype(low)
                    rhs[4 + c, some, :] = slope.astype(low)
                    hidden_t[c * width : (c + 1) * width, some] = hidden.T
                    term = dot(hidden, weight(8 + c)).reshape(part_blocks, rows, width)
                    total[sum_at] = term if c == 0 else total[sum_at] + term
                by_rows(norm_out, half)
                hop_copy(u, half).start()

        if u == 0:
            whole()
        else:
            pl.when(early)(by_halves)
            pl.when(late)(whole)

    def feed_backward(u):
        span = slice(u * unit, (u + 1) * unit)

        def back_out(block, some, across):
            own = pl.ds(u * unit + across.start, size)
            upstream = sends[(6 + u) * blocks + block, some, :].astype(f32)
            normal = stash[(5 + u) * blocks + block, some, :].astype(f32)
            add_sums(1, 1, upstream, normal)
            dz = whiten_back(upstream * gain(1, 1), normal, spreads[own, 1:2])
            dz_down[own, :] = dz.astype(low)

        for half in range(2):
            await_grad(u, half)
            by_rows(back_out, half)
        for c in range(4):
            d_hidden = dot_cols(dz_down[span, :], weight(8 + c))
            d_pre = (d_hidden * rhs[4 + c, span, :].astype(f32)).astype(low)
            rhs[4 + c, span, :] = d_pre
            add_branch(dot_cols(d_pre, weight(4 + c)), c == 0)

        def back_in(block, some, across):
            own = pl.ds(u * unit + across.start, size)
            normal, spread = whiten(kept[0, u, block, some, :].astype(f32))
            d_normed = total[2 * blocks + block, some, :]
            add_sums(1, 0, d_normed, normal)
            d_ln = whiten_back(d_normed * gain(1, 0), normal, spread)
            d_middle = (sends[(6 + u) * blocks + block, some, :].astype(f32) + d_ln).astype(low)
            kept[0, u, block, some, :] = d_middle
            upstream = d_middle.astype(f32)
            normal = stash[(2 + u) * blocks + block, some, :].astype(f32)
            add_sums(0, 1, upstream, normal)
            dz = whiten_back(upstream * gain(0, 1), normal, spreads[own, 0:1])
            stash[4 * blocks + block, some, :] = dz.astype(low)

        outputs_sent(u)
        if u == 0:
            for other in (left, right):
                pl.semaphore_signal(
                    ready, inc=1, device_id=(other, section), device_id_type=MESH
                )
            pl.semaphore_signal(ready, inc=1, device_id=(dp, peer), device_id_type=MESH)
        by_rows(back_in)

    def attention_backward(u):
        span = slice(u * unit, (u + 1) * unit)
        keys = (u + 1) * unit
        lhs[1, :, span] = stash_read(4).T
        d_context = dot(stash_read(4), weight(3)).astype(low)
        stash_write(4, d_context)
        product = (d_context.astype(f32) * rhs[3, span, :].astype(f32)).astype(low)
        head = lax.broadcasted_iota(jnp.int32, (HEADS, width), 0)
        column = lax.broadcasted_iota(jnp.int32, (HEADS, width), 1)
        inside = (column >= head * HEAD) & (column < (head + 1) * HEAD)
        delta_t[...] = dot_cols(jnp.where(inside, 1.0, 0.0).astype(low), product)
        mask[:keys, :] = mask_of((keys, unit), 1, u * unit, 0)

        def pair(p, carry):
            lanes = pair_lanes(p)
            query = projected(0, lanes, u).astype(f32)
            key = projected(1, lanes, 0, u + 1)
            value = projected(2, lanes, 0, u + 1)
            d_out = stash[pl.ds(4 * blocks, blocks), :, lanes].reshape(unit, LANES).astype(f32)
            key_t = key.T
            heads = range(2)
            query_both = [(query * half_lanes(h, score_scale)).astype(low) for h in heads]
            query_both = jnp.concatenate(query_both, axis=0)
            d_out_both = [(d_out * half_lanes(h, 1.0)).astype(low) for h in heads]
            d_out_both = jnp.concatenate(d_out_both, axis=0)
            logs = jnp.concatenate([log_t[u, pl.ds(2 * p + h, 1), :] for h in heads], axis=1)
            delta = jnp.concatenate([delta_t[pl.ds(2 * p + h, 1), :] for h in heads], axis=1)
            added = mask[:keys, :]
            scores = dot_cols(key, query_both) + jnp.concatenate([added, added], axis=1)
            prob = jnp.exp(scores - logs)
            d_prob = dot_cols(value, d_out_both)
            d_scores = (prob * (d_prob - delta)).astype(low)
            d_value = dot(prob.astype(low), d_out_both)
            d_key = dot(d_scores, query_both)
            d_query = [
                dot(key_t[h * HEAD : (h + 1) * HEAD, :], d_scores[:, h * unit : (h + 1) * unit])
                for h in heads
            ]
            d_query = jnp.concatenate(d_query, axis=0) * score_scale
            rhs[0, span, lanes] = d_query.T.astype(low)
            for i, grad in ((0, d_key), (1, d_value)):
                carried = pl.ds(i * blocks, blocks)
                if u == 1:
                    rhs[1 + i, span, lanes] = grad[unit:].astype(low)
                    total[carried, :, lanes] = grad[:unit].reshape(blocks, rows, LANES)
                else:
                    grad = grad + total[carried, :, lanes].reshape(unit, LANES)
                    rhs[1 + i, span, lanes] = grad.astype(low)
            return carry

        lax.fori_loop(0, PAIRS, pair, 0, unroll=4)
        for part in range(3):
            add_branch(dot_cols(rhs[part, span, :], weight(part)), part == 0)

        def back_in(block, some, across):
            normal, spread = whiten(stash[u * blocks + block, some, :].astype(f32))
            d_normed = total[2 * blocks + block, some, :]
            add_sums(0, 0, d_normed, normal)
            d_ln = whiten_back(d_normed * gain(0, 0), normal, spread)
            d_input = kept[0, u, block, some, :].astype(f32) + d_ln
            kept[1, u, block, some, :] = d_input.astype(low)

        for half in range(2):
            by_rows(back_in, half)
            send_part(late, 2 + u, half)

    def pair_block(step, stream=0):
        return jnp.where(step == 0, 6 * count, 6 * (step - 1)) + stream

    def ring_block(step, stream):
        return 12 * count - 6 * (step + 1) + stream

    def pair_slot(step):
        return jnp.where(lax.rem(step, 2) == 0, 5 * blocks, 0)

    def ring_slot(step):
        return jnp.where(lax.rem(step, 2) == 0, 6 * blocks, 0)

    def pair_copy(step):
        return to_peer(
            stash.at[pl.ds(pair_slot(step), 6)],
            pool.at[pl.ds(pair_block(step), 6)],
            pair_ss.at[lax.rem(step, 2)],
            pair_rs.at[step],
        )

    def pair_first(stream):
        return to_peer(
            stash.at[5 * blocks + stream],
            pool.at[6 * count + stream],
            first_ss.at[stream],
            first_rs.at[stream],
        )

    def ring_copy(step, stream):
        return pltpu.make_async_remote_copy(
            src_ref=sends.at[ring_slot(step) + stream],
            dst_ref=pool.at[ring_block(step, stream)],
            send_sem=ring_ss.at[lax.rem(step, 2), stream],
            recv_sem=ring_rs.at[step, stream],
            device_id=(jnp.where(stream < 3, right, left), section),
            device_id_type=MESH,
        )

    def ring_row(step, stream):
        behind = lax.rem(place + 2 * count - 1 - step, count)
        ahead = lax.rem(place + 1 + step, count)
        return ring_index(jnp.where(stream < 3, behind, ahead), count)

    def stream_of(group):
        return group + group // 2

    def product(step, group, part):
        block = ring_row(step, stream_of(group))
        side = jnp.where(part == 1, 2, jnp.where(group == 3, 1, 0))
        piece = lhs[side, pl.ds(pl.multiple_of(block * rows, rows), rows), :]
        return dot(piece, rhs[part * 4 + group])

    def down_product(step, turn, part):
        block = ring_row(step, 2 + 3 * turn)
        start = part * (2 * width) + block * (2 * rows) + turn * rows
        return dot(hidden_t[pl.ds(pl.multiple_of(start, rows), rows), :], dz_down[...])

    def each(count_of, action):
        def step(i, carry):
            action(i)
            return carry

        lax.fori_loop(0, count_of, step, 0)

    def pair_part(step):
        slot = pair_slot(step)

        def group_part(group):
            value = product(step, group, 1 - core)
            stash[slot + stream_of(group)] = value.astype(low)

        def down_part(turn):
            stash[slot + 2 + 3 * turn] = down_product(step, turn, 1 - core).astype(low)

        each(4, group_part)
        each(2, down_part)

    def own_part(step):
        def group_part(group):
            total[stream_of(group)] = product(step, group, core)

        def down_part(turn):
            total[2 + 3 * turn] = down_product(step, turn, core)

        each(4, group_part)
        each(2, down_part)

    def turn_about(i):
        return i // 2 + 2 * lax.rem(i, 2)

    def first_pair_group(i):
        group = turn_about(i)
        stream = stream_of(group)
        stash[5 * blocks + stream] = product(0, group, 1 - core).astype(low)
        pair_first(stream).start()

    def first_pair_down(turn):
        stash[5 * blocks + 2 + 3 * turn] = down_product(0, turn, 1 - core).astype(low)

    def first_own_group(group):
        stream = stream_of(group)
        sends[6 * blocks + stream] = product(0, group, core).astype(low)

    def first_own_down(turn):
        sends[6 * blocks + 2 + 3 * turn] = down_product(0, turn, core).astype(low)

    def first_ring_group(i):
        first_ring(stream_of(turn_about(i)))

    def first_ring(stream):
        pair_first(stream).wait_recv()
        value = sends[6 * blocks + stream].astype(f32) + pool[6 * count + stream].astype(f32)
        sends[6 * blocks + stream] = value.astype(low)
        ring_copy(0, stream).start()

    def feed_first():
        each(2, first_pair_down)
        pl.semaphore_wait(ready, 3)
        each(2, lambda turn: pair_first(2 + 3 * turn).start())
        each(2, first_own_down)

        @pl.when(core == 0)
        def _():
            each(4, first_pair_group)

        @pl.when(core == 1)
        def _():
            each(4, first_own_group)

        each(2, lambda turn: first_ring(2 + 3 * turn))

        @pl.when(core == 1)
        def _():
            each(4, first_ring_group)

    for u in range(2):
        attention_forward(u)
        feed_forward(u)
        for copy in out_copies(0, u):
            copy.start()

    feed_backward(1)
    attention_backward(1)
    for copy in out_copies(1, 1):
        copy.start()
    feed_backward(0)

    def last_attention(turn):
        pl.when(turn == jnp.where(early, 0, 1))(feed_first)

        @pl.when(turn == 0)
        def _():
            attention_backward(0)

    each(2, last_attention)
    for copy in out_copies(1, 0):
        copy.start()
    for k in range(8):
        (weight_remote(k) if k < 6 else affine_remote(k - 6)).wait_send()
    pl.semaphore_signal(pair_ready, inc=1, device_id=(dp, peer), device_id_type=MESH)

    @pl.when(core == 1)
    def _():
        each(4, first_pair_group)

    @pl.when(core == 0)
    def _():
        each(4, first_own_group)
        each(4, first_ring_group)

    @pl.when(late)
    def _():
        for k in (2, 3):
            for half in range(2):
                hop_copy(k, half).wait_send()

    pair_part(1)
    pl.semaphore_wait(pair_ready, 1)
    pair_copy(1).start()
    own_part(1)

    slice_width = width // count
    for j in range(count):
        piece = sums[:, :, j * slice_width : (j + 1) * slice_width]
        small[j, :, :slice_width] = jnp.sum(piece, axis=1)

    gb_pair = to_peer(small, small_pair, small_sems.at[0], small_sems.at[1])

    def gb_copy(step):
        other = lax.rem(dp + step, count)
        return pltpu.make_async_remote_copy(
            src_ref=small_sum.at[other],
            dst_ref=small_recv.at[step],
            send_sem=small_ss.at[step],
            recv_sem=small_rs.at[step],
            device_id=(other, section),
            device_id_type=MESH,
        )

    gb_pair.start()
    gb_pair.wait()
    small_sum[...] = small[...] + small_pair[...]

    def gb_start(step, carry):
        gb_copy(step).start()
        return carry

    lax.fori_loop(1, count, gb_start, 0)

    for stream in range(6):
        pair_first(stream).wait_send()

    def ring_step(step, carry):
        pair_copy(step).wait_recv()

        def forward(i):
            turn = i // 2
            stream = 3 * lax.rem(i, 2) + jnp.where(turn == 0, 2, turn - 1)
            ring_copy(step - 1, stream).wait_recv()
            value = total[stream] + pool[pair_block(step, stream)].astype(f32)
            value = value + pool[ring_block(step - 1, stream)].astype(f32)

            @pl.when(step >= 2)
            def _():
                ring_copy(step - 2, stream).wait_send()

            sends[ring_slot(step) + stream] = value.astype(low)
            ring_copy(step, stream).start()

        each(6, forward)

        @pl.when(step >= 2)
        def _():
            pair_copy(step - 1).wait_send()

        pair_part(step + 1)
        pair_copy(step + 1).start()
        own_part(step + 1)
        return carry

    lax.fori_loop(1, count - 1, ring_step, 0)

    def grad_copy(stream):
        if stream % 3 < 2:
            group = stream % 3 + 2 * (stream // 3)
            target = first_grad.at[:, pl.ds(group * width, width)]
        else:
            target = down_grad.at[pl.ds((stream // 3) * rows, rows)]
        return pltpu.make_async_copy(total.at[stream], target, grad_ls.at[stream])

    last = count - 1
    pair_copy(last).wait_recv()
    for stream in (2, 5, 0, 3, 1, 4):
        total[stream] += pool[pair_block(last, stream)].astype(f32)
        ring_copy(last - 1, stream).wait_recv()
        total[stream] += pool[ring_block(last - 1, stream)].astype(f32)
        grad_copy(stream).start()

    small_out[...] = small_sum[dp]

    def gb_finish(step, carry):
        gb_copy(step).wait()
        small_out[...] += small_recv[step]
        return carry

    lax.fori_loop(1, count, gb_finish, 0)
    for stream in range(6):
        ring_copy(last - 1, stream).wait_send()
        ring_copy(last - 2, stream).wait_send()
        grad_copy(stream).wait()
    pair_copy(last).wait_send()
    pair_copy(last - 1).wait_send()
    for u in range(2):
        out_copies(0, u)[1].wait_recv()
        local_copy, remote_copy = out_copies(1, u)
        local_copy.wait()
        remote_copy.wait()


def layers(tokens, cotangent, lengths, first, down, gains, biases):
    count = lax.axis_size("dp")
    token_count, width = tokens.shape
    row_len = token_count // lengths.shape[0]
    unit = row_len // 2
    rows = width // count
    blocks = unit // rows
    vmem = pl.BlockSpec(memory_space=pltpu.VMEM)
    anywhere = pl.BlockSpec(memory_space=pl.ANY)
    sem = pltpu.SemaphoreType.DMA
    shape = jax.ShapeDtypeStruct
    buffer = pltpu.VMEM
    cut = (token_count // rows, rows, width)
    small = (count, 8, max(128, width // count))
    outs = pl.pallas_call(
        functools.partial(layers_kernel, count),
        out_shape=(
            shape(cut, low),
            shape(cut, low),
            shape((rows, 4 * width), f32),
            shape((2 * rows, width), f32),
            shape(small[1:], f32),
        ),
        in_specs=[anywhere, anywhere, pl.BlockSpec(memory_space=pltpu.SMEM)] + [anywhere] * 4,
        out_specs=(anywhere, anywhere, anywhere, anywhere, vmem),
        scratch_shapes=[
            buffer((12 * count, rows, width), low),
            buffer((8 * blocks + max(0, 6 - 2 * blocks), rows, width), low),
            buffer((7 * blocks + max(0, 6 - 2 * blocks), rows, width), low),
            buffer((row_len, 128), f32),
            buffer((2, 2, blocks, rows, width), low),
            buffer((row_len, unit), f32),
            buffer((max(6, 3 * blocks), rows, width), f32),
            buffer((3, width, row_len), low),
            buffer((4 * width, row_len), low),
            buffer((8, row_len, width), low),
            buffer((row_len, width), low),
            buffer((2, 2, 2, width), f32),
            buffer((2, HEADS, unit), f32),
            buffer((unit, LANES), f32),
            buffer((HEADS, unit), f32),
            buffer((8, 8, width), f32),
            buffer(small, f32),
            buffer(small, f32),
            buffer(small, f32),
            buffer(small, f32),
            sem((8,)),
            sem((8,)),
            sem((8,)),
            sem((4,)),
            sem((4, 2)),
            sem((4, 2)),
            sem((4,)),
            sem((4,)),
            sem((4,)),
            pltpu.SemaphoreType.REGULAR,
            pltpu.SemaphoreType.REGULAR,
            sem((6,)),
            sem((6,)),
            sem((2,)),
            sem((count,)),
            sem((2, 6)),
            sem((count - 1, 6)),
            sem((2,)),
            sem((count,)),
            sem((count,)),
            sem((6,)),
        ],
        compiler_params=pltpu.CompilerParams(
            collective_id=0, has_side_effects=True, vmem_limit_bytes=63 * 1024 * 1024
        ),
        name="layers",
    )(
        tokens.reshape(cut),
        cotangent.reshape(cut),
        lengths,
        first.reshape(count, rows, 4 * width),
        down.reshape(2 * count, rows, width),
        gains,
        biases,
    )
    return outs


def place_kernel(*refs):
    sources, small, targets, (gain_grad, bias_grad) = refs[:4], refs[4], refs[5:9], refs[9:11]
    buffers, (arrived, written) = refs[11:15], refs[15:]
    reads, writes = [], []
    for i, (source, target, buffer) in enumerate(zip(sources, targets, buffers)):
        reads.append(pltpu.make_async_copy(source, buffer, arrived.at[i]))
        writes.append(pltpu.make_async_copy(buffer, target.at[0], written.at[i]))
    for read in reads:
        read.start()
    feed = lax.axis_index("section") % 2 == 1
    width = gain_grad.shape[2]
    gain_grad[0] = jnp.where(feed, small[4:6, :width], small[0:2, :width])
    bias_grad[0] = jnp.where(feed, small[6:8, :width], small[2:4, :width])
    for read, write in zip(reads, writes):
        read.wait()
        write.start()
    for write in writes:
        write.wait()


def local(tokens, doc_lengths, first_weights, down_weights, norm_gains, norm_biases, cotangent):
    width = tokens.shape[1]
    outputs, input_grads, first_part, down_part, small = layers(
        tokens,
        cotangent,
        doc_lengths,
        first_weights[0],
        down_weights[0],
        norm_gains,
        norm_biases,
    )
    slice_width = width // lax.axis_size("dp")
    results = [outputs.reshape(tokens.shape), input_grads.reshape(tokens.shape)]
    results += [first_part, down_part]
    norm_part = jax.ShapeDtypeStruct((1, 2, slice_width), f32)
    anywhere = pl.BlockSpec(memory_space=pl.ANY)
    vmem = pl.BlockSpec(memory_space=pltpu.VMEM)
    return pl.pallas_call(
        place_kernel,
        out_shape=[jax.ShapeDtypeStruct((1,) + r.shape, r.dtype) for r in results]
        + [norm_part, norm_part],
        in_specs=[anywhere] * 4 + [vmem],
        out_specs=[anywhere] * 4 + [vmem] * 2,
        scratch_shapes=[pltpu.VMEM(r.shape, r.dtype) for r in results]
        + [pltpu.SemaphoreType.DMA((4,))] * 2,
        name="place",
    )(*results, small)


def solution(mesh):
    placed = (
        P("dp", None),
        P("dp", None),
        P("section", None, None),
        P("section", None, None),
        P("section", None, None),
        P("section", None, None),
        P("dp", None),
    )
    return jax.shard_map(
        local,
        mesh=mesh,
        in_specs=placed,
        out_specs=(
            P("section", "dp", None),
            P("section", "dp", None),
            P("section", "dp", None),
            P("section", "dp", None),
            P("section", None, "dp"),
            P("section", None, "dp"),
        ),
        check_vma=False,
    )
```

```python
import functools

import jax
import jax.numpy as jnp
from jax import lax
from jax.experimental import pallas as pl
from jax.experimental.pallas import tpu as pltpu
from jax.sharding import PartitionSpec as P

HEADS = 16
HEAD = 64
PAIRS = HEADS // 2
LANES = 2 * HEAD
eps = 1e-05
masked_value = -1e30
score_scale = HEAD ** (-0.5)
MESH = pl.DeviceIdType.MESH
low = jnp.bfloat16
f32 = jnp.float32
tanh_linear = (2.0 / 3.141592653589793) ** 0.5
tanh_cubic = tanh_linear * 0.044715


def ring_place(index, count):
    return jnp.where(index % 2 == 0, index // 2, count - 1 - index // 2)


def ring_index(place, count):
    return jnp.where(place < count // 2, 2 * place, 2 * (count - 1 - place) + 1)


def dot(left, right):
    return jnp.dot(left, right, preferred_element_type=f32)


def dot_cols(left, right):
    return lax.dot_general(left, right, (((1,), (1,)), ((), ())), preferred_element_type=f32)


def whiten(values):
    average = jnp.mean(values, axis=-1, keepdims=True)
    centered = values - average
    variance = jnp.mean(centered * centered, axis=-1, keepdims=True)
    spread = lax.rsqrt(variance + eps)
    return centered * spread, spread


def whiten_back(grad, normal, spread):
    first = jnp.mean(grad, axis=-1, keepdims=True)
    second = jnp.mean(grad * normal, axis=-1, keepdims=True)
    return spread * (grad - first - normal * second)


def gelu_both(u):
    square = u * u
    half = 0.5 + 0.5 * jnp.tanh(u * (tanh_linear + tanh_cubic * square))
    value = u * half
    slope = half + value * (1.0 - half) * (2.0 * tanh_linear + 6.0 * tanh_cubic * square)
    return value, slope


def layers_kernel(
    count,
    tokens,
    cotangent,
    lengths,
    first,
    down,
    gains,
    biases,
    outputs,
    input_grads,
    first_grad,
    down_grad,
    small_out,
    pool,
    sends,
    stash,
    spreads,
    kept,
    mask,
    total,
    lhs,
    hidden_t,
    rhs,
    dz_down,
    affine,
    log_t,
    log_rows,
    delta_t,
    sums,
    small,
    small_pair,
    small_sum,
    small_recv,
    weight_ls,
    weight_ss,
    weight_rs,
    row_ls,
    hop_ss,
    hop_rs,
    out_ls,
    out_ss,
    out_rs,
    ready,
    pair_ready,
    first_ss,
    first_rs,
    pair_ss,
    pair_rs,
    ring_ss,
    ring_rs,
    small_sems,
    small_ss,
    small_rs,
    grad_ls,
):
    rows, width = pool.shape[1:]
    row_len = rhs.shape[1]
    unit = row_len // 2
    blocks = unit // rows
    dp = lax.axis_index("dp")
    section = lax.axis_index("section")
    section_count = lax.axis_size("section")
    core = lax.rem(section, 2)
    peer = section + 1 - 2 * core
    early = section < 2
    late = section >= 2
    partner = lax.rem(section + 2, section_count)
    place = ring_place(dp, count)
    left = ring_index(lax.rem(place + count - 1, count), count)
    right = ring_index(lax.rem(place + 1, count), count)

    barrier = pltpu.get_barrier_semaphore()

    def greet(step, carry):
        other = lax.rem(dp + step, count)
        pl.semaphore_signal(barrier, inc=1, device_id=(other, section), device_id_type=MESH)
        return carry

    lax.fori_loop(1, count, greet, 0)
    for other in (peer, partner):
        pl.semaphore_signal(barrier, inc=1, device_id=(dp, other), device_id_type=MESH)

    def own_chunk(k):
        if k < 4:
            return first.at[:, :, pl.ds(k * width, width)], 4 * core + k
        return down.at[pl.ds((k - 4) * count, count)], 8 + 2 * core + k - 4

    def weight_local(k):
        source, chunk = own_chunk(k)
        target = pool.at[pl.ds(chunk * count, count)]
        return pltpu.make_async_copy(source, target, weight_ls.at[k])

    def to_peer(source, target, send_sem, recv_sem):
        return pltpu.make_async_remote_copy(
            src_ref=source,
            dst_ref=target,
            send_sem=send_sem,
            recv_sem=recv_sem,
            device_id=(dp, peer),
            device_id_type=MESH,
        )

    def weight_remote(k):
        source, chunk = own_chunk(k)
        target = pool.at[pl.ds(chunk * count, count)]
        return to_peer(source, target, weight_ss.at[k], weight_rs.at[k])

    def affine_local(i):
        source = (gains, biases)[i].at[0]
        return pltpu.make_async_copy(source, affine.at[core, i], weight_ls.at[6 + i])

    def affine_remote(i):
        source = (gains, biases)[i].at[0]
        return to_peer(source, affine.at[core, i], weight_ss.at[6 + i], weight_rs.at[6 + i])

    def await_chunk(chunk):
        owner = 1 if 4 <= chunk < 8 or chunk >= 10 else 0
        k = chunk % 4 if chunk < 8 else 4 + chunk % 2

        @pl.when(core == owner)
        def _():
            weight_local(k).wait()

        @pl.when(core != owner)
        def _():
            weight_remote(k).wait_recv()

    def await_feed(i):
        @pl.when(core == 0)
        def _():
            weight_remote(i).wait_recv()

        @pl.when(core == 1)
        def _():
            weight_local((i + 2) % 4).wait()

    def await_down(i):
        if i < 2:
            weight_local(4 + i).wait()
        else:
            weight_remote(2 + i).wait_recv()

    def weight(chunk):
        return pool[pl.ds(chunk * count, count)].reshape(width, width)

    def weight_cols(chunk, some):
        return pool[pl.ds(chunk * count, count), :, some].reshape(width, width // 2)

    def weight_rows(chunk, half):
        start = chunk * count + half * (count // 2)
        return pool[pl.ds(start, count // 2)].reshape(width // 2, width)

    def stash_at(place_in):
        return stash.at[pl.ds(place_in * blocks, blocks)]

    def stash_read(place_in):
        return stash[pl.ds(place_in * blocks, blocks)].reshape(unit, width)

    def stash_write(place_in, value):
        stash[pl.ds(place_in * blocks, blocks)] = value.astype(low).reshape(blocks, rows, width)

    def row_copy(u, source, target, sem):
        start = (core * 2 + u) * blocks
        return pltpu.make_async_copy(source.at[pl.ds(start, blocks)], target, sem)

    def token_copy(u):
        return row_copy(u, tokens, stash_at(u), row_ls.at[u])

    def cotangent_copy(u):
        return row_copy(u, cotangent, sends.at[pl.ds((6 + u) * blocks, blocks)], row_ls.at[2 + u])

    def hop_copy(k, part):
        u = k % 2
        some = pl.ds(part * (blocks // 2), blocks // 2)
        arriving = pl.ds(u * blocks + part * (blocks // 2), blocks // 2)
        grad_arriving = pl.ds((6 + u) * blocks + part * (blocks // 2), blocks // 2)
        return pltpu.make_async_remote_copy(
            src_ref=kept.at[1, u, some],
            dst_ref=stash.at[arriving] if k < 2 else sends.at[grad_arriving],
            send_sem=hop_ss.at[k, part],
            recv_sem=hop_rs.at[k, part],
            device_id=(dp, partner),
            device_id_type=MESH,
        )

    def out_copies(kind, u):
        target = (outputs, input_grads)[kind]
        place_out = target.at[pl.ds((core * 2 + u) * blocks, blocks)]
        k = 2 * kind + u
        own, other = (core, 1 - core) if kind == 0 else (1 - core, core)
        return (
            pltpu.make_async_copy(kept.at[own, u], place_out, out_ls.at[k]),
            to_peer(kept.at[other, u], place_out, out_ss.at[k], out_rs.at[k]),
        )

    def outputs_sent(u):
        local_copy, remote_copy = out_copies(0, u)
        local_copy.wait()
        remote_copy.wait_send()

        @pl.when(early)
        def _():
            for part in range(2):
                hop_copy(u, part).wait_send()

    for k in range(6):
        weight_local(k).start()
    for i in range(2):
        affine_local(i).start()

    @pl.when(early)
    def _():
        for u in range(2):
            token_copy(u).start()

    @pl.when(late)
    def _():
        for u in range(2):
            cotangent_copy(u).start()

    pl.semaphore_wait(barrier, count + 1)
    for i in range(2):
        affine_remote(i).start()
    for k in range(6):
        weight_remote(k).start()

    sums[...] = jnp.zeros_like(sums)
    log_rows[...] = jnp.zeros_like(log_rows)
    small[...] = jnp.zeros_like(small)
    for i in range(2):
        affine_local(i).wait()
        affine_remote(i).wait_recv()

    def gain(sub, which):
        return affine[sub, 0, which : which + 1, :]

    def bias(sub, which):
        return affine[sub, 1, which : which + 1, :]

    ends = [lengths[core, 0]]
    for j in range(1, lengths.shape[1]):
        ends.append(ends[-1] + lengths[core, j])

    def mask_of(shape, query_axis, first_query, first_key):
        query = lax.broadcasted_iota(jnp.int32, shape, query_axis) + first_query
        key = lax.broadcasted_iota(jnp.int32, shape, 1 - query_axis) + first_key
        apart = jnp.zeros(shape, jnp.int32)
        for end in ends:
            apart += (query >= end).astype(jnp.int32) - (key >= end).astype(jnp.int32)
        return jnp.where((apart == 0) & (key <= query), 0.0, masked_value)

    def projected(part, lanes, u=0, halves=1):
        span = pl.ds((2 * part + u) * blocks, halves * blocks)
        return sends[span, :, lanes].reshape(halves * unit, LANES)

    def half_lanes(h, scale):
        lane = lax.broadcasted_iota(jnp.int32, (1, LANES), 1)
        return jnp.where((lane >= h * HEAD) & (lane < (h + 1) * HEAD), scale, 0.0)

    def pair_lanes(p):
        return pl.ds(pl.multiple_of(p * LANES, LANES), LANES)

    def branch():
        return total[pl.ds(2 * blocks, blocks)].reshape(unit, width)

    def add_branch(term, begin):
        value = term if begin else branch() + term
        total[pl.ds(2 * blocks, blocks)] = value.reshape(blocks, rows, width)

    size = min(rows, 64)
    groups = rows // size

    def by_rows(body, part=None):
        def step(i, carry):
            block, start = i // groups, pl.multiple_of(lax.rem(i, groups) * size, size)
            body(block, pl.ds(start, size), pl.ds(pl.multiple_of(i * size, size), size))
            return carry

        half = unit // size // 2
        begin, end = (0, 2 * half) if part is None else (part * half, (part + 1) * half)
        lax.fori_loop(begin, end, step, 0, unroll=True)

    def add_sums(sub, which, grad, normal):
        row = 4 * sub + which
        sums[row] += jnp.sum((grad * normal).reshape(size // 8, 8, width), axis=0)
        sums[row + 2] += jnp.sum(grad.reshape(size // 8, 8, width), axis=0)

    def normed_input(sub, values):
        return (whiten(values)[0] * gain(sub, 0) + bias(sub, 0)).astype(low)

    def await_input(u, half):
        @pl.when(late)
        def _():
            hop_copy(u, half).wait_recv()

        if half == 0:

            @pl.when(early)
            def _():
                token_copy(u).wait()

    def await_grad(u, half):
        @pl.when(early)
        def _():
            hop_copy(2 + u, half).wait_recv()

        if half == 0:

            @pl.when(late)
            def _():
                cotangent_copy(u).wait()

    def send_part(stage, k, part):
        @pl.when(stage)
        def _():
            hop_copy(k, part).start()

    def attention_forward(u):
        span = slice(u * unit, (u + 1) * unit)

        def norm_in(block, some, _):
            values = stash[u * blocks + block, some, :].astype(f32)
            stash[4 * blocks + block, some, :] = normed_input(0, values)

        for i in range(u + 1):
            mask[i * unit : (i + 1) * unit, :] = mask_of((unit, unit), 0, u * unit, i * unit)

        def project_all(stage_weights):
            for part in range(3):
                if stage_weights:
                    await_chunk(part)
                value = dot(stash_read(4), weight(part)).astype(low)
                target = pl.ds((2 * part + u) * blocks, blocks)
                sends[target] = value.reshape(blocks, rows, width)

        if u == 1:
            for half in range(2):
                await_input(u, half)
                by_rows(norm_in, half)
            project_all(False)
        else:

            @pl.when(early)
            def _():
                token_copy(u).wait()
                by_rows(norm_in)
                project_all(True)

            @pl.when(late)
            def _():
                for part in range(3):
                    await_chunk(part)
                part_blocks = blocks // 2
                for half in range(2):
                    hop_copy(u, half).wait_recv()
                    by_rows(norm_in, half)
                    normed = stash[pl.ds(4 * blocks + half * part_blocks, part_blocks)]
                    normed = normed.reshape(unit // 2, width)
                    for part in range(3):
                        value = dot(normed, weight(part)).astype(low)
                        target = pl.ds(2 * part * blocks + half * part_blocks, part_blocks)
                        sends[target] = value.reshape(part_blocks, rows, width)

        lhs[0, :, span] = stash_read(4).T
        lane = lax.broadcasted_iota(jnp.int32, (unit, LANES), 1)

        def pair(p, carry):
            lanes = pair_lanes(p)
            query = projected(0, lanes, u).astype(f32)
            key = projected(1, lanes, 0, u + 1)
            value = projected(2, lanes, 0, u + 1)
            added = jnp.concatenate([mask[i * unit : (i + 1) * unit, :] for i in range(u + 1)], 1)
            both = [(query * half_lanes(h, score_scale)).astype(low) for h in range(2)]
            scores = dot_cols(jnp.concatenate(both, axis=0), key)
            scores = scores + jnp.concatenate([added, added], axis=0)
            top = jnp.max(scores, axis=-1, keepdims=True)
            exponent = jnp.exp(scores - top)
            summed = jnp.sum(exponent, axis=-1, keepdims=True)
            context = dot(exponent.astype(low), value) * (1.0 / summed)
            log_total = top + jnp.log(summed)
            logs = jnp.where(lane == 2 * p, log_total[:unit], log_rows[...])
            log_rows[...] = jnp.where(lane == 2 * p + 1, log_total[unit:], logs)
            context = jnp.where(lane < HEAD, context[:unit], context[unit:])
            rhs[3, span, lanes] = context.astype(low)
            return carry

        lax.fori_loop(0, PAIRS, pair, 0, unroll=4)
        log_t[u] = log_rows[...].T[:HEADS]
        if u == 0:
            await_chunk(3)
        add_branch(dot_cols(rhs[3, span, :], weight(3)), True)

        def norm_out(block, some, across):
            normal, spread = whiten(total[2 * blocks + block, some, :])
            stash[(2 + u) * blocks + block, some, :] = normal.astype(low)
            spreads[pl.ds(u * unit + across.start, size), 0:1] = spread
            middle = stash[u * blocks + block, some, :].astype(f32)
            middle = (middle + (normal * gain(0, 1) + bias(0, 1))).astype(low)
            kept[0, u, block, some, :] = middle
            stash[4 * blocks + block, some, :] = normed_input(1, middle.astype(f32))

        by_rows(norm_out)

    def feed_forward(u):
        span = slice(u * unit, (u + 1) * unit)
        lhs[2, :, span] = stash_read(4).T
        def norm_out(block, some, across):
            normal, spread = whiten(total[2 * blocks + block, some, :])
            stash[(5 + u) * blocks + block, some, :] = normal.astype(low)
            spreads[pl.ds(u * unit + across.start, size), 1:2] = spread
            middle = kept[0, u, block, some, :].astype(f32)
            output = middle + (normal * gain(1, 1) + bias(1, 1))
            kept[1, u, block, some, :] = output.astype(low)

        def whole():
            for i in range(4):
                c = lax.rem(2 * core + i, 4) if u == 0 else i
                if u == 0:
                    await_feed(i)
                hidden, slope = gelu_both(dot(stash_read(4), weight(4 + c)))
                hidden = hidden.astype(low)
                rhs[4 + c, span, :] = slope.astype(low)
                hidden_t[pl.ds(pl.multiple_of(c * width, width), width), span] = hidden.T
                if u == 0:
                    await_down(i)
                add_branch(dot(hidden, weight(8 + c)), i == 0)
            for half in range(2):
                by_rows(norm_out, half)
                send_part(early, u, half)

        def by_halves():
            part_blocks, part_rows = blocks // 2, unit // 2
            for half in range(2):
                some = slice(u * unit + half * part_rows, u * unit + (half + 1) * part_rows)
                sum_at = pl.ds(2 * blocks + half * part_blocks, part_blocks)
                normed = stash[pl.ds(4 * blocks + half * part_blocks, part_blocks)]
                normed = normed.reshape(part_rows, width)
                for c in range(4):
                    hidden, slope = gelu_both(dot(normed, weight(4 + c)))
                    hidden = hidden.astype(low)
                    rhs[4 + c, some, :] = slope.astype(low)
                    hidden_t[c * width : (c + 1) * width, some] = hidden.T
                    term = dot(hidden, weight(8 + c)).reshape(part_blocks, rows, width)
                    total[sum_at] = term if c == 0 else total[sum_at] + term
                by_rows(norm_out, half)
                hop_copy(u, half).start()

        if u == 0:
            whole()
        else:
            pl.when(early)(by_halves)
            pl.when(late)(whole)

    def feed_backward(u):
        span = slice(u * unit, (u + 1) * unit)

        def back_out(block, some, across):
            own = pl.ds(u * unit + across.start, size)
            upstream = sends[(6 + u) * blocks + block, some, :].astype(f32)
            normal = stash[(5 + u) * blocks + block, some, :].astype(f32)
            add_sums(1, 1, upstream, normal)
            dz = whiten_back(upstream * gain(1, 1), normal, spreads[own, 1:2])
            dz_down[own, :] = dz.astype(low)

        for half in range(2):
            await_grad(u, half)
            by_rows(back_out, half)
        for c in range(4):
            d_hidden = dot_cols(dz_down[span, :], weight(8 + c))
            d_pre = (d_hidden * rhs[4 + c, span, :].astype(f32)).astype(low)
            rhs[4 + c, span, :] = d_pre
            add_branch(dot_cols(d_pre, weight(4 + c)), c == 0)

        def back_in(block, some, across):
            own = pl.ds(u * unit + across.start, size)
            normal, spread = whiten(kept[0, u, block, some, :].astype(f32))
            d_normed = total[2 * blocks + block, some, :]
            add_sums(1, 0, d_normed, normal)
            d_ln = whiten_back(d_normed * gain(1, 0), normal, spread)
            d_middle = (sends[(6 + u) * blocks + block, some, :].astype(f32) + d_ln).astype(low)
            kept[0, u, block, some, :] = d_middle
            upstream = d_middle.astype(f32)
            normal = stash[(2 + u) * blocks + block, some, :].astype(f32)
            add_sums(0, 1, upstream, normal)
            dz = whiten_back(upstream * gain(0, 1), normal, spreads[own, 0:1])
            stash[4 * blocks + block, some, :] = dz.astype(low)

        outputs_sent(u)
        if u == 0:
            for other in (left, right):
                pl.semaphore_signal(
                    ready, inc=1, device_id=(other, section), device_id_type=MESH
                )
            pl.semaphore_signal(ready, inc=1, device_id=(dp, peer), device_id_type=MESH)
            pl.when(early)(down_first)
        by_rows(back_in)

    def attention_backward(u):
        span = slice(u * unit, (u + 1) * unit)
        keys = (u + 1) * unit
        lhs[1, :, span] = stash_read(4).T
        d_context = dot(stash_read(4), weight(3)).astype(low)
        stash_write(4, d_context)
        product = (d_context.astype(f32) * rhs[3, span, :].astype(f32)).astype(low)
        head = lax.broadcasted_iota(jnp.int32, (HEADS, width), 0)
        column = lax.broadcasted_iota(jnp.int32, (HEADS, width), 1)
        inside = (column >= head * HEAD) & (column < (head + 1) * HEAD)
        delta_t[...] = dot_cols(jnp.where(inside, 1.0, 0.0).astype(low), product)
        mask[:keys, :] = mask_of((keys, unit), 1, u * unit, 0)

        def pair(p, carry):
            lanes = pair_lanes(p)
            query = projected(0, lanes, u).astype(f32)
            key = projected(1, lanes, 0, u + 1)
            value = projected(2, lanes, 0, u + 1)
            d_out = stash[pl.ds(4 * blocks, blocks), :, lanes].reshape(unit, LANES).astype(f32)
            key_t = key.T
            heads = range(2)
            query_both = [(query * half_lanes(h, score_scale)).astype(low) for h in heads]
            query_both = jnp.concatenate(query_both, axis=0)
            d_out_both = [(d_out * half_lanes(h, 1.0)).astype(low) for h in heads]
            d_out_both = jnp.concatenate(d_out_both, axis=0)
            logs = jnp.concatenate([log_t[u, pl.ds(2 * p + h, 1), :] for h in heads], axis=1)
            delta = jnp.concatenate([delta_t[pl.ds(2 * p + h, 1), :] for h in heads], axis=1)
            added = mask[:keys, :]
            scores = dot_cols(key, query_both) + jnp.concatenate([added, added], axis=1)
            prob = jnp.exp(scores - logs)
            d_prob = dot_cols(value, d_out_both)
            d_scores = (prob * (d_prob - delta)).astype(low)
            d_value = dot(prob.astype(low), d_out_both)
            d_key = dot(d_scores, query_both)
            d_query = [
                dot(key_t[h * HEAD : (h + 1) * HEAD, :], d_scores[:, h * unit : (h + 1) * unit])
                for h in heads
            ]
            d_query = jnp.concatenate(d_query, axis=0) * score_scale
            rhs[0, span, lanes] = d_query.T.astype(low)
            for i, grad in ((0, d_key), (1, d_value)):
                carried = pl.ds(i * blocks, blocks)
                if u == 1:
                    rhs[1 + i, span, lanes] = grad[unit:].astype(low)
                    total[carried, :, lanes] = grad[:unit].reshape(blocks, rows, LANES)
                else:
                    grad = grad + total[carried, :, lanes].reshape(unit, LANES)
                    rhs[1 + i, span, lanes] = grad.astype(low)
            return carry

        lax.fori_loop(0, PAIRS, pair, 0, unroll=4)
        for part in range(3):
            add_branch(dot_cols(rhs[part, span, :], weight(part)), part == 0)

        def back_in(block, some, across):
            normal, spread = whiten(stash[u * blocks + block, some, :].astype(f32))
            d_normed = total[2 * blocks + block, some, :]
            add_sums(0, 0, d_normed, normal)
            d_ln = whiten_back(d_normed * gain(0, 0), normal, spread)
            d_input = kept[0, u, block, some, :].astype(f32) + d_ln
            kept[1, u, block, some, :] = d_input.astype(low)

        for half in range(2):
            by_rows(back_in, half)
            send_part(late, 2 + u, half)

    def pair_block(step, stream=0):
        return jnp.where(step == 0, 6 * count, 6 * (step - 1)) + stream

    def ring_block(step, stream):
        return 12 * count - 6 * (step + 1) + stream

    def pair_slot(step):
        return jnp.where(lax.rem(step, 2) == 0, 5 * blocks, 0)

    def ring_slot(step):
        return jnp.where(lax.rem(step, 2) == 0, 6 * blocks, 0)

    def pair_copy(step):
        return to_peer(
            stash.at[pl.ds(pair_slot(step), 6)],
            pool.at[pl.ds(pair_block(step), 6)],
            pair_ss.at[lax.rem(step, 2)],
            pair_rs.at[step],
        )

    def pair_first(stream):
        return to_peer(
            stash.at[5 * blocks + stream],
            pool.at[6 * count + stream],
            first_ss.at[stream],
            first_rs.at[stream],
        )

    def ring_copy(step, stream):
        return pltpu.make_async_remote_copy(
            src_ref=sends.at[ring_slot(step) + stream],
            dst_ref=pool.at[ring_block(step, stream)],
            send_sem=ring_ss.at[lax.rem(step, 2), stream],
            recv_sem=ring_rs.at[step, stream],
            device_id=(jnp.where(stream < 3, right, left), section),
            device_id_type=MESH,
        )

    def ring_row(step, stream):
        behind = lax.rem(place + 2 * count - 1 - step, count)
        ahead = lax.rem(place + 1 + step, count)
        return ring_index(jnp.where(stream < 3, behind, ahead), count)

    def stream_of(group):
        return group + group // 2

    def product(step, group, part):
        block = ring_row(step, stream_of(group))
        side = jnp.where(part == 1, 2, jnp.where(group == 3, 1, 0))
        piece = lhs[side, pl.ds(pl.multiple_of(block * rows, rows), rows), :]
        return dot(piece, rhs[part * 4 + group])

    def down_product(step, turn, part):
        block = ring_row(step, 2 + 3 * turn)
        start = part * (2 * width) + block * (2 * rows) + turn * rows
        return dot(hidden_t[pl.ds(pl.multiple_of(start, rows), rows), :], dz_down[...])

    def each(count_of, action):
        def step(i, carry):
            action(i)
            return carry

        lax.fori_loop(0, count_of, step, 0)

    def pair_part(step):
        slot = pair_slot(step)

        def group_part(group):
            value = product(step, group, 1 - core)
            stash[slot + stream_of(group)] = value.astype(low)

        def down_part(turn):
            stash[slot + 2 + 3 * turn] = down_product(step, turn, 1 - core).astype(low)

        each(4, group_part)
        each(2, down_part)

    def own_part(step):
        def group_part(group):
            total[stream_of(group)] = product(step, group, core)

        def down_part(turn):
            total[2 + 3 * turn] = down_product(step, turn, core)

        each(4, group_part)
        each(2, down_part)

    def turn_about(i):
        return i // 2 + 2 * lax.rem(i, 2)

    def first_pair_group(i):
        group = turn_about(i)
        stream = stream_of(group)
        stash[5 * blocks + stream] = product(0, group, 1 - core).astype(low)
        pair_first(stream).start()

    def first_pair_down(turn):
        stash[5 * blocks + 2 + 3 * turn] = down_product(0, turn, 1 - core).astype(low)

    def first_own_group(group):
        stream = stream_of(group)
        sends[6 * blocks + stream] = product(0, group, core).astype(low)

    def first_own_down(turn):
        sends[6 * blocks + 2 + 3 * turn] = down_product(0, turn, core).astype(low)

    def first_ring_group(i):
        first_ring(stream_of(turn_about(i)))

    def first_ring(stream):
        pair_first(stream).wait_recv()
        value = sends[6 * blocks + stream].astype(f32) + pool[6 * count + stream].astype(f32)
        sends[6 * blocks + stream] = value.astype(low)
        ring_copy(0, stream).start()

    def down_first():
        each(2, first_pair_down)
        each(2, first_own_down)
        pl.semaphore_wait(ready, 3)
        each(2, lambda turn: pair_first(2 + 3 * turn).start())

    def feed_first():
        pl.when(late)(down_first)
        each(2, lambda turn: first_ring(2 + 3 * turn))

        @pl.when(core == 0)
        def _():
            each(4, first_pair_group)

        @pl.when(core == 1)
        def _():
            each(4, first_own_group)
            each(4, first_ring_group)

    for u in range(2):
        attention_forward(u)
        feed_forward(u)
        for copy in out_copies(0, u):
            copy.start()

    feed_backward(1)
    attention_backward(1)
    for copy in out_copies(1, 1):
        copy.start()
    feed_backward(0)

    def last_attention(turn):
        pl.when(turn == jnp.where(early, 0, 1))(feed_first)

        @pl.when(turn == 0)
        def _():
            attention_backward(0)

    each(2, last_attention)
    for copy in out_copies(1, 0):
        copy.start()
    for k in range(8):
        (weight_remote(k) if k < 6 else affine_remote(k - 6)).wait_send()
    pl.semaphore_signal(pair_ready, inc=1, device_id=(dp, peer), device_id_type=MESH)

    @pl.when(core == 1)
    def _():
        each(4, first_pair_group)

    @pl.when(core == 0)
    def _():
        each(4, first_own_group)
        each(4, first_ring_group)

    @pl.when(late)
    def _():
        for k in (2, 3):
            for half in range(2):
                hop_copy(k, half).wait_send()

    pair_part(1)
    pl.semaphore_wait(pair_ready, 1)
    pair_copy(1).start()
    own_part(1)

    slice_width = width // count
    for j in range(count):
        piece = sums[:, :, j * slice_width : (j + 1) * slice_width]
        small[j, :, :slice_width] = jnp.sum(piece, axis=1)

    gb_pair = to_peer(small, small_pair, small_sems.at[0], small_sems.at[1])

    def gb_copy(step):
        other = lax.rem(dp + step, count)
        return pltpu.make_async_remote_copy(
            src_ref=small_sum.at[other],
            dst_ref=small_recv.at[step],
            send_sem=small_ss.at[step],
            recv_sem=small_rs.at[step],
            device_id=(other, section),
            device_id_type=MESH,
        )

    gb_pair.start()
    gb_pair.wait()
    small_sum[...] = small[...] + small_pair[...]

    def gb_start(step, carry):
        gb_copy(step).start()
        return carry

    lax.fori_loop(1, count, gb_start, 0)

    for stream in range(6):
        pair_first(stream).wait_send()

    def ring_step(step, carry):
        pair_copy(step).wait_recv()

        def forward(i):
            turn = i // 2
            stream = 3 * lax.rem(i, 2) + jnp.where(turn == 0, 2, turn - 1)
            ring_copy(step - 1, stream).wait_recv()
            value = total[stream] + pool[pair_block(step, stream)].astype(f32)
            value = value + pool[ring_block(step - 1, stream)].astype(f32)

            @pl.when(step >= 2)
            def _():
                ring_copy(step - 2, stream).wait_send()

            sends[ring_slot(step) + stream] = value.astype(low)
            ring_copy(step, stream).start()

        each(6, forward)

        @pl.when(step >= 2)
        def _():
            pair_copy(step - 1).wait_send()

        pair_part(step + 1)
        pair_copy(step + 1).start()
        own_part(step + 1)
        return carry

    lax.fori_loop(1, count - 1, ring_step, 0)

    def grad_copy(stream):
        if stream % 3 < 2:
            group = stream % 3 + 2 * (stream // 3)
            target = first_grad.at[:, pl.ds(group * width, width)]
        else:
            target = down_grad.at[pl.ds((stream // 3) * rows, rows)]
        return pltpu.make_async_copy(total.at[stream], target, grad_ls.at[stream])

    last = count - 1
    pair_copy(last).wait_recv()
    for stream in (2, 5, 0, 3, 1, 4):
        total[stream] += pool[pair_block(last, stream)].astype(f32)
        ring_copy(last - 1, stream).wait_recv()
        total[stream] += pool[ring_block(last - 1, stream)].astype(f32)
        grad_copy(stream).start()

    small_out[...] = small_sum[dp]

    def gb_finish(step, carry):
        gb_copy(step).wait()
        small_out[...] += small_recv[step]
        return carry

    lax.fori_loop(1, count, gb_finish, 0)
    for stream in range(6):
        ring_copy(last - 1, stream).wait_send()
        ring_copy(last - 2, stream).wait_send()
        grad_copy(stream).wait()
    pair_copy(last).wait_send()
    pair_copy(last - 1).wait_send()
    for u in range(2):
        out_copies(0, u)[1].wait_recv()
        local_copy, remote_copy = out_copies(1, u)
        local_copy.wait()
        remote_copy.wait()


def layers(tokens, cotangent, lengths, first, down, gains, biases):
    count = lax.axis_size("dp")
    token_count, width = tokens.shape
    row_len = token_count // lengths.shape[0]
    unit = row_len // 2
    rows = width // count
    blocks = unit // rows
    vmem = pl.BlockSpec(memory_space=pltpu.VMEM)
    anywhere = pl.BlockSpec(memory_space=pl.ANY)
    sem = pltpu.SemaphoreType.DMA
    shape = jax.ShapeDtypeStruct
    buffer = pltpu.VMEM
    cut = (token_count // rows, rows, width)
    small = (count, 8, max(128, width // count))
    outs = pl.pallas_call(
        functools.partial(layers_kernel, count),
        out_shape=(
            shape(cut, low),
            shape(cut, low),
            shape((rows, 4 * width), f32),
            shape((2 * rows, width), f32),
            shape(small[1:], f32),
        ),
        in_specs=[anywhere, anywhere, pl.BlockSpec(memory_space=pltpu.SMEM)] + [anywhere] * 4,
        out_specs=(anywhere, anywhere, anywhere, anywhere, vmem),
        scratch_shapes=[
            buffer((12 * count, rows, width), low),
            buffer((8 * blocks + max(0, 6 - 2 * blocks), rows, width), low),
            buffer((7 * blocks + max(0, 6 - 2 * blocks), rows, width), low),
            buffer((row_len, 128), f32),
            buffer((2, 2, blocks, rows, width), low),
            buffer((row_len, unit), f32),
            buffer((max(6, 3 * blocks), rows, width), f32),
            buffer((3, width, row_len), low),
            buffer((4 * width, row_len), low),
            buffer((8, row_len, width), low),
            buffer((row_len, width), low),
            buffer((2, 2, 2, width), f32),
            buffer((2, HEADS, unit), f32),
            buffer((unit, LANES), f32),
            buffer((HEADS, unit), f32),
            buffer((8, 8, width), f32),
            buffer(small, f32),
            buffer(small, f32),
            buffer(small, f32),
            buffer(small, f32),
            sem((8,)),
            sem((8,)),
            sem((8,)),
            sem((4,)),
            sem((4, 2)),
            sem((4, 2)),
            sem((4,)),
            sem((4,)),
            sem((4,)),
            pltpu.SemaphoreType.REGULAR,
            pltpu.SemaphoreType.REGULAR,
            sem((6,)),
            sem((6,)),
            sem((2,)),
            sem((count,)),
            sem((2, 6)),
            sem((count - 1, 6)),
            sem((2,)),
            sem((count,)),
            sem((count,)),
            sem((6,)),
        ],
        compiler_params=pltpu.CompilerParams(
            collective_id=0, has_side_effects=True, vmem_limit_bytes=63 * 1024 * 1024
        ),
        name="layers",
    )(
        tokens.reshape(cut),
        cotangent.reshape(cut),
        lengths,
        first.reshape(count, rows, 4 * width),
        down.reshape(2 * count, rows, width),
        gains,
        biases,
    )
    return outs


def place_kernel(*refs):
    sources, small, targets, (gain_grad, bias_grad) = refs[:4], refs[4], refs[5:9], refs[9:11]
    buffers, (arrived, written) = refs[11:15], refs[15:]
    reads, writes = [], []
    for i, (source, target, buffer) in enumerate(zip(sources, targets, buffers)):
        reads.append(pltpu.make_async_copy(source, buffer, arrived.at[i]))
        writes.append(pltpu.make_async_copy(buffer, target.at[0], written.at[i]))
    for read in reads:
        read.start()
    feed = lax.axis_index("section") % 2 == 1
    width = gain_grad.shape[2]
    gain_grad[0] = jnp.where(feed, small[4:6, :width], small[0:2, :width])
    bias_grad[0] = jnp.where(feed, small[6:8, :width], small[2:4, :width])
    for read, write in zip(reads, writes):
        read.wait()
        write.start()
    for write in writes:
        write.wait()


def local(tokens, doc_lengths, first_weights, down_weights, norm_gains, norm_biases, cotangent):
    width = tokens.shape[1]
    outputs, input_grads, first_part, down_part, small = layers(
        tokens,
        cotangent,
        doc_lengths,
        first_weights[0],
        down_weights[0],
        norm_gains,
        norm_biases,
    )
    slice_width = width // lax.axis_size("dp")
    results = [outputs.reshape(tokens.shape), input_grads.reshape(tokens.shape)]
    results += [first_part, down_part]
    norm_part = jax.ShapeDtypeStruct((1, 2, slice_width), f32)
    anywhere = pl.BlockSpec(memory_space=pl.ANY)
    vmem = pl.BlockSpec(memory_space=pltpu.VMEM)
    return pl.pallas_call(
        place_kernel,
        out_shape=[jax.ShapeDtypeStruct((1,) + r.shape, r.dtype) for r in results]
        + [norm_part, norm_part],
        in_specs=[anywhere] * 4 + [vmem],
        out_specs=[anywhere] * 4 + [vmem] * 2,
        scratch_shapes=[pltpu.VMEM(r.shape, r.dtype) for r in results]
        + [pltpu.SemaphoreType.DMA((4,))] * 2,
        name="place",
    )(*results, small)


def solution(mesh):
    placed = (
        P("dp", None),
        P("dp", None),
        P("section", None, None),
        P("section", None, None),
        P("section", None, None),
        P("section", None, None),
        P("dp", None),
    )
    return jax.shard_map(
        local,
        mesh=mesh,
        in_specs=placed,
        out_specs=(
            P("section", "dp", None),
            P("section", "dp", None),
            P("section", "dp", None),
            P("section", "dp", None),
            P("section", None, "dp"),
            P("section", None, "dp"),
        ),
        check_vma=False,
    )
```
